32 devices in a mesh: seq: 8 (over z, y), fsdp: 4 (over x, core).
Axes of the slice: x: 2, y: 2, z: 4, core: 2. Of those that a mesh axis runs over, the one named last changes fastest.
Arguments:
- tokens: bfloat16 [1024, 4096], P('seq', 'fsdp'), may hold values from -6 to 6
- in_weight: bfloat16 [3, 4096, 4096], P(None, 'seq', 'fsdp'), may hold values from -0.09375 to 0.09375
- out_weight: bfloat16 [4096, 4096], P('fsdp', 'seq'), may hold values from -0.09375 to 0.09375
- filters: float32 [4096, 128], P('fsdp'), may hold values from -0.5 to 0.5
- cotangent: bfloat16 [1024, 4096], P('seq', 'fsdp'), may hold values from -6 to 6
Outputs:
- mixed_out: bfloat16 [1024, 4096], P('seq', 'fsdp')
- grad_tokens: bfloat16 [1024, 4096], P('seq', 'fsdp')
- grad_in_weight: float32 [3, 4096, 4096], P(None, 'seq', 'fsdp')
- grad_out_weight: float32 [4096, 4096], P('fsdp', 'seq')
- grad_filters: float32 [4096, 128], P('fsdp')
The draws below stay inside these ranges and needn't reach their ends.
All inputs are finite; a program needn't handle non-finite values.
Results may differ from the reference program's by a relative error of at most 0.018.
Values may be sent and summed in bfloat16 or wider, within the bound.
No kernel may reach another device: no remote copies, remote signals or barrier semaphores. Data moves between devices by JAX's collectives and lax.ppermute only.
A program may use at most 128 MiB of HBM per device.

```python
import jax
import jax.numpy as jnp
from jax import lax

D = 4096
C = 4096
TAPS = 128
TOK_DEV = 128
TOKENS = 1024
N_SEQ = 8
N_FSDP = 4


def raised(array, key, source, target, shards_of, factor):
    def block_of(axis_at):
        return (jnp.arange(array.shape[axis_at]) // (array.shape[axis_at] // shards_of)).reshape((-1,) + (1,) * (array.ndim - 1 - axis_at))

    one_side = jax.random.permutation(key, shards_of)[block_of(target)]
    other_side = (block_of(target) + shards_of // 2) % shards_of
    return jnp.where((block_of(source) == one_side) | (block_of(source) == other_side), factor * array, array)


def block_levels(rng, shape, shards, low, top_value):
    factor_of, own = 1.0, jax.random.fold_in(rng, 6)
    for dim, parts in shards:
        draws = jnp.exp(jax.random.uniform(jax.random.fold_in(own, dim), (parts,), jnp.float32, low / len(shards), top_value / len(shards)))
        factor_of = factor_of * jnp.repeat(draws, shape[dim] // parts).reshape([-1 if axis == dim else 1 for axis in range(len(shape))])
    return factor_of


def scatter_about(rng, shape, deviation, limit, pieces=(), held_as=jnp.bfloat16):
    entries = jax.random.normal(rng, shape, jnp.float32) * deviation
    if len(pieces) > 0:
        entries = block_levels(rng, shape, pieces, -0.22, 0.18) * entries
    return jnp.clip(entries, min=-limit, max=limit).astype(held_as)


def bell_draw_with(rng, extent, scale, limit, cuts, heavy, kind=jnp.bfloat16):
    array = scale * jax.random.normal(rng, extent, jnp.float32)
    if cuts:
        array = array * block_levels(rng, extent, cuts, -0.22, 0.18)
    return jnp.clip(raised(array, jax.random.fold_in(rng, 3), *heavy), -limit, limit).astype(kind)


def setup_inputs(seed: int = 0) -> dict:
    key_of = jax.random.split(jax.random.key(seed), 6)
    tokens = bell_draw_with(key_of[0], (TOKENS, D), 1.0, 6.0, ((0, 8), (1, 4)), (0, 1, 8, 2.0))
    in_weight = scatter_about(key_of[1], (3, D, C), D ** -0.5, 0.09375, ((1, 8), (2, 4)))
    out_weight = scatter_about(key_of[2], (C, D), C ** -0.5, 0.09375, ((0, 4), (1, 8)))
    filters = scatter_about(key_of[3], (C, TAPS), TAPS ** -0.5, 0.5, ((0, 4),), jnp.float32)
    cotangent = bell_draw_with(key_of[4], (TOKENS, D), 1.0, 6.0, ((0, 8), (1, 4)), (0, 1, 8, 2.0))
    return {"tokens": tokens, "in_weight": in_weight, "out_weight": out_weight, "filters": filters, "cotangent": cotangent}


def causal_filter(extended, filters):
    length = extended.shape[0] - filters.shape[1] + 1
    margin = filters.shape[1] - 1
    weights = jnp.transpose(filters)

    def add_tap(index, running):
        start = (margin - index).astype(jnp.int32)
        piece = lax.dynamic_slice_in_dim(extended, start, length, 0)
        tap_row = lax.dynamic_slice_in_dim(weights, index.astype(jnp.int32), 1, 0)
        return running + piece * tap_row
    start_sum = jnp.zeros((length, filters.shape[0]), jnp.float32)
    return lax.fori_loop(jnp.int32(0), jnp.int32(filters.shape[1]), add_tap, start_sum)

def reverse_filter(extended, filters):
    length = extended.shape[0] - filters.shape[1] + 1
    weights = jnp.transpose(filters)

    def add_tap(index, running):
        piece = lax.dynamic_slice_in_dim(extended, index.astype(jnp.int32), length, 0)
        tap_row = lax.dynamic_slice_in_dim(weights, index.astype(jnp.int32), 1, 0)
        return running + piece * tap_row
    start_sum = jnp.zeros((length, filters.shape[0]), jnp.float32)
    return lax.fori_loop(jnp.int32(0), jnp.int32(filters.shape[1]), add_tap, start_sum)

def filter_grad(extended, gradient, taps):
    length = gradient.shape[0]
    margin = taps - 1

    def one_tap(index):
        start = (margin - index).astype(jnp.int32)
        piece = lax.dynamic_slice_in_dim(extended, start, length, 0)
        return lax.optimization_barrier(jnp.sum(piece * gradient, axis=0))
    columns = lax.map(one_tap, jnp.arange(taps, dtype=jnp.int32))
    return jnp.transpose(columns)

def rounded(value):
    return lax.optimization_barrier(value.astype(jnp.bfloat16)).astype(jnp.float32)

def reference(tokens, in_weight, out_weight, filters, cotangent):
    margin = TAPS - 1
    channels = C // N_FSDP
    projected = jnp.einsum('td,idc->itc', tokens.astype(jnp.float32), in_weight.astype(jnp.float32)).astype(jnp.bfloat16)
    queries = projected[0].astype(jnp.float32)
    key_part = projected[1].astype(jnp.float32)
    value_part = projected[2].astype(jnp.float32)
    signal = (key_part * value_part).astype(jnp.bfloat16)
    zero_rows = jnp.zeros((margin, C), jnp.float32)
    extended = jnp.concatenate([zero_rows, signal.astype(jnp.float32)], 0)
    filtered = causal_filter(extended, filters)
    gated_rows = (queries * filtered).astype(jnp.bfloat16)
    gated_blocks = jnp.transpose(gated_rows.reshape(TOKENS, N_FSDP, channels), (1, 0, 2))
    out_blocks = out_weight.reshape(N_FSDP, channels, D)

    def add_mixed(running, pair):
        return (running + rounded(jnp.dot(pair[0], pair[1], preferred_element_type=jnp.float32)), None)
    mixed_sum, unused = lax.scan(add_mixed, jnp.zeros((TOKENS, D), jnp.float32), (gated_blocks, out_blocks))
    mixed_out = mixed_sum.astype(jnp.bfloat16)
    grad_gated = jnp.dot(cotangent, jnp.transpose(out_weight), preferred_element_type=jnp.float32)
    grad_queries = grad_gated * filtered
    grad_filtered = (grad_gated * queries).astype(jnp.bfloat16)
    grad_signal = reverse_filter(jnp.concatenate([grad_filtered.astype(jnp.float32), zero_rows], 0), filters)
    grad_filters = filter_grad(extended, grad_filtered.astype(jnp.float32), TAPS)
    grad_projected = jnp.stack([grad_queries, grad_signal * value_part, grad_signal * key_part]).astype(jnp.bfloat16)
    grad_blocks = jnp.transpose(grad_projected.reshape(3, TOKENS, N_FSDP, channels), (2, 0, 1, 3))
    weight_blocks = jnp.transpose(in_weight.reshape(3, D, N_FSDP, channels), (2, 0, 1, 3))

    def add_input(running, pair):
        term = jnp.einsum('itc,idc->td', pair[0].astype(jnp.float32), pair[1].astype(jnp.float32))
        return (running + rounded(term), None)
    grad_sum, unused = lax.scan(add_input, jnp.zeros((TOKENS, D), jnp.float32), (grad_blocks, weight_blocks))
    grad_tokens = grad_sum.astype(jnp.bfloat16)
    token_blocks = tokens.reshape(N_SEQ, TOK_DEV, D)
    proj_blocks = jnp.transpose(grad_projected.reshape(3, N_SEQ, TOK_DEV, C), (1, 0, 2, 3))
    gate_blocks = gated_rows.reshape(N_SEQ, TOK_DEV, C)
    cot_blocks = cotangent.reshape(N_SEQ, TOK_DEV, D)

    def add_weights(running, group):
        term_in = jnp.einsum('td,itc->idc', group[0].astype(jnp.float32), group[1].astype(jnp.float32))
        term_out = jnp.dot(jnp.transpose(group[2]), group[3], preferred_element_type=jnp.float32)
        return ((running[0] + rounded(term_in), running[1] + rounded(term_out)), None)
    start_sums = (jnp.zeros((3, D, C), jnp.float32), jnp.zeros((C, D), jnp.float32))
    weight_sums, unused = lax.scan(add_weights, start_sums, (token_blocks, proj_blocks, gate_blocks, cot_blocks))
    return (mixed_out, grad_tokens, weight_sums[0], weight_sums[1], grad_filters)
```

```python
import jax
import jax.numpy as jnp
from jax import lax
from jax.sharding import PartitionSpec as P

highest = lax.Precision.HIGHEST


def from_behind(value, axis, by):
    length = lax.axis_size(axis)
    pairs = [(i, i + by) for i in range(length) if 0 <= i + by < length]
    return lax.ppermute(value, axis, pairs)


def causal_filter(extended, filters):
    kernel = jnp.flip(jnp.transpose(filters), 0)[:, None, :]
    result = lax.conv_general_dilated(
        extended[None],
        kernel,
        (1,),
        "VALID",
        dimension_numbers=("NWC", "WIO", "NWC"),
        feature_group_count=filters.shape[0],
        precision=highest,
    )
    return result[0]


def reverse_filter(extended, filters):
    kernel = jnp.transpose(filters)[:, None, :]
    result = lax.conv_general_dilated(
        extended[None],
        kernel,
        (1,),
        "VALID",
        dimension_numbers=("NWC", "WIO", "NWC"),
        feature_group_count=filters.shape[0],
        precision=highest,
    )
    return result[0]


def filter_grad(extended, gradient):
    result = lax.conv_general_dilated(
        extended[None],
        gradient[:, None, :],
        (1,),
        "VALID",
        dimension_numbers=("NWC", "WIO", "NWC"),
        feature_group_count=gradient.shape[1],
        precision=highest,
    )
    return jnp.transpose(jnp.flip(result[0], 0))


def to_feature_rows(value):
    wide = lax.all_gather(value, "fsdp", axis=value.ndim - 1, tiled=True)
    return lax.all_to_all(wide, "seq", split_axis=wide.ndim - 1, concat_axis=wide.ndim - 2, tiled=True)


def to_token_rows(partial):
    swapped = lax.all_to_all(
        partial, "seq", split_axis=partial.ndim - 2, concat_axis=partial.ndim - 1, tiled=True
    )
    return lax.psum_scatter(swapped, "fsdp", scatter_dimension=partial.ndim - 1, tiled=True)


def on_device(tokens, in_weight, out_weight, filters, cotangent):
    taps = filters.shape[1]
    margin = taps - 1
    activations = to_feature_rows(jnp.stack([tokens, cotangent]))
    features, cot_rows = activations[0], activations[1]
    projected_part = jnp.einsum(
        "td,idc->itc", features, in_weight, preferred_element_type=jnp.float32
    ).astype(jnp.bfloat16)
    gated_part = lax.dot_general(
        cot_rows, out_weight, (((1,), (1,)), ((), ())), preferred_element_type=jnp.float32
    ).astype(jnp.bfloat16)
    summed = lax.psum_scatter(
        jnp.concatenate([projected_part, gated_part[None]], 0),
        "seq",
        scatter_dimension=2,
        tiled=True,
    ).astype(jnp.float32)
    queries, key_part, value_part, grad_gated = summed[0], summed[1], summed[2], summed[3]
    channels = queries.shape[1]
    own_filters = lax.dynamic_slice_in_dim(
        filters, lax.axis_index("seq") * channels, channels, 0
    )
    signal = (key_part * value_part).astype(jnp.bfloat16)
    extended = jnp.pad(signal, ((margin, 0), (0, 0))).astype(jnp.float32)
    filtered = causal_filter(extended, own_filters)
    gated = (queries * filtered).astype(jnp.bfloat16)
    grad_queries = grad_gated * filtered
    grad_filtered = (grad_gated * queries).astype(jnp.bfloat16)
    grad_signal = reverse_filter(
        jnp.pad(grad_filtered, ((0, margin), (0, 0))).astype(jnp.float32), own_filters
    )
    own_grad_filters = filter_grad(extended, grad_filtered.astype(jnp.float32))
    grad_projected = jnp.stack(
        [grad_queries, grad_signal * value_part, grad_signal * key_part]
    ).astype(jnp.bfloat16)
    rows = lax.all_gather(
        jnp.concatenate([grad_projected, gated[None]], 0), "seq", axis=2, tiled=True
    )
    grad_filters = lax.all_gather(own_grad_filters, "seq", axis=0, tiled=True)
    mixed_part = jnp.dot(rows[3], out_weight, preferred_element_type=jnp.float32)
    grad_part = jnp.einsum(
        "itc,idc->td", rows[:3], in_weight, preferred_element_type=jnp.float32
    )
    outward = to_token_rows(jnp.stack([mixed_part, grad_part]).astype(jnp.bfloat16))
    grad_in_weight = jnp.einsum(
        "td,itc->idc", features, rows[:3], preferred_element_type=jnp.float32
    )
    grad_out_weight = lax.dot_general(
        rows[3], cot_rows, (((0,), (0,)), ((), ())), preferred_element_type=jnp.float32
    )
    return (outward[0], outward[1], grad_in_weight, grad_out_weight, grad_filters)


def solution(mesh):
    placed = (
        P("seq", "fsdp"),
        P(None, "seq", "fsdp"),
        P("fsdp", "seq"),
        P("fsdp", None),
        P("seq", "fsdp"),
    )
    return jax.shard_map(
        on_device,
        mesh=mesh,
        in_specs=placed,
        out_specs=(
            P("seq", "fsdp"),
            P("seq", "fsdp"),
            P(None, "seq", "fsdp"),
            P("fsdp", "seq"),
            P("fsdp", None),
        ),
        check_vma=False,
    )
```

```python
import jax
import jax.numpy as jnp
from jax import lax
from jax.experimental import pallas as pl
from jax.experimental.pallas import tpu as pltpu
from jax.sharding import PartitionSpec as P

highest = lax.Precision.HIGHEST
bf16 = jnp.bfloat16
f32 = jnp.float32
lanes = 128
sublanes = 8
vmem_bytes = 48 * 1024 * 1024


def causal_filter(extended, filters):
    kernel = jnp.flip(jnp.transpose(filters), 0)[:, None, :]
    result = lax.conv_general_dilated(
        extended[None],
        kernel,
        (1,),
        "VALID",
        dimension_numbers=("NWC", "WIO", "NWC"),
        feature_group_count=filters.shape[0],
        precision=highest,
    )
    return result[0]


def reverse_filter(extended, filters):
    kernel = jnp.transpose(filters)[:, None, :]
    result = lax.conv_general_dilated(
        extended[None],
        kernel,
        (1,),
        "VALID",
        dimension_numbers=("NWC", "WIO", "NWC"),
        feature_group_count=filters.shape[0],
        precision=highest,
    )
    return result[0]


def filter_grad(extended, gradient):
    result = lax.conv_general_dilated(
        extended[None],
        gradient[:, None, :],
        (1,),
        "VALID",
        dimension_numbers=("NWC", "WIO", "NWC"),
        feature_group_count=gradient.shape[1],
        precision=highest,
    )
    return jnp.transpose(jnp.flip(result[0], 0))


def to_feature_rows(value):
    wide = lax.all_gather(value, "fsdp", axis=value.ndim - 1, tiled=True)
    return lax.all_to_all(wide, "seq", split_axis=wide.ndim - 1, concat_axis=wide.ndim - 2, tiled=True)


def to_token_rows(partial):
    swapped = lax.all_to_all(
        partial, "seq", split_axis=partial.ndim - 2, concat_axis=partial.ndim - 1, tiled=True
    )
    return lax.psum_scatter(swapped, "fsdp", scatter_dimension=partial.ndim - 1, tiled=True)


def on_any_mesh(tokens, in_weight, out_weight, filters, cotangent):
    taps = filters.shape[1]
    margin = taps - 1
    activations = to_feature_rows(jnp.stack([tokens, cotangent]))
    features, cot_rows = activations[0], activations[1]
    projected_part = jnp.einsum(
        "td,idc->itc", features, in_weight, preferred_element_type=jnp.float32
    ).astype(jnp.bfloat16)
    gated_part = lax.dot_general(
        cot_rows, out_weight, (((1,), (1,)), ((), ())), preferred_element_type=jnp.float32
    ).astype(jnp.bfloat16)
    summed = lax.psum_scatter(
        jnp.concatenate([projected_part, gated_part[None]], 0),
        "seq",
        scatter_dimension=2,
        tiled=True,
    ).astype(jnp.float32)
    queries, key_part, value_part, grad_gated = summed[0], summed[1], summed[2], summed[3]
    channels = queries.shape[1]
    own_filters = lax.dynamic_slice_in_dim(
        filters, lax.axis_index("seq") * channels, channels, 0
    )
    signal = (key_part * value_part).astype(jnp.bfloat16)
    extended = jnp.pad(signal, ((margin, 0), (0, 0))).astype(jnp.float32)
    filtered = causal_filter(extended, own_filters)
    gated = (queries * filtered).astype(jnp.bfloat16)
    grad_queries = grad_gated * filtered
    grad_filtered = (grad_gated * queries).astype(jnp.bfloat16)
    grad_signal = reverse_filter(
        jnp.pad(grad_filtered, ((0, margin), (0, 0))).astype(jnp.float32), own_filters
    )
    own_grad_filters = filter_grad(extended, grad_filtered.astype(jnp.float32))
    grad_projected = jnp.stack(
        [grad_queries, grad_signal * value_part, grad_signal * key_part]
    ).astype(jnp.bfloat16)
    rows = lax.all_gather(
        jnp.concatenate([grad_projected, gated[None]], 0), "seq", axis=2, tiled=True
    )
    grad_filters = lax.all_gather(own_grad_filters, "seq", axis=0, tiled=True)
    mixed_part = jnp.dot(rows[3], out_weight, preferred_element_type=jnp.float32)
    grad_part = jnp.einsum(
        "itc,idc->td", rows[:3], in_weight, preferred_element_type=jnp.float32
    )
    outward = to_token_rows(jnp.stack([mixed_part, grad_part]).astype(jnp.bfloat16))
    grad_in_weight = jnp.einsum(
        "td,itc->idc", features, rows[:3], preferred_element_type=jnp.float32
    )
    grad_out_weight = lax.dot_general(
        rows[3], cot_rows, (((0,), (0,)), ((), ())), preferred_element_type=jnp.float32
    )
    return (outward[0], outward[1], grad_in_weight, grad_out_weight, grad_filters)


def params(**more):
    return pltpu.CompilerParams(vmem_limit_bytes=vmem_bytes, **more)


def cost(flops, moved):
    return pl.CostEstimate(flops=flops, bytes_accessed=moved, transcendentals=0)


def flip(value, axis, bit):
    return lax.ppermute(value, axis, [(i, i ^ bit) for i in range(lax.axis_size(axis))])


def trade_places(value):
    size = lax.axis_size("fsdp")
    pairs = [
        ((2 * line + pair) * size + own, (2 * own + pair) * size + line)
        for line in range(size)
        for pair in range(2)
        for own in range(size)
    ]
    return lax.ppermute(value, ("seq", "fsdp"), pairs)


def along_line(value, by, holds):
    length = lax.axis_size("seq") // 2
    pairs = [
        (2 * i + pair, 2 * (i + by) + pair)
        for i in range(length)
        for pair in range(2)
        if 0 <= i + by < length and holds(i)
    ]
    return lax.ppermute(value, "seq", pairs)


def added(one, other):
    return (one.astype(f32) + other.astype(f32)).astype(bf16)


def line_scatter(blocks):
    length = blocks.shape[0]
    up, down = blocks[length - 1], blocks[1]
    for step in range(1, length):
        up_in = along_line(up, 1, lambda i: i <= step - 1)
        down_in = along_line(down, -1, lambda i: i >= length - step)
        if step < length - 1:
            up = added(blocks[length - 1 - step], up_in)
            down = added(blocks[1 + step], down_in)
    return up_in, down_in


def line_gather(block):
    length = lax.axis_size("seq") // 2
    before, after = [], []
    up = down = block
    for step in range(1, length):
        up = along_line(up, 1, lambda i: i >= step - 1)
        down = along_line(down, -1, lambda i: i <= length - step)
        before.append(up)
        after.append(down)
    return before, after


def project_pair(place, first, second):
    tokens, width = first[0].shape
    half = width // 2
    rows = 256
    count = half // lanes

    def body(place_ref, *refs):
        out = refs[-1]
        line = place_ref[0]
        for which in range(2):
            own, other, kept, given = refs[4 * which : 4 * which + 4]
            turned = (first, second)[which][3]
            dims = (((1,), (1,)), ((), ())) if turned else (((1,), (0,)), ((), ()))
            kept_value = kept[...].reshape(half, half)
            given_value = given[...].reshape(half, half)
            result = lax.dot_general(own[...], kept_value, dims, preferred_element_type=f32)
            result += lax.dot_general(other[...], given_value, dims, preferred_element_type=f32)
            result = result.astype(bf16)
            for j in range(count):
                out[lax.rem(j - line + count, count), which] = result[:, j * lanes : (j + 1) * lanes]

    operands, specs = [], []
    for value, kept, given, turned, index in (first, second):
        operands += [value, value, kept, given]
        specs += [
            pl.BlockSpec((rows, half), lambda g, place: (g, place[1])),
            pl.BlockSpec((rows, half), lambda g, place: (g, 1 - place[1])),
        ]
        if turned:
            specs += [
                pl.BlockSpec((half, half), lambda g, place: (place[1], 0)),
                pl.BlockSpec((half, half), lambda g, place: (0, 0)),
            ]
        else:
            specs += [
                pl.BlockSpec((1, half, half), lambda g, place, index=index: (index, 0, place[1])),
                pl.BlockSpec((half, half), lambda g, place: (0, 0)),
            ]
    return pl.pallas_call(
        body,
        out_shape=jax.ShapeDtypeStruct((count, 2, tokens, lanes), bf16),
        grid_spec=pltpu.PrefetchScalarGridSpec(
            num_scalar_prefetch=1,
            grid=(tokens // rows,),
            in_specs=specs,
            out_specs=pl.BlockSpec((count, 2, rows, lanes), lambda g, place: (0, 0, g, 0)),
        ),
        compiler_params=params(),
        cost_estimate=cost(4 * tokens * width * half, 8 * tokens * width),
        name="project_pair",
    )(place, *operands)


def block_rows(order, r, size):
    return pl.ds(pl.multiple_of(order[r] * size, size), size)


def window_filter(load, tap, tiles, reach):
    steps = range(reach // sublanes)
    sums = [jnp.zeros((sublanes, lanes), f32) for _ in range(tiles)]
    for shift in range(sublanes):
        held = {}
        for q in steps:
            weight = tap(shift, q)
            for i in range(tiles):
                if i - q not in held:
                    held[i - q] = load(shift, i - q)
                sums[i] = sums[i] + weight * held[i - q]
    return sums


def own_sum(blocks, up, down, which, rows):
    return (
        blocks[0, which, rows, :].astype(f32)
        + up[which, rows, :].astype(f32)
        + down[which, rows, :].astype(f32)
    ).astype(bf16)


def forward_filter(order, blocks, up, down, spread_taps):
    tokens = up.shape[1]
    taps = spread_taps.shape[0] // sublanes
    n_blocks = order.shape[0]
    size = tokens // n_blocks
    tiles = 8

    def body(order_ref, blocks_ref, up_ref, down_ref, taps_ref, kv_ref, signal_ref, filtered_ref, moved):
        for shift in range(sublanes):
            moved[shift, : taps + sublanes, :] = jnp.zeros((taps + sublanes, lanes), f32)

        def one_block(r, carry):
            rows = pl.ds(pl.multiple_of(r * size, size), size)
            place = block_rows(order_ref, r, size)
            key_part = own_sum(blocks_ref, up_ref, down_ref, 0, rows)
            value_part = own_sum(blocks_ref, up_ref, down_ref, 1, rows)
            kv_ref[0, place, :] = key_part
            kv_ref[1, place, :] = value_part
            product = (key_part.astype(f32) * value_part.astype(f32)).astype(bf16)
            signal_ref[place, :] = product
            moved[0, pl.ds(pl.multiple_of(taps + order_ref[r] * size, size), size), :] = product.astype(f32)
            return carry

        lax.fori_loop(0, n_blocks, one_block, 0)
        for shift in range(1, sublanes):
            moved[shift, taps : taps + tokens, :] = moved[0, taps - shift : taps - shift + tokens, :]

        def run(g, carry):
            start = pl.multiple_of(g * tiles * sublanes, tiles * sublanes)

            def load(shift, at):
                return moved[shift, pl.ds(start + taps + at * sublanes, sublanes), :]

            def tap(shift, q):
                index = q * sublanes + shift
                return taps_ref[index * sublanes : (index + 1) * sublanes, :]

            sums = window_filter(load, tap, tiles, taps)
            for i in range(tiles):
                filtered_ref[pl.ds(start + i * sublanes, sublanes), :] = sums[i]
            return carry

        lax.fori_loop(0, tokens // (tiles * sublanes), run, 0)

    whole = lambda shape: pl.BlockSpec(shape, lambda g, order: (0,) * len(shape))
    return pl.pallas_call(
        body,
        out_shape=(
            jax.ShapeDtypeStruct((2, tokens, lanes), bf16),
            jax.ShapeDtypeStruct((tokens, lanes), bf16),
            jax.ShapeDtypeStruct((tokens, lanes), f32),
        ),
        grid_spec=pltpu.PrefetchScalarGridSpec(
            num_scalar_prefetch=1,
            grid=(1,),
            in_specs=[
                whole((1, 2, tokens, lanes)),
                whole((2, tokens, lanes)),
                whole((2, tokens, lanes)),
                whole(spread_taps.shape),
            ],
            out_specs=(
                whole((2, tokens, lanes)),
                whole((tokens, lanes)),
                whole((tokens, lanes)),
            ),
            scratch_shapes=[pltpu.VMEM((sublanes, taps + tokens, lanes), f32)],
        ),
        compiler_params=params(),
        cost_estimate=cost(400 * tokens * lanes * taps, 12 * tokens * lanes),
        name="forward_filter",
    )(order, blocks, up, down, spread_taps)


def gate_rows(order, blocks, up, down, filtered):
    tokens = up.shape[1]
    n_blocks = order.shape[0]
    size = tokens // n_blocks

    def body(order_ref, blocks_ref, up_ref, down_ref, filtered_ref, out_ref, grad_ref):
        def one_block(r, carry):
            rows = pl.ds(pl.multiple_of(r * size, size), size)
            place = block_rows(order_ref, r, size)
            queries = own_sum(blocks_ref, up_ref, down_ref, 0, rows).astype(f32)
            grad_gated = (
                blocks_ref[0, 1, rows, :].astype(f32)
                + up_ref[1, rows, :].astype(f32)
                + down_ref[1, rows, :].astype(f32)
            )
            kept = filtered_ref[place, :]
            out_ref[0, rows, :] = (queries * kept).astype(bf16)
            out_ref[1, rows, :] = (grad_gated * kept).astype(bf16)
            grad_ref[place, :] = (grad_gated * queries).astype(bf16)
            return carry

        lax.fori_loop(0, n_blocks, one_block, 0)

    whole = lambda shape: pl.BlockSpec(shape, lambda g, order: (0,) * len(shape))
    return pl.pallas_call(
        body,
        out_shape=(
            jax.ShapeDtypeStruct((2, tokens, lanes), bf16),
            jax.ShapeDtypeStruct((tokens, lanes), bf16),
        ),
        grid_spec=pltpu.PrefetchScalarGridSpec(
            num_scalar_prefetch=1,
            grid=(1,),
            in_specs=[
                whole((1, 2, tokens, lanes)),
                whole((2, tokens, lanes)),
                whole((2, tokens, lanes)),
                whole((tokens, lanes)),
            ],
            out_specs=(whole((2, tokens, lanes)), whole((tokens, lanes))),
        ),
        compiler_params=params(),
        cost_estimate=cost(20 * tokens * lanes, 20 * tokens * lanes),
        name="gate_rows",
    )(order, blocks, up, down, filtered)


def backward_filter(order, grad_filtered, key_values, spread_taps):
    tokens = grad_filtered.shape[0]
    taps = spread_taps.shape[0] // sublanes
    n_blocks = order.shape[0]
    size = tokens // n_blocks
    tiles = 8

    def body(order_ref, grad_ref, kv_ref, taps_ref, out_ref, moved, signal_grad):
        for shift in range(sublanes):
            moved[shift, tokens - sublanes :, :] = jnp.zeros((taps + sublanes, lanes), f32)
        moved[0, :tokens, :] = grad_ref[...].astype(f32)
        for shift in range(1, sublanes):
            moved[shift, :tokens, :] = moved[0, shift : shift + tokens, :]

        def run(g, carry):
            start = pl.multiple_of(g * tiles * sublanes, tiles * sublanes)

            def load(shift, at):
                return moved[shift, pl.ds(start + (tiles - 1 - at) * sublanes, sublanes), :]

            def tap(shift, q):
                index = q * sublanes + shift
                return taps_ref[index * sublanes : (index + 1) * sublanes, :]

            sums = window_filter(load, tap, tiles, taps)
            for i in range(tiles):
                signal_grad[pl.ds(start + (tiles - 1 - i) * sublanes, sublanes), :] = sums[i]
            return carry

        lax.fori_loop(0, tokens // (tiles * sublanes), run, 0)

        def one_block(r, carry):
            rows = pl.ds(pl.multiple_of(r * size, size), size)
            place = block_rows(order_ref, r, size)
            gradient = signal_grad[place, :]
            out_ref[0, rows, :] = (gradient * kv_ref[1, place, :].astype(f32)).astype(bf16)
            out_ref[1, rows, :] = (gradient * kv_ref[0, place, :].astype(f32)).astype(bf16)
            return carry

        lax.fori_loop(0, n_blocks, one_block, 0)

    whole = lambda shape: pl.BlockSpec(shape, lambda g, order: (0,) * len(shape))
    return pl.pallas_call(
        body,
        out_shape=jax.ShapeDtypeStruct((2, tokens, lanes), bf16),
        grid_spec=pltpu.PrefetchScalarGridSpec(
            num_scalar_prefetch=1,
            grid=(1,),
            in_specs=[
                whole((tokens, lanes)),
                whole((2, tokens, lanes)),
                whole(spread_taps.shape),
            ],
            out_specs=whole((2, tokens, lanes)),
            scratch_shapes=[
                pltpu.VMEM((sublanes, tokens + taps, lanes), f32),
                pltpu.VMEM((tokens, lanes), f32),
            ],
        ),
        compiler_params=params(),
        cost_estimate=cost(400 * tokens * lanes * taps, 12 * tokens * lanes),
        name="backward_filter",
    )(order, grad_filtered, key_values, spread_taps)


def taps_gradient(signal, grad_filtered, taps):
    tokens = signal.shape[0]
    tiles = 8
    steps = taps // sublanes

    def body(signal_ref, grad_ref, out_ref, moved, gradient):
        for shift in range(sublanes):
            moved[shift, : taps + sublanes, :] = jnp.zeros((taps + sublanes, lanes), f32)
        moved[0, taps:, :] = signal_ref[...].astype(f32)
        gradient[...] = grad_ref[...].astype(f32)
        for shift in range(1, sublanes):
            moved[shift, taps : taps + tokens, :] = moved[0, taps - shift : taps - shift + tokens, :]
        for shift in range(sublanes):

            def run(g, sums):
                start = pl.multiple_of(g * tiles * sublanes, tiles * sublanes)
                sums = list(sums)
                held = {}
                for i in range(tiles):
                    here = gradient[pl.ds(start + i * sublanes, sublanes), :]
                    for q in range(steps):
                        if i - q not in held:
                            held[i - q] = moved[shift, pl.ds(start + taps + (i - q) * sublanes, sublanes), :]
                        sums[q] = sums[q] + here * held[i - q]
                return tuple(sums)

            zero = tuple(jnp.zeros((sublanes, lanes), f32) for _ in range(steps))
            sums = lax.fori_loop(0, tokens // (tiles * sublanes), run, zero)
            for q in range(steps):
                index = q * sublanes + shift
                out_ref[index : index + 1, :] = jnp.sum(sums[q], axis=0, keepdims=True)

    return pl.pallas_call(
        body,
        out_shape=jax.ShapeDtypeStruct((taps, lanes), f32),
        in_specs=[pl.BlockSpec(memory_space=pltpu.VMEM)] * 2,
        out_specs=pl.BlockSpec(memory_space=pltpu.VMEM),
        scratch_shapes=[
            pltpu.VMEM((sublanes, tokens + taps, lanes), f32),
            pltpu.VMEM((tokens, lanes), f32),
        ],
        compiler_params=params(),
        cost_estimate=cost(400 * tokens * lanes * taps, 8 * tokens * lanes),
        name="taps_gradient",
    )(signal, grad_filtered)


def merge_blocks(place, block, before, after):
    tokens = block.shape[1]
    length = len(before) + 1
    rows = 256

    def body(place_ref, *refs):
        out = refs[-1]
        own, ups, downs = refs[0], refs[1:length], refs[length : 2 * length - 1]
        line = place_ref[0]
        for offset in range(length):
            if offset == 0:
                value = own[...]
            else:
                value = downs[offset - 1][...] + ups[length - offset - 1][...]
            at = pl.multiple_of(lax.rem(line + offset, length) * lanes, lanes)
            out[:, :, pl.ds(at, lanes)] = value

    spec = pl.BlockSpec((2, rows, lanes), lambda g, place: (0, g, 0))
    return pl.pallas_call(
        body,
        out_shape=jax.ShapeDtypeStruct((2, tokens, length * lanes), bf16),
        grid_spec=pltpu.PrefetchScalarGridSpec(
            num_scalar_prefetch=1,
            grid=(tokens // rows,),
            in_specs=[spec] * (2 * length - 1),
            out_specs=pl.BlockSpec((2, rows, length * lanes), lambda g, place: (0, g, 0)),
        ),
        compiler_params=params(),
        cost_estimate=cost(tokens * lanes * 8, 2 * 2 * tokens * lanes * 11),
        name="merge_blocks",
    )(place, block, *before, *after)


def project_back(place, merged, in_weight, given, indices):
    tokens, half = merged[0][0].shape[1:]
    rows = 256
    n = len(merged)

    def body(place_ref, *refs):
        out = refs[-1]
        dims = (((1,), (1,)), ((), ()))
        own = jnp.zeros((rows, half), f32)
        other = jnp.zeros((rows, half), f32)
        for k in range(n):
            value, kept, sent = refs[3 * k], refs[3 * k + 1], refs[3 * k + 2]
            value = value[...].reshape(rows, half)
            own += lax.dot_general(value, kept[...].reshape(half, half), dims, preferred_element_type=f32)
            other += lax.dot_general(value, sent[...], dims, preferred_element_type=f32)
        at = place_ref[1]
        out[:, pl.ds(pl.multiple_of(at * half, half), half)] = own.astype(bf16)
        out[:, pl.ds(pl.multiple_of((1 - at) * half, half), half)] = other.astype(bf16)

    operands, specs = [], []
    for (value, which), sent, index in zip(merged, given, indices):
        operands += [value, in_weight, sent]
        specs += [
            pl.BlockSpec((1, rows, half), lambda g, place, which=which: (which, g, 0)),
            pl.BlockSpec((1, half, half), lambda g, place, index=index: (index, 0, place[1])),
            pl.BlockSpec((half, half), lambda g, place: (0, 0)),
        ]
    return pl.pallas_call(
        body,
        out_shape=jax.ShapeDtypeStruct((tokens, 2 * half), bf16),
        grid_spec=pltpu.PrefetchScalarGridSpec(
            num_scalar_prefetch=1,
            grid=(tokens // rows,),
            in_specs=specs,
            out_specs=pl.BlockSpec((rows, 2 * half), lambda g, place: (g, 0)),
        ),
        compiler_params=params(),
        cost_estimate=cost(4 * n * tokens * half * half, 8 * tokens * half),
        name="project_back",
    )(place, *operands)


def project_out(place, merged, out_weight, given):
    tokens, half = merged.shape[1:]
    rows = 256

    def body(place_ref, value_ref, kept, sent, out):
        value = value_ref[...].reshape(rows, half)
        at = place_ref[1]
        own = jnp.dot(value, kept[...], preferred_element_type=f32)
        other = jnp.dot(value, sent[...], preferred_element_type=f32)
        out[:, pl.ds(pl.multiple_of(at * half, half), half)] = own.astype(bf16)
        out[:, pl.ds(pl.multiple_of((1 - at) * half, half), half)] = other.astype(bf16)

    return pl.pallas_call(
        body,
        out_shape=jax.ShapeDtypeStruct((tokens, 2 * half), bf16),
        grid_spec=pltpu.PrefetchScalarGridSpec(
            num_scalar_prefetch=1,
            grid=(tokens // rows,),
            in_specs=[
                pl.BlockSpec((1, rows, half), lambda g, place: (0, g, 0)),
                pl.BlockSpec((half, half), lambda g, place: (place[1], 0)),
                pl.BlockSpec((half, half), lambda g, place: (0, 0)),
            ],
            out_specs=pl.BlockSpec((rows, 2 * half), lambda g, place: (g, 0)),
        ),
        compiler_params=params(),
        cost_estimate=cost(4 * tokens * half * half, 8 * tokens * half),
        name="project_out",
    )(place, merged, out_weight, given)


def in_gradient(place, turned, merged, which, index, total, running):
    tokens, half = merged.shape[1:]
    rows = 256

    def body(place_ref, own, other, value_ref, *refs):
        kept, sent = refs[-2:]
        value = value_ref[...].reshape(tokens, half)
        kept[...] = jnp.dot(own[...], value, preferred_element_type=f32)[None]
        sent[...] = jnp.dot(other[...], value, preferred_element_type=f32).astype(bf16)

    steps = half // rows
    more = [] if running is None else [running]
    return pl.pallas_call(
        body,
        out_shape=(
            jax.ShapeDtypeStruct((total, half, 2 * half), f32),
            jax.ShapeDtypeStruct((half, half), bf16),
        ),
        grid_spec=pltpu.PrefetchScalarGridSpec(
            num_scalar_prefetch=1,
            grid=(steps,),
            in_specs=[
                pl.BlockSpec((rows, tokens), lambda g, place: (place[1] * steps + g, 0)),
                pl.BlockSpec((rows, tokens), lambda g, place: ((1 - place[1]) * steps + g, 0)),
                pl.BlockSpec((1, tokens, half), lambda g, place: (which, 0, 0)),
            ]
            + [pl.BlockSpec(memory_space=pl.ANY)] * len(more),
            out_specs=(
                pl.BlockSpec((1, rows, half), lambda g, place: (index, g, place[1])),
                pl.BlockSpec((rows, half), lambda g, place: (g, 0)),
            ),
        ),
        input_output_aliases={4: 0} if more else {},
        compiler_params=params(),
        cost_estimate=cost(4 * tokens * half * half, 8 * tokens * half),
        name="in_gradient",
    )(place, turned, turned, merged, *more)


def out_gradient(place, merged, rows_of):
    tokens, half = merged.shape[1:]
    rows = 256
    steps = half // rows

    def body(place_ref, value_ref, own, other, kept, sent):
        value = value_ref[...].reshape(tokens, rows)
        dims = (((0,), (0,)), ((), ()))
        kept[...] = lax.dot_general(value, own[...], dims, preferred_element_type=f32)
        sent[...] = lax.dot_general(value, other[...], dims, preferred_element_type=f32).astype(bf16)

    return pl.pallas_call(
        body,
        out_shape=(
            jax.ShapeDtypeStruct((2 * half, half), f32),
            jax.ShapeDtypeStruct((half, half), bf16),
        ),
        grid_spec=pltpu.PrefetchScalarGridSpec(
            num_scalar_prefetch=1,
            grid=(steps,),
            in_specs=[
                pl.BlockSpec((1, tokens, rows), lambda g, place: (0, 0, g)),
                pl.BlockSpec((tokens, half), lambda g, place: (0, place[1])),
                pl.BlockSpec((tokens, half), lambda g, place: (0, 1 - place[1])),
            ],
            out_specs=(
                pl.BlockSpec((rows, half), lambda g, place: (place[1] * steps + g, 0)),
                pl.BlockSpec((rows, half), lambda g, place: (g, 0)),
            ),
        ),
        compiler_params=params(),
        cost_estimate=cost(4 * tokens * half * half, 8 * tokens * half),
        name="out_gradient",
    )(place, merged, rows_of, rows_of)


def take_in_half(place, running, pieces):
    n = len(pieces)
    half = pieces[0].shape[0]

    def body(place_ref, *refs):
        out = refs[-1]
        for k in range(n):

            @pl.when(pl.program_id(0) == k)
            def _():
                out[...] = refs[k][...].astype(f32)[None]

    return pl.pallas_call(
        body,
        out_shape=jax.ShapeDtypeStruct(running.shape, f32),
        grid_spec=pltpu.PrefetchScalarGridSpec(
            num_scalar_prefetch=1,
            grid=(n,),
            in_specs=[pl.BlockSpec((half, half), lambda g, place: (0, 0))] * n
            + [pl.BlockSpec(memory_space=pl.ANY)],
            out_specs=pl.BlockSpec((1, half, half), lambda g, place: (g, 0, 1 - place[1])),
        ),
        input_output_aliases={n + 1: 0},
        compiler_params=params(),
        cost_estimate=cost(n * half * half, 6 * n * half * half),
        name="take_in_half",
    )(place, *pieces, running)


def take_out_half(place, running, piece):
    half = piece.shape[0]

    def body(place_ref, piece_ref, running_ref, out):
        out[...] = piece_ref[...].astype(f32)

    return pl.pallas_call(
        body,
        out_shape=jax.ShapeDtypeStruct(running.shape, f32),
        grid_spec=pltpu.PrefetchScalarGridSpec(
            num_scalar_prefetch=1,
            grid=(1,),
            in_specs=[
                pl.BlockSpec((half, half), lambda g, place: (0, 0)),
                pl.BlockSpec(memory_space=pl.ANY),
            ],
            out_specs=pl.BlockSpec((half, half), lambda g, place: (1 - place[1], 0)),
        ),
        input_output_aliases={2: 0},
        compiler_params=params(),
        cost_estimate=cost(half * half, 6 * half * half),
        name="take_out_half",
    )(place, piece, running)


def on_paired_mesh(tokens, in_weight, out_weight, filters, cotangent):
    taps = filters.shape[1]
    seq_at, fsdp_at = lax.axis_index("seq"), lax.axis_index("fsdp")
    line, pair = seq_at // 2, seq_at % 2
    place = jnp.stack([line, pair]).astype(jnp.int32)
    half_in, half_out = in_weight.shape[2] // 2, out_weight.shape[0] // 2
    relative = jnp.arange(8, dtype=jnp.int32)
    order = (
        2 * (fsdp_at ^ (2 * (relative % 2) + relative // 4)) + (pair ^ (relative // 2 % 2))
    ).astype(jnp.int32)

    tokens_here = trade_places(tokens)
    cot_here = trade_places(cotangent)
    given_in = {}
    for i in (1, 2, 0):
        sent = lax.dynamic_slice_in_dim(in_weight[i], (1 - pair) * half_in, half_in, 1)
        given_in[i] = flip(sent, "seq", 1)
    given_out = flip(
        lax.dynamic_slice_in_dim(out_weight, (1 - pair) * half_out, half_out, 0), "seq", 1
    )
    x_rows = jnp.stack([tokens_here, flip(tokens_here, "fsdp", 2)])
    x_rows = jnp.stack([x_rows, flip(x_rows, "seq", 1)])
    x_rows = jnp.stack([x_rows, flip(x_rows, "fsdp", 1)])
    g_rows = jnp.stack([cot_here, flip(cot_here, "seq", 1)])
    g_rows = jnp.stack([g_rows, flip(g_rows, "fsdp", 2)], axis=1)
    g_rows = jnp.stack([g_rows, flip(g_rows, "fsdp", 1)])
    width = tokens.shape[1]
    x_rows = x_rows.reshape(-1, width)
    g_rows = g_rows.reshape(-1, width)
    turned = jnp.transpose(x_rows)
    own_filters = lax.dynamic_slice_in_dim(
        filters, pair * half_in + line * lanes, lanes, 0
    )
    spread_taps = jnp.repeat(jnp.transpose(own_filters), sublanes, axis=0)

    kv_blocks = project_pair(
        place,
        (x_rows, in_weight, given_in[1], False, 1),
        (x_rows, in_weight, given_in[2], False, 2),
    )
    qg_blocks = project_pair(
        place,
        (x_rows, in_weight, given_in[0], False, 0),
        (g_rows, out_weight, given_out, True, 0),
    )
    kv_up, kv_down = line_scatter(kv_blocks)
    qg_up, qg_down = line_scatter(qg_blocks)
    key_values, signal, filtered = forward_filter(order, kv_blocks, kv_up, kv_down, spread_taps)
    gated_pair, grad_filtered = gate_rows(order, qg_blocks, qg_up, qg_down, filtered)
    gated_before, gated_after = line_gather(gated_pair)
    kv_grads = backward_filter(order, grad_filtered, key_values, spread_taps)
    kv_before, kv_after = line_gather(kv_grads)
    own_taps = taps_gradient(signal, grad_filtered, taps)
    all_taps = lax.all_gather(jnp.transpose(own_taps), "seq", axis=0)
    length = lax.axis_size("seq") // 2
    grad_filters = jnp.swapaxes(all_taps.reshape(length, 2, lanes, taps), 0, 1).reshape(filters.shape)

    first = merge_blocks(place, gated_pair, gated_before, gated_after)
    mixed_part = project_out(place, first, out_weight, given_out)
    out_kept, out_sent = out_gradient(place, first, g_rows)
    in_kept, q_sent = in_gradient(place, turned, first, 1, 0, in_weight.shape[0], None)
    out_given = flip(out_sent, "seq", 1)
    q_given = flip(q_sent, "seq", 1)

    second = merge_blocks(place, kv_grads, kv_before, kv_after)
    grad_part = project_back(
        place,
        [(first, 1), (second, 0), (second, 1)],
        in_weight,
        [given_in[0], given_in[1], given_in[2]],
        [0, 1, 2],
    )
    in_kept, k_sent = in_gradient(place, turned, second, 0, 1, in_weight.shape[0], in_kept)
    in_kept, v_sent = in_gradient(place, turned, second, 1, 2, in_weight.shape[0], in_kept)
    k_given, v_given = flip(k_sent, "seq", 1), flip(v_sent, "seq", 1)

    def outward(part, x_first):
        parts = part.reshape(2, 2, 2, part.shape[0] // 8, width)
        parts = added(parts[0], flip(parts[1], "fsdp", 1))
        if x_first:
            parts = added(parts[:, 0], flip(parts[:, 1], "fsdp", 2))
            parts = added(parts[0], flip(parts[1], "seq", 1))
        else:
            parts = added(parts[0], flip(parts[1], "seq", 1))
            parts = added(parts[0], flip(parts[1], "fsdp", 2))
        return trade_places(parts)

    mixed_out = outward(mixed_part, True)
    grad_tokens = outward(grad_part, False)
    grad_out_weight = take_out_half(place, out_kept, out_given)
    grad_in_weight = take_in_half(place, in_kept, [q_given, k_given, v_given])
    return (mixed_out, grad_tokens, grad_in_weight, grad_out_weight, grad_filters)


def solution(mesh):
    placed = (
        P("seq", "fsdp"),
        P(None, "seq", "fsdp"),
        P("fsdp", "seq"),
        P("fsdp", None),
        P("seq", "fsdp"),
    )
    paired = (mesh.shape["seq"], mesh.shape["fsdp"]) == (8, 4)
    return jax.shard_map(
        on_paired_mesh if paired else on_any_mesh,
        mesh=mesh,
        in_specs=placed,
        out_specs=(
            P("seq", "fsdp"),
            P("seq", "fsdp"),
            P(None, "seq", "fsdp"),
            P("fsdp", "seq"),
            P("fsdp", None),
        ),
        check_vma=False,
    )
```

```python
import jax
import jax.numpy as jnp
from jax import lax
from jax.experimental import pallas as pl
from jax.experimental.pallas import tpu as pltpu
from jax.sharding import PartitionSpec as P

highest = lax.Precision.HIGHEST
bf16 = jnp.bfloat16
f32 = jnp.float32
lanes = 128
sublanes = 8
vmem_bytes = 48 * 1024 * 1024


def causal_filter(extended, filters):
    kernel = jnp.flip(jnp.transpose(filters), 0)[:, None, :]
    result = lax.conv_general_dilated(
        extended[None],
        kernel,
        (1,),
        "VALID",
        dimension_numbers=("NWC", "WIO", "NWC"),
        feature_group_count=filters.shape[0],
        precision=highest,
    )
    return result[0]


def reverse_filter(extended, filters):
    kernel = jnp.transpose(filters)[:, None, :]
    result = lax.conv_general_dilated(
        extended[None],
        kernel,
        (1,),
        "VALID",
        dimension_numbers=("NWC", "WIO", "NWC"),
        feature_group_count=filters.shape[0],
        precision=highest,
    )
    return result[0]


def filter_grad(extended, gradient):
    result = lax.conv_general_dilated(
        extended[None],
        gradient[:, None, :],
        (1,),
        "VALID",
        dimension_numbers=("NWC", "WIO", "NWC"),
        feature_group_count=gradient.shape[1],
        precision=highest,
    )
    return jnp.transpose(jnp.flip(result[0], 0))


def to_feature_rows(value):
    wide = lax.all_gather(value, "fsdp", axis=value.ndim - 1, tiled=True)
    return lax.all_to_all(wide, "seq", split_axis=wide.ndim - 1, concat_axis=wide.ndim - 2, tiled=True)


def to_token_rows(partial):
    swapped = lax.all_to_all(
        partial, "seq", split_axis=partial.ndim - 2, concat_axis=partial.ndim - 1, tiled=True
    )
    return lax.psum_scatter(swapped, "fsdp", scatter_dimension=partial.ndim - 1, tiled=True)


def on_any_mesh(tokens, in_weight, out_weight, filters, cotangent):
    taps = filters.shape[1]
    margin = taps - 1
    activations = to_feature_rows(jnp.stack([tokens, cotangent]))
    features, cot_rows = activations[0], activations[1]
    projected_part = jnp.einsum(
        "td,idc->itc", features, in_weight, preferred_element_type=jnp.float32
    ).astype(jnp.bfloat16)
    gated_part = lax.dot_general(
        cot_rows, out_weight, (((1,), (1,)), ((), ())), preferred_element_type=jnp.float32
    ).astype(jnp.bfloat16)
    summed = lax.psum_scatter(
        jnp.concatenate([projected_part, gated_part[None]], 0),
        "seq",
        scatter_dimension=2,
        tiled=True,
    ).astype(jnp.float32)
    queries, key_part, value_part, grad_gated = summed[0], summed[1], summed[2], summed[3]
    channels = queries.shape[1]
    own_filters = lax.dynamic_slice_in_dim(
        filters, lax.axis_index("seq") * channels, channels, 0
    )
    signal = (key_part * value_part).astype(jnp.bfloat16)
    extended = jnp.pad(signal, ((margin, 0), (0, 0))).astype(jnp.float32)
    filtered = causal_filter(extended, own_filters)
    gated = (queries * filtered).astype(jnp.bfloat16)
    grad_queries = grad_gated * filtered
    grad_filtered = (grad_gated * queries).astype(jnp.bfloat16)
    grad_signal = reverse_filter(
        jnp.pad(grad_filtered, ((0, margin), (0, 0))).astype(jnp.float32), own_filters
    )
    own_grad_filters = filter_grad(extended, grad_filtered.astype(jnp.float32))
    grad_projected = jnp.stack(
        [grad_queries, grad_signal * value_part, grad_signal * key_part]
    ).astype(jnp.bfloat16)
    rows = lax.all_gather(
        jnp.concatenate([grad_projected, gated[None]], 0), "seq", axis=2, tiled=True
    )
    grad_filters = lax.all_gather(own_grad_filters, "seq", axis=0, tiled=True)
    mixed_part = jnp.dot(rows[3], out_weight, preferred_element_type=jnp.float32)
    grad_part = jnp.einsum(
        "itc,idc->td", rows[:3], in_weight, preferred_element_type=jnp.float32
    )
    outward = to_token_rows(jnp.stack([mixed_part, grad_part]).astype(jnp.bfloat16))
    grad_in_weight = jnp.einsum(
        "td,itc->idc", features, rows[:3], preferred_element_type=jnp.float32
    )
    grad_out_weight = lax.dot_general(
        rows[3], cot_rows, (((0,), (0,)), ((), ())), preferred_element_type=jnp.float32
    )
    return (outward[0], outward[1], grad_in_weight, grad_out_weight, grad_filters)


def params(**more):
    return pltpu.CompilerParams(vmem_limit_bytes=vmem_bytes, **more)


def cost(flops, moved):
    return pl.CostEstimate(flops=flops, bytes_accessed=moved, transcendentals=0)


def flip(value, axis, bit):
    return lax.ppermute(value, axis, [(i, i ^ bit) for i in range(lax.axis_size(axis))])


def crossed(index):
    return 2 * (index % 2) + index // 2


def trade_places(value, back):
    size = lax.axis_size("fsdp")
    pairs = [
        ((2 * line + pair) * size + own, (2 * own + pair) * size + crossed(line))
        for line in range(size)
        for pair in range(2)
        for own in range(size)
    ]
    return lax.ppermute(value, ("seq", "fsdp"), [p[::-1] for p in pairs] if back else pairs)


def flip_both(value):
    size = lax.axis_size("fsdp")
    pairs = [
        (seq * size + own, (seq ^ 1) * size + (own ^ 2))
        for seq in range(lax.axis_size("seq"))
        for own in range(size)
    ]
    return lax.ppermute(value, ("seq", "fsdp"), pairs)


def after(values, *others):
    return lax.optimization_barrier((values, others))[0]


def along_line(value, by, holds):
    length = lax.axis_size("seq") // 2
    pairs = [
        (2 * i + pair, 2 * (i + by) + pair)
        for i in range(length)
        for pair in range(2)
        if 0 <= i + by < length and holds(i)
    ]
    return lax.ppermute(value, "seq", pairs)


def added(one, other):
    return (one.astype(f32) + other.astype(f32)).astype(bf16)


def line_scatter(blocks):
    length = blocks.shape[0]
    up, down = blocks[length - 1], blocks[1]
    for step in range(1, length):
        up_in = along_line(up, 1, lambda i: i <= step - 1)
        down_in = along_line(down, -1, lambda i: i >= length - step)
        if step < length - 1:
            up = added(blocks[length - 1 - step], up_in)
            down = added(blocks[1 + step], down_in)
    return up_in, down_in


def next_block(block, by, step):
    length = lax.axis_size("seq") // 2
    if by > 0:
        return along_line(block, 1, lambda i: i >= step - 1)
    return along_line(block, -1, lambda i: i <= length - step)


def project_pair(place, first, second):
    tokens, width = first[0].shape
    half = width // 2
    rows = 256
    count = half // lanes

    def body(place_ref, *refs):
        out = refs[-1]
        line = place_ref[0]
        for which in range(2):
            own, other, kept, given = refs[4 * which : 4 * which + 4]
            turned = (first, second)[which][3]
            dims = (((1,), (1,)), ((), ())) if turned else (((1,), (0,)), ((), ()))
            kept_value = kept[...].reshape(half, half)
            given_value = given[...].reshape(half, half)
            result = lax.dot_general(own[...], kept_value, dims, preferred_element_type=f32)
            result += lax.dot_general(other[...], given_value, dims, preferred_element_type=f32)
            result = result.astype(bf16)
            for j in range(count):
                out[lax.rem(j - line + count, count), which] = result[:, j * lanes : (j + 1) * lanes]

    operands, specs = [], []
    for value, kept, given, turned, index in (first, second):
        operands += [value, value, kept, given]
        specs += [
            pl.BlockSpec((rows, half), lambda g, place: (g, place[1])),
            pl.BlockSpec((rows, half), lambda g, place: (g, 1 - place[1])),
        ]
        if turned:
            specs += [
                pl.BlockSpec((half, half), lambda g, place: (place[1], 0)),
                pl.BlockSpec((half, half), lambda g, place: (0, 0)),
            ]
        else:
            specs += [
                pl.BlockSpec((1, half, half), lambda g, place, index=index: (index, 0, place[1])),
                pl.BlockSpec((half, half), lambda g, place: (0, 0)),
            ]
    return pl.pallas_call(
        body,
        out_shape=jax.ShapeDtypeStruct((count, 2, tokens, lanes), bf16),
        grid_spec=pltpu.PrefetchScalarGridSpec(
            num_scalar_prefetch=1,
            grid=(tokens // rows,),
            in_specs=specs,
            out_specs=pl.BlockSpec((count, 2, rows, lanes), lambda g, place: (0, 0, g, 0)),
        ),
        compiler_params=params(),
        cost_estimate=cost(4 * tokens * width * half, 8 * tokens * width),
        name="project_pair",
    )(place, *operands)


def block_rows(order, r, size):
    return pl.ds(pl.multiple_of(order[r] * size, size), size)


def window_filter(load, tap, tiles, reach):
    steps = range(reach // sublanes)
    sums = [jnp.zeros((sublanes, lanes), f32) for _ in range(tiles)]
    for shift in range(sublanes):
        held = {}
        for q in steps:
            weight = tap(shift, q)
            for i in range(tiles):
                if i - q not in held:
                    held[i - q] = load(shift, i - q)
                sums[i] = sums[i] + weight * held[i - q]
    return sums


def own_sum(blocks, up, down, which, rows):
    return (
        blocks[0, which, rows, :].astype(f32)
        + up[which, rows, :].astype(f32)
        + down[which, rows, :].astype(f32)
    ).astype(bf16)


def forward_filter(order, blocks, up, down, spread_taps):
    tokens = up.shape[1]
    taps = spread_taps.shape[0] // sublanes
    n_blocks = order.shape[0]
    size = tokens // n_blocks
    tiles = 8

    def body(order_ref, blocks_ref, up_ref, down_ref, taps_ref, kv_ref, signal_ref, filtered_ref, moved):
        for shift in range(sublanes):
            moved[shift, : taps + sublanes, :] = jnp.zeros((taps + sublanes, lanes), f32)

        def one_block(r, carry):
            rows = pl.ds(pl.multiple_of(r * size, size), size)
            place = block_rows(order_ref, r, size)
            key_part = own_sum(blocks_ref, up_ref, down_ref, 0, rows)
            value_part = own_sum(blocks_ref, up_ref, down_ref, 1, rows)
            kv_ref[0, place, :] = key_part
            kv_ref[1, place, :] = value_part
            product = (key_part.astype(f32) * value_part.astype(f32)).astype(bf16)
            signal_ref[place, :] = product
            moved[0, pl.ds(pl.multiple_of(taps + order_ref[r] * size, size), size), :] = product.astype(f32)
            return carry

        lax.fori_loop(0, n_blocks, one_block, 0)
        for shift in range(1, sublanes):
            moved[shift, taps : taps + tokens, :] = moved[0, taps - shift : taps - shift + tokens, :]

        def run(g, carry):
            start = pl.multiple_of(g * tiles * sublanes, tiles * sublanes)

            def load(shift, at):
                return moved[shift, pl.ds(start + taps + at * sublanes, sublanes), :]

            def tap(shift, q):
                index = q * sublanes + shift
                return taps_ref[index * sublanes : (index + 1) * sublanes, :]

            sums = window_filter(load, tap, tiles, taps)
            for i in range(tiles):
                filtered_ref[pl.ds(start + i * sublanes, sublanes), :] = sums[i]
            return carry

        lax.fori_loop(0, tokens // (tiles * sublanes), run, 0)

    whole = lambda shape: pl.BlockSpec(shape, lambda g, order: (0,) * len(shape))
    return pl.pallas_call(
        body,
        out_shape=(
            jax.ShapeDtypeStruct((2, tokens, lanes), bf16),
            jax.ShapeDtypeStruct((tokens, lanes), bf16),
            jax.ShapeDtypeStruct((tokens, lanes), f32),
        ),
        grid_spec=pltpu.PrefetchScalarGridSpec(
            num_scalar_prefetch=1,
            grid=(1,),
            in_specs=[
                whole((1, 2, tokens, lanes)),
                whole((2, tokens, lanes)),
                whole((2, tokens, lanes)),
                whole(spread_taps.shape),
            ],
            out_specs=(
                whole((2, tokens, lanes)),
                whole((tokens, lanes)),
                whole((tokens, lanes)),
            ),
            scratch_shapes=[pltpu.VMEM((sublanes, taps + tokens, lanes), f32)],
        ),
        compiler_params=params(),
        cost_estimate=cost(400 * tokens * lanes * taps, 12 * tokens * lanes),
        name="forward_filter",
    )(order, blocks, up, down, spread_taps)


def gate_rows(order, blocks, up, down, filtered):
    tokens = up.shape[1]
    n_blocks = order.shape[0]
    size = tokens // n_blocks

    def body(order_ref, blocks_ref, up_ref, down_ref, filtered_ref, out_ref, grad_ref):
        def one_block(r, carry):
            rows = pl.ds(pl.multiple_of(r * size, size), size)
            place = block_rows(order_ref, r, size)
            queries = own_sum(blocks_ref, up_ref, down_ref, 0, rows).astype(f32)
            grad_gated = (
                blocks_ref[0, 1, rows, :].astype(f32)
                + up_ref[1, rows, :].astype(f32)
                + down_ref[1, rows, :].astype(f32)
            )
            kept = filtered_ref[place, :]
            out_ref[rows, :] = (queries * kept).astype(bf16)
            later = pl.ds(pl.multiple_of(tokens + r * size, size), size)
            out_ref[later, :] = (grad_gated * kept).astype(bf16)
            grad_ref[place, :] = (grad_gated * queries).astype(bf16)
            return carry

        lax.fori_loop(0, n_blocks, one_block, 0)

    whole = lambda shape: pl.BlockSpec(shape, lambda g, order: (0,) * len(shape))
    return pl.pallas_call(
        body,
        out_shape=(
            jax.ShapeDtypeStruct((2 * tokens, lanes), bf16),
            jax.ShapeDtypeStruct((tokens, lanes), bf16),
        ),
        grid_spec=pltpu.PrefetchScalarGridSpec(
            num_scalar_prefetch=1,
            grid=(1,),
            in_specs=[
                whole((1, 2, tokens, lanes)),
                whole((2, tokens, lanes)),
                whole((2, tokens, lanes)),
                whole((tokens, lanes)),
            ],
            out_specs=(whole((2 * tokens, lanes)), whole((tokens, lanes))),
        ),
        compiler_params=params(),
        cost_estimate=cost(20 * tokens * lanes, 20 * tokens * lanes),
        name="gate_rows",
    )(order, blocks, up, down, filtered)


def backward_filter(order, grad_filtered, key_values, signal, spread_taps):
    tokens = grad_filtered.shape[0]
    taps = spread_taps.shape[0] // sublanes
    n_blocks = order.shape[0]
    size = tokens // n_blocks
    tiles = 8
    steps = taps // sublanes

    def body(order_ref, grad_ref, kv_ref, signal_ref, taps_ref, out_ref, moved, signal_grad, behind, gradient):
        for shift in range(sublanes):
            moved[shift, tokens - sublanes :, :] = jnp.zeros((taps + sublanes, lanes), f32)
            behind[shift, : taps + sublanes, :] = jnp.zeros((taps + sublanes, lanes), f32)
        moved[0, :tokens, :] = grad_ref[...].astype(f32)
        behind[0, taps:, :] = signal_ref[...].astype(f32)
        gradient[...] = grad_ref[...].astype(f32)
        for shift in range(1, sublanes):
            moved[shift, :tokens, :] = moved[0, shift : shift + tokens, :]
            behind[shift, taps:, :] = behind[0, taps - shift : taps - shift + tokens, :]

        def run(g, carry):
            start = pl.multiple_of(g * tiles * sublanes, tiles * sublanes)

            def load(shift, at):
                return moved[shift, pl.ds(start + (tiles - 1 - at) * sublanes, sublanes), :]

            def tap(shift, q):
                index = q * sublanes + shift
                return taps_ref[index * sublanes : (index + 1) * sublanes, :]

            sums = window_filter(load, tap, tiles, taps)
            for i in range(tiles):
                signal_grad[pl.ds(start + (tiles - 1 - i) * sublanes, sublanes), :] = sums[i]
            return carry

        lax.fori_loop(0, tokens // (tiles * sublanes), run, 0)

        def one_block(r, carry):
            start = pl.multiple_of(r * size, size)
            place = block_rows(order_ref, r, size)
            value = signal_grad[place, :]
            out_ref[pl.ds(start, size), :] = (value * kv_ref[1, place, :].astype(f32)).astype(bf16)
            out_ref[pl.ds(tokens + start, size), :] = (value * kv_ref[0, place, :].astype(f32)).astype(bf16)
            return carry

        lax.fori_loop(0, n_blocks, one_block, 0)

        for shift in range(sublanes):

            def sum_run(g, sums):
                start = pl.multiple_of(g * tiles * sublanes, tiles * sublanes)
                sums = list(sums)
                held = {}
                for i in range(tiles):
                    here = gradient[pl.ds(start + i * sublanes, sublanes), :]
                    for q in range(steps):
                        if i - q not in held:
                            held[i - q] = behind[shift, pl.ds(start + taps + (i - q) * sublanes, sublanes), :]
                        sums[q] = sums[q] + here * held[i - q]
                return tuple(sums)

            zero = tuple(jnp.zeros((sublanes, lanes), f32) for _ in range(steps))
            sums = lax.fori_loop(0, tokens // (tiles * sublanes), sum_run, zero)
            for q in range(steps):
                index = q * sublanes + shift
                signal_grad[index : index + 1, :] = jnp.sum(sums[q], axis=0, keepdims=True)
        out_ref[2 * tokens :, :] = signal_grad[:taps, :].astype(bf16)

    whole = lambda shape: pl.BlockSpec(shape, lambda g, order: (0,) * len(shape))
    return pl.pallas_call(
        body,
        out_shape=jax.ShapeDtypeStruct((2 * tokens + taps, lanes), bf16),
        grid_spec=pltpu.PrefetchScalarGridSpec(
            num_scalar_prefetch=1,
            grid=(1,),
            in_specs=[
                whole((tokens, lanes)),
                whole((2, tokens, lanes)),
                whole((tokens, lanes)),
                whole(spread_taps.shape),
            ],
            out_specs=whole((2 * tokens + taps, lanes)),
            scratch_shapes=[
                pltpu.VMEM((sublanes, tokens + taps, lanes), f32),
                pltpu.VMEM((tokens, lanes), f32),
                pltpu.VMEM((sublanes, tokens + taps, lanes), f32),
                pltpu.VMEM((tokens, lanes), f32),
            ],
        ),
        compiler_params=params(),
        cost_estimate=cost(800 * tokens * lanes * taps, 12 * tokens * lanes),
        name="backward_filter",
    )(order, grad_filtered, key_values, signal, spread_taps)


def merge_blocks(place, block, before, behind, tokens):
    length = len(before) + 1
    rows = 256
    steps = tokens // rows

    def body(place_ref, *refs):
        out = refs[-1]
        own, ups, downs = refs[0], refs[1:length], refs[length : 2 * length - 1]
        line = place_ref[0]
        for offset in range(length):
            if offset == 0:
                value = own[...]
            else:
                value = downs[offset - 1][...] + ups[length - offset - 1][...]
            at = pl.multiple_of(lax.rem(line + offset, length) * lanes, lanes)
            out[0, :, pl.ds(at, lanes)] = value

    spec = pl.BlockSpec((rows, lanes), lambda which, g, place: (which * steps + g, 0))
    return pl.pallas_call(
        body,
        out_shape=jax.ShapeDtypeStruct((2, tokens, length * lanes), bf16),
        grid_spec=pltpu.PrefetchScalarGridSpec(
            num_scalar_prefetch=1,
            grid=(2, steps),
            in_specs=[spec] * (2 * length - 1),
            out_specs=pl.BlockSpec((1, rows, length * lanes), lambda which, g, place: (which, g, 0)),
        ),
        compiler_params=params(),
        cost_estimate=cost(tokens * lanes * 8, 2 * 2 * tokens * lanes * 11),
        name="merge_blocks",
    )(place, block, *before, *behind)


def merge_taps(place, block, before, behind, taps):
    length = len(before) + 1
    last = block.shape[0] // taps - 1

    def body(place_ref, *refs):
        out = refs[-1]
        own, ups, downs = refs[0], refs[1:length], refs[length : 2 * length - 1]
        line = place_ref[0]
        for offset in range(length):
            if offset == 0:
                value = own[...]
            else:
                value = downs[offset - 1][...] + ups[length - offset - 1][...]
            at = pl.multiple_of(lax.rem(line + offset, length) * lanes, lanes)
            out[pl.ds(at, lanes), :] = jnp.transpose(value.astype(f32)).astype(bf16)

    return pl.pallas_call(
        body,
        out_shape=jax.ShapeDtypeStruct((length * lanes, taps), bf16),
        grid_spec=pltpu.PrefetchScalarGridSpec(
            num_scalar_prefetch=1,
            grid=(1,),
            in_specs=[pl.BlockSpec((taps, lanes), lambda g, place: (last, 0))] * (2 * length - 1),
            out_specs=pl.BlockSpec((length * lanes, taps), lambda g, place: (0, 0)),
        ),
        compiler_params=params(),
        cost_estimate=cost(taps * lanes * 8, 2 * taps * lanes * 11),
        name="merge_taps",
    )(place, block, *before, *behind)


def project_back(place, merged, in_weight, given, indices):
    tokens, half = merged[0][0].shape[1:]
    rows = 256
    n = len(merged)

    def body(place_ref, *refs):
        out = refs[-1]
        dims = (((1,), (1,)), ((), ()))
        own = jnp.zeros((rows, half), f32)
        other = jnp.zeros((rows, half), f32)
        for k in range(n):
            value, kept, sent = refs[3 * k], refs[3 * k + 1], refs[3 * k + 2]
            value = value[...].reshape(rows, half)
            own += lax.dot_general(value, kept[...].reshape(half, half), dims, preferred_element_type=f32)
            other += lax.dot_general(value, sent[...], dims, preferred_element_type=f32)
        at = place_ref[1]
        out[:, pl.ds(pl.multiple_of(at * half, half), half)] = own.astype(bf16)
        out[:, pl.ds(pl.multiple_of((1 - at) * half, half), half)] = other.astype(bf16)

    operands, specs = [], []
    for (value, which), sent, index in zip(merged, given, indices):
        operands += [value, in_weight, sent]
        specs += [
            pl.BlockSpec((1, rows, half), lambda g, place, which=which: (which, g, 0)),
            pl.BlockSpec((1, half, half), lambda g, place, index=index: (index, 0, place[1])),
            pl.BlockSpec((half, half), lambda g, place: (0, 0)),
        ]
    return pl.pallas_call(
        body,
        out_shape=jax.ShapeDtypeStruct((tokens, 2 * half), bf16),
        grid_spec=pltpu.PrefetchScalarGridSpec(
            num_scalar_prefetch=1,
            grid=(tokens // rows,),
            in_specs=specs,
            out_specs=pl.BlockSpec((rows, 2 * half), lambda g, place: (g, 0)),
        ),
        compiler_params=params(),
        cost_estimate=cost(4 * n * tokens * half * half, 8 * tokens * half),
        name="project_back",
    )(place, *operands)


def project_out(place, merged, out_weight, given):
    tokens, half = merged.shape[1:]
    rows = 256

    def body(place_ref, value_ref, kept, sent, out):
        value = value_ref[...].reshape(rows, half)
        at = place_ref[1]
        own = jnp.dot(value, kept[...], preferred_element_type=f32)
        other = jnp.dot(value, sent[...], preferred_element_type=f32)
        out[:, pl.ds(pl.multiple_of(at * half, half), half)] = own.astype(bf16)
        out[:, pl.ds(pl.multiple_of((1 - at) * half, half), half)] = other.astype(bf16)

    return pl.pallas_call(
        body,
        out_shape=jax.ShapeDtypeStruct((tokens, 2 * half), bf16),
        grid_spec=pltpu.PrefetchScalarGridSpec(
            num_scalar_prefetch=1,
            grid=(tokens // rows,),
            in_specs=[
                pl.BlockSpec((1, rows, half), lambda g, place: (0, g, 0)),
                pl.BlockSpec((half, half), lambda g, place: (place[1], 0)),
                pl.BlockSpec((half, half), lambda g, place: (0, 0)),
            ],
            out_specs=pl.BlockSpec((rows, 2 * half), lambda g, place: (g, 0)),
        ),
        compiler_params=params(),
        cost_estimate=cost(4 * tokens * half * half, 8 * tokens * half),
        name="project_out",
    )(place, merged, out_weight, given)


def in_gradient(place, turned, merged, which, index, total, running):
    tokens, half = merged.shape[1:]
    rows = 256

    def body(place_ref, own, other, value_ref, *refs):
        kept, sent = refs[-2:]
        value = value_ref[...].reshape(tokens, half)
        kept[...] = jnp.dot(own[...], value, preferred_element_type=f32)[None]
        sent[...] = jnp.dot(other[...], value, preferred_element_type=f32).astype(bf16)

    steps = half // rows
    more = [] if running is None else [running]
    return pl.pallas_call(
        body,
        out_shape=(
            jax.ShapeDtypeStruct((total, half, 2 * half), f32),
            jax.ShapeDtypeStruct((half, half), bf16),
        ),
        grid_spec=pltpu.PrefetchScalarGridSpec(
            num_scalar_prefetch=1,
            grid=(steps,),
            in_specs=[
                pl.BlockSpec((rows, tokens), lambda g, place: (place[1] * steps + g, 0)),
                pl.BlockSpec((rows, tokens), lambda g, place: ((1 - place[1]) * steps + g, 0)),
                pl.BlockSpec((1, tokens, half), lambda g, place: (which, 0, 0)),
            ]
            + [pl.BlockSpec(memory_space=pl.ANY)] * len(more),
            out_specs=(
                pl.BlockSpec((1, rows, half), lambda g, place: (index, g, place[1])),
                pl.BlockSpec((rows, half), lambda g, place: (g, 0)),
            ),
        ),
        input_output_aliases={4: 0} if more else {},
        compiler_params=params(),
        cost_estimate=cost(4 * tokens * half * half, 8 * tokens * half),
        name="in_gradient",
    )(place, turned, turned, merged, *more)


def out_gradient(place, merged, rows_of):
    tokens, half = merged.shape[1:]
    rows = 256
    steps = half // rows

    def body(place_ref, value_ref, own, other, kept, sent):
        value = value_ref[...].reshape(tokens, rows)
        dims = (((0,), (0,)), ((), ()))
        kept[...] = lax.dot_general(value, own[...], dims, preferred_element_type=f32)
        sent[...] = lax.dot_general(value, other[...], dims, preferred_element_type=f32).astype(bf16)

    return pl.pallas_call(
        body,
        out_shape=(
            jax.ShapeDtypeStruct((2 * half, half), f32),
            jax.ShapeDtypeStruct((half, half), bf16),
        ),
        grid_spec=pltpu.PrefetchScalarGridSpec(
            num_scalar_prefetch=1,
            grid=(steps,),
            in_specs=[
                pl.BlockSpec((1, tokens, rows), lambda g, place: (0, 0, g)),
                pl.BlockSpec((tokens, half), lambda g, place: (0, place[1])),
                pl.BlockSpec((tokens, half), lambda g, place: (0, 1 - place[1])),
            ],
            out_specs=(
                pl.BlockSpec((rows, half), lambda g, place: (place[1] * steps + g, 0)),
                pl.BlockSpec((rows, half), lambda g, place: (g, 0)),
            ),
        ),
        compiler_params=params(),
        cost_estimate=cost(4 * tokens * half * half, 8 * tokens * half),
        name="out_gradient",
    )(place, merged, rows_of, rows_of)


def take_in_half(place, running, pieces):
    n = len(pieces)
    half = pieces[0].shape[0]

    def body(place_ref, *refs):
        out = refs[-1]
        for k in range(n):

            @pl.when(pl.program_id(0) == k)
            def _():
                out[...] = refs[k][...].astype(f32)[None]

    return pl.pallas_call(
        body,
        out_shape=jax.ShapeDtypeStruct(running.shape, f32),
        grid_spec=pltpu.PrefetchScalarGridSpec(
            num_scalar_prefetch=1,
            grid=(n,),
            in_specs=[pl.BlockSpec((half, half), lambda g, place: (0, 0))] * n
            + [pl.BlockSpec(memory_space=pl.ANY)],
            out_specs=pl.BlockSpec((1, half, half), lambda g, place: (g, 0, 1 - place[1])),
        ),
        input_output_aliases={n + 1: 0},
        compiler_params=params(),
        cost_estimate=cost(n * half * half, 6 * n * half * half),
        name="take_in_half",
    )(place, *pieces, running)


def take_out_half(place, running, piece):
    half = piece.shape[0]

    def body(place_ref, piece_ref, running_ref, out):
        out[...] = piece_ref[...].astype(f32)

    return pl.pallas_call(
        body,
        out_shape=jax.ShapeDtypeStruct(running.shape, f32),
        grid_spec=pltpu.PrefetchScalarGridSpec(
            num_scalar_prefetch=1,
            grid=(1,),
            in_specs=[
                pl.BlockSpec((half, half), lambda g, place: (0, 0)),
                pl.BlockSpec(memory_space=pl.ANY),
            ],
            out_specs=pl.BlockSpec((half, half), lambda g, place: (1 - place[1], 0)),
        ),
        input_output_aliases={2: 0},
        compiler_params=params(),
        cost_estimate=cost(half * half, 6 * half * half),
        name="take_out_half",
    )(place, piece, running)


def on_paired_mesh(tokens, in_weight, out_weight, filters, cotangent):
    taps = filters.shape[1]
    seq_at, fsdp_at = lax.axis_index("seq"), lax.axis_index("fsdp")
    line, pair = seq_at // 2, seq_at % 2
    place = jnp.stack([line, pair]).astype(jnp.int32)
    half_in, half_out = in_weight.shape[2] // 2, out_weight.shape[0] // 2
    width = tokens.shape[1]
    count = tokens.shape[0] * lax.axis_size("seq")
    relative = jnp.arange(8, dtype=jnp.int32)
    order = (
        2 * crossed(fsdp_at ^ (2 * (relative % 2) + relative // 4)) + (pair ^ (relative // 2 % 2))
    ).astype(jnp.int32)

    def sent_in(i):
        return lax.dynamic_slice_in_dim(in_weight[i], (1 - pair) * half_in, half_in, 1)

    given_k, given_v = flip(sent_in(1), "seq", 1), flip(sent_in(2), "seq", 1)
    x_own, g_own = trade_places(tokens, False), trade_places(cotangent, False)
    x_own, given_k = lax.optimization_barrier((x_own, given_k))
    x_rows = jnp.stack([x_own, flip(x_own, "fsdp", 2), flip(x_own, "seq", 1), flip_both(x_own)])
    x_rows, given_v, g_own = lax.optimization_barrier((x_rows, given_v, g_own))
    x_rows = jnp.stack([x_rows, flip(x_rows, "fsdp", 1)]).reshape(-1, width)
    g_pair = jnp.stack([g_own, flip(g_own, "seq", 1)])
    sent_out = lax.dynamic_slice_in_dim(out_weight, (1 - pair) * half_out, half_out, 0)
    sent_q, sent_out = after((sent_in(0), sent_out), x_rows)
    given_q, given_out = flip(sent_q, "seq", 1), flip(sent_out, "seq", 1)
    g_rows = jnp.stack([g_pair, flip(g_pair, "fsdp", 2)], axis=1)
    g_rows = jnp.stack([g_rows, flip(g_rows, "fsdp", 1)]).reshape(-1, width)
    own_filters = lax.dynamic_slice_in_dim(filters, pair * half_in + line * lanes, lanes, 0)
    spread_taps = jnp.repeat(jnp.transpose(own_filters), sublanes, axis=0)

    kv_blocks = project_pair(
        place,
        (x_rows, in_weight, given_k, False, 1),
        (x_rows, in_weight, given_v, False, 2),
    )
    kv_up, kv_down = line_scatter(kv_blocks)
    qg_blocks = project_pair(
        place,
        (x_rows, in_weight, given_q, False, 0),
        (g_rows, out_weight, given_out, True, 0),
    )
    turned = jnp.transpose(after(x_rows, qg_blocks))
    qg_up, qg_down = line_scatter(qg_blocks)
    key_values, signal, filtered = forward_filter(order, kv_blocks, kv_up, kv_down, spread_taps)
    gated_rows, grad_filtered = gate_rows(order, qg_blocks, qg_up, qg_down, filtered)

    gated_before = [next_block(gated_rows, 1, 1)]
    gated_behind = [next_block(gated_rows, -1, 1)]
    grad_filtered = after(grad_filtered, gated_before[0], gated_behind[0])
    kv_grads = backward_filter(order, grad_filtered, key_values, signal, spread_taps)
    for step in (2, 3):
        gated_before.append(next_block(gated_before[-1], 1, step))
        gated_behind.append(next_block(gated_behind[-1], -1, step))
        if step == 2:
            kv_grads = after(kv_grads, gated_before[-1], gated_behind[-1])
    kv_before = [next_block(kv_grads, 1, 1)]
    kv_behind = [next_block(kv_grads, -1, 1)]
    kv_before.append(next_block(kv_before[0], 1, 2))
    kv_behind.append(next_block(kv_behind[0], -1, 2))

    first = merge_blocks(place, gated_rows, gated_before, gated_behind, count)
    out_kept, out_sent = out_gradient(place, first, g_rows)
    in_kept, q_sent = in_gradient(place, turned, first, 1, 0, in_weight.shape[0], None)
    mixed_part = project_out(place, first, out_weight, given_out)
    out_given, q_given = flip(out_sent, "seq", 1), flip(q_sent, "seq", 1)
    last_up, last_down = after((kv_before[1], kv_behind[1]), out_sent, q_sent, mixed_part)
    kv_before.append(next_block(last_up, 1, 3))
    kv_behind.append(next_block(last_down, -1, 3))

    def across_cores(part):
        parts = part.reshape(2, 4, count // 8, width)
        return added(parts[0], flip(parts[1], "fsdp", 1))

    mixed_part = across_cores(mixed_part)
    kv_behind[2], kv_before[2], mixed_part, out_given, q_given = lax.optimization_barrier(
        (kv_behind[2], kv_before[2], mixed_part, out_given, q_given)
    )
    second = merge_blocks(place, kv_grads, kv_before, kv_behind, count)
    grad_part = project_back(
        place,
        [(first, 1), (second, 0), (second, 1)],
        in_weight,
        [given_q, given_k, given_v],
        [0, 1, 2],
    )

    def outward(parts):
        total = parts[0].astype(f32) + flip(parts[1], "fsdp", 2).astype(f32)
        total += flip(parts[2], "seq", 1).astype(f32) + flip_both(parts[3]).astype(f32)
        return trade_places(total.astype(bf16), True)

    mixed_out = outward(mixed_part)
    grad_part = across_cores(grad_part)
    grad_tokens = outward(grad_part)
    in_kept, k_sent = in_gradient(place, turned, second, 0, 1, in_weight.shape[0], in_kept)
    in_kept, v_sent = in_gradient(place, turned, second, 1, 2, in_weight.shape[0], in_kept)
    half_taps = merge_taps(place, kv_grads, kv_before, kv_behind, taps)
    k_given, v_given = flip(k_sent, "seq", 1), flip(v_sent, "seq", 1)
    given_taps = flip(half_taps, "seq", 1)
    grad_filters = jnp.where(
        pair == 0,
        jnp.concatenate([half_taps, given_taps], 0),
        jnp.concatenate([given_taps, half_taps], 0),
    ).astype(f32)
    grad_out_weight = take_out_half(place, out_kept, out_given)
    grad_in_weight = take_in_half(place, in_kept, [q_given, k_given, v_given])
    return (mixed_out, grad_tokens, grad_in_weight, grad_out_weight, grad_filters)


def solution(mesh):
    placed = (
        P("seq", "fsdp"),
        P(None, "seq", "fsdp"),
        P("fsdp", "seq"),
        P("fsdp", None),
        P("seq", "fsdp"),
    )
    paired = (mesh.shape["seq"], mesh.shape["fsdp"]) == (8, 4)
    return jax.shard_map(
        on_paired_mesh if paired else on_any_mesh,
        mesh=mesh,
        in_specs=placed,
        out_specs=(
            P("seq", "fsdp"),
            P("seq", "fsdp"),
            P(None, "seq", "fsdp"),
            P("fsdp", "seq"),
            P("fsdp", None),
        ),
        check_vma=False,
    )
```

```python
import jax
import jax.numpy as jnp
from jax import lax
from jax.experimental import pallas as pl
from jax.experimental.pallas import tpu as pltpu
from jax.sharding import PartitionSpec as P

highest = lax.Precision.HIGHEST
bf16 = jnp.bfloat16
f32 = jnp.float32
lanes = 128
sublanes = 8
vmem_bytes = 48 * 1024 * 1024


def causal_filter(extended, filters):
    kernel = jnp.flip(jnp.transpose(filters), 0)[:, None, :]
    result = lax.conv_general_dilated(
        extended[None],
        kernel,
        (1,),
        "VALID",
        dimension_numbers=("NWC", "WIO", "NWC"),
        feature_group_count=filters.shape[0],
        precision=highest,
    )
    return result[0]


def reverse_filter(extended, filters):
    kernel = jnp.transpose(filters)[:, None, :]
    result = lax.conv_general_dilated(
        extended[None],
        kernel,
        (1,),
        "VALID",
        dimension_numbers=("NWC", "WIO", "NWC"),
        feature_group_count=filters.shape[0],
        precision=highest,
    )
    return result[0]


def filter_grad(extended, gradient):
    result = lax.conv_general_dilated(
        extended[None],
        gradient[:, None, :],
        (1,),
        "VALID",
        dimension_numbers=("NWC", "WIO", "NWC"),
        feature_group_count=gradient.shape[1],
        precision=highest,
    )
    return jnp.transpose(jnp.flip(result[0], 0))


def to_feature_rows(value):
    wide = lax.all_gather(value, "fsdp", axis=value.ndim - 1, tiled=True)
    return lax.all_to_all(wide, "seq", split_axis=wide.ndim - 1, concat_axis=wide.ndim - 2, tiled=True)


def to_token_rows(partial):
    swapped = lax.all_to_all(
        partial, "seq", split_axis=partial.ndim - 2, concat_axis=partial.ndim - 1, tiled=True
    )
    return lax.psum_scatter(swapped, "fsdp", scatter_dimension=partial.ndim - 1, tiled=True)


def on_any_mesh(tokens, in_weight, out_weight, filters, cotangent):
    taps = filters.shape[1]
    margin = taps - 1
    activations = to_feature_rows(jnp.stack([tokens, cotangent]))
    features, cot_rows = activations[0], activations[1]
    projected_part = jnp.einsum(
        "td,idc->itc", features, in_weight, preferred_element_type=jnp.float32
    ).astype(jnp.bfloat16)
    gated_part = lax.dot_general(
        cot_rows, out_weight, (((1,), (1,)), ((), ())), preferred_element_type=jnp.float32
    ).astype(jnp.bfloat16)
    summed = lax.psum_scatter(
        jnp.concatenate([projected_part, gated_part[None]], 0),
        "seq",
        scatter_dimension=2,
        tiled=True,
    ).astype(jnp.float32)
    queries, key_part, value_part, grad_gated = summed[0], summed[1], summed[2], summed[3]
    channels = queries.shape[1]
    own_filters = lax.dynamic_slice_in_dim(
        filters, lax.axis_index("seq") * channels, channels, 0
    )
    signal = (key_part * value_part).astype(jnp.bfloat16)
    extended = jnp.pad(signal, ((margin, 0), (0, 0))).astype(jnp.float32)
    filtered = causal_filter(extended, own_filters)
    gated = (queries * filtered).astype(jnp.bfloat16)
    grad_queries = grad_gated * filtered
    grad_filtered = (grad_gated * queries).astype(jnp.bfloat16)
    grad_signal = reverse_filter(
        jnp.pad(grad_filtered, ((0, margin), (0, 0))).astype(jnp.float32), own_filters
    )
    own_grad_filters = filter_grad(extended, grad_filtered.astype(jnp.float32))
    grad_projected = jnp.stack(
        [grad_queries, grad_signal * value_part, grad_signal * key_part]
    ).astype(jnp.bfloat16)
    rows = lax.all_gather(
        jnp.concatenate([grad_projected, gated[None]], 0), "seq", axis=2, tiled=True
    )
    grad_filters = lax.all_gather(own_grad_filters, "seq", axis=0, tiled=True)
    mixed_part = jnp.dot(rows[3], out_weight, preferred_element_type=jnp.float32)
    grad_part = jnp.einsum(
        "itc,idc->td", rows[:3], in_weight, preferred_element_type=jnp.float32
    )
    outward = to_token_rows(jnp.stack([mixed_part, grad_part]).astype(jnp.bfloat16))
    grad_in_weight = jnp.einsum(
        "td,itc->idc", features, rows[:3], preferred_element_type=jnp.float32
    )
    grad_out_weight = lax.dot_general(
        rows[3], cot_rows, (((0,), (0,)), ((), ())), preferred_element_type=jnp.float32
    )
    return (outward[0], outward[1], grad_in_weight, grad_out_weight, grad_filters)


def params(**more):
    return pltpu.CompilerParams(vmem_limit_bytes=vmem_bytes, **more)


def cost(flops, moved):
    return pl.CostEstimate(flops=flops, bytes_accessed=moved, transcendentals=0)


def flip(value, axis, bit):
    return lax.ppermute(value, axis, [(i, i ^ bit) for i in range(lax.axis_size(axis))])


def crossed(index):
    return 2 * (index % 2) + index // 2


def trade_places(value, back):
    size = lax.axis_size("fsdp")
    pairs = [
        ((2 * line + pair) * size + own, (2 * own + pair) * size + crossed(line))
        for line in range(size)
        for pair in range(2)
        for own in range(size)
    ]
    return lax.ppermute(value, ("seq", "fsdp"), [p[::-1] for p in pairs] if back else pairs)


def flip_both(value):
    size = lax.axis_size("fsdp")
    pairs = [
        (seq * size + own, (seq ^ 1) * size + (own ^ 2))
        for seq in range(lax.axis_size("seq"))
        for own in range(size)
    ]
    return lax.ppermute(value, ("seq", "fsdp"), pairs)


def after(values, *others):
    return lax.optimization_barrier((values, others))[0]


def along_line(value, by, holds):
    length = lax.axis_size("seq") // 2
    pairs = [
        (2 * i + pair, 2 * (i + by) + pair)
        for i in range(length)
        for pair in range(2)
        if 0 <= i + by < length and holds(i)
    ]
    return lax.ppermute(value, "seq", pairs)


def added(one, other):
    return (one.astype(f32) + other.astype(f32)).astype(bf16)


def scatter_step(blocks, up, down, step):
    length = blocks.shape[0]
    up_in = along_line(up, 1, lambda i: i <= step - 1)
    down_in = along_line(down, -1, lambda i: i >= length - step)
    return up_in, down_in


def scatter_start(blocks):
    return scatter_step(blocks, blocks[blocks.shape[0] - 1], blocks[1], 1)


def scatter_next(blocks, up_in, down_in, step):
    up = added(blocks[blocks.shape[0] - step], up_in)
    down = added(blocks[step], down_in)
    return scatter_step(blocks, up, down, step)


def next_block(block, by, step):
    length = lax.axis_size("seq") // 2
    if by > 0:
        return along_line(block, 1, lambda i: i >= step - 1)
    return along_line(block, -1, lambda i: i <= length - step)


def project_pair(place, first, second):
    near = first[0][0]
    tokens = 2 * near.shape[0] * near.shape[1] * near.shape[2]
    width = near.shape[3]
    half = width // 2
    rows = 2 * near.shape[2]
    count = half // lanes

    def body(place_ref, *refs):
        out = refs[-1]
        line = place_ref[0]
        is_near = pl.program_id(0) < 2
        for which in range(2):
            own, own_far, other, other_far, kept, given = refs[6 * which : 6 * which + 6]
            turned = (first, second)[which][3]
            dims = (((1,), (1,)), ((), ())) if turned else (((1,), (0,)), ((), ()))
            kept_value = kept[...].reshape(half, half)
            given_value = given[...].reshape(half, half)
            own_value = jnp.where(is_near, own[...], own_far[...]).reshape(rows, half)
            other_value = jnp.where(is_near, other[...], other_far[...]).reshape(rows, half)
            result = lax.dot_general(own_value, kept_value, dims, preferred_element_type=f32)
            result += lax.dot_general(other_value, given_value, dims, preferred_element_type=f32)
            result = result.astype(bf16)
            for j in range(count):
                out[lax.rem(j - line + count, count), which] = result[:, j * lanes : (j + 1) * lanes]

    operands, specs = [], []
    for (near, far), kept, (given, given_at), turned, index in (first, second):
        operands += [near, far, near, far, kept, given]
        for mine in (True, False):
            for is_far in (False, True):

                def index_of(g, place, mine=mine, is_far=is_far):
                    at = jnp.maximum(g - 2, 0) if is_far else jnp.minimum(g, 1)
                    return (at, 0, 0, place[1] if mine else 1 - place[1])

                specs.append(pl.BlockSpec((1, 2, rows // 2, half), index_of))
        if turned:
            specs.append(pl.BlockSpec((half, half), lambda g, place: (place[1], 0)))
        else:
            specs.append(pl.BlockSpec((1, half, half), lambda g, place, index=index: (index, 0, place[1])))
        specs.append(pl.BlockSpec((1, half, half), lambda g, place, at=given_at: (at, 0, 0)))
    return pl.pallas_call(
        body,
        out_shape=jax.ShapeDtypeStruct((count, 2, tokens, lanes), bf16),
        grid_spec=pltpu.PrefetchScalarGridSpec(
            num_scalar_prefetch=1,
            grid=(tokens // rows,),
            in_specs=specs,
            out_specs=pl.BlockSpec((count, 2, rows, lanes), lambda g, place: (0, 0, g, 0)),
        ),
        compiler_params=params(),
        cost_estimate=cost(4 * tokens * width * half, 8 * tokens * width),
        name="project_pair",
    )(place, *operands)


def block_rows(order, r, size):
    return pl.ds(pl.multiple_of(order[r] * size, size), size)


def window_filter(load, tap, tiles, reach):
    steps = range(reach // sublanes)
    sums = [jnp.zeros((sublanes, lanes), f32) for _ in range(tiles)]
    for shift in range(sublanes):
        held = {}
        for q in steps:
            weight = tap(shift, q)
            for i in range(tiles):
                if i - q not in held:
                    held[i - q] = load(shift, i - q)
                sums[i] = sums[i] + weight * held[i - q]
    return sums


def own_sum(blocks, up, down, which, rows):
    return (
        blocks[0, which, rows, :].astype(f32)
        + up[which, rows, :].astype(f32)
        + down[which, rows, :].astype(f32)
    ).astype(bf16)


def forward_filter(order, blocks, up, down, spread_taps):
    tokens = up.shape[1]
    taps = spread_taps.shape[0] // sublanes
    n_blocks = order.shape[0]
    size = tokens // n_blocks
    tiles = 8

    def body(order_ref, blocks_ref, up_ref, down_ref, taps_ref, kv_ref, signal_ref, filtered_ref, moved):
        for shift in range(sublanes):
            moved[shift, : taps + sublanes, :] = jnp.zeros((taps + sublanes, lanes), f32)

        def one_block(r, carry):
            rows = pl.ds(pl.multiple_of(r * size, size), size)
            place = block_rows(order_ref, r, size)
            key_part = own_sum(blocks_ref, up_ref, down_ref, 0, rows)
            value_part = own_sum(blocks_ref, up_ref, down_ref, 1, rows)
            kv_ref[0, place, :] = key_part
            kv_ref[1, place, :] = value_part
            product = (key_part.astype(f32) * value_part.astype(f32)).astype(bf16)
            signal_ref[place, :] = product
            moved[0, pl.ds(pl.multiple_of(taps + order_ref[r] * size, size), size), :] = product.astype(f32)
            return carry

        lax.fori_loop(0, n_blocks, one_block, 0)
        for shift in range(1, sublanes):
            moved[shift, taps : taps + tokens, :] = moved[0, taps - shift : taps - shift + tokens, :]

        def run(g, carry):
            start = pl.multiple_of(g * tiles * sublanes, tiles * sublanes)

            def load(shift, at):
                return moved[shift, pl.ds(start + taps + at * sublanes, sublanes), :]

            def tap(shift, q):
                index = q * sublanes + shift
                return taps_ref[index * sublanes : (index + 1) * sublanes, :]

            sums = window_filter(load, tap, tiles, taps)
            for i in range(tiles):
                filtered_ref[pl.ds(start + i * sublanes, sublanes), :] = sums[i]
            return carry

        lax.fori_loop(0, tokens // (tiles * sublanes), run, 0)

    whole = lambda shape: pl.BlockSpec(shape, lambda g, order: (0,) * len(shape))
    return pl.pallas_call(
        body,
        out_shape=(
            jax.ShapeDtypeStruct((2, tokens, lanes), bf16),
            jax.ShapeDtypeStruct((tokens, lanes), bf16),
            jax.ShapeDtypeStruct((tokens, lanes), f32),
        ),
        grid_spec=pltpu.PrefetchScalarGridSpec(
            num_scalar_prefetch=1,
            grid=(1,),
            in_specs=[
                whole((1, 2, tokens, lanes)),
                whole((2, tokens, lanes)),
                whole((2, tokens, lanes)),
                whole(spread_taps.shape),
            ],
            out_specs=(
                whole((2, tokens, lanes)),
                whole((tokens, lanes)),
                whole((tokens, lanes)),
            ),
            scratch_shapes=[pltpu.VMEM((sublanes, taps + tokens, lanes), f32)],
        ),
        compiler_params=params(),
        cost_estimate=cost(400 * tokens * lanes * taps, 12 * tokens * lanes),
        name="forward_filter",
    )(order, blocks, up, down, spread_taps)


def gate_rows(order, blocks, up, down, filtered):
    tokens = up.shape[1]
    n_blocks = order.shape[0]
    size = tokens // n_blocks

    def body(order_ref, blocks_ref, up_ref, down_ref, filtered_ref, out_ref, grad_ref):
        def one_block(r, carry):
            rows = pl.ds(pl.multiple_of(r * size, size), size)
            place = block_rows(order_ref, r, size)
            queries = own_sum(blocks_ref, up_ref, down_ref, 0, rows).astype(f32)
            grad_gated = (
                blocks_ref[0, 1, rows, :].astype(f32)
                + up_ref[1, rows, :].astype(f32)
                + down_ref[1, rows, :].astype(f32)
            )
            kept = filtered_ref[place, :]
            out_ref[rows, :] = (queries * kept).astype(bf16)
            later = pl.ds(pl.multiple_of(tokens + r * size, size), size)
            out_ref[later, :] = (grad_gated * kept).astype(bf16)
            grad_ref[place, :] = (grad_gated * queries).astype(bf16)
            return carry

        lax.fori_loop(0, n_blocks, one_block, 0)

    whole = lambda shape: pl.BlockSpec(shape, lambda g, order: (0,) * len(shape))
    return pl.pallas_call(
        body,
        out_shape=(
            jax.ShapeDtypeStruct((2 * tokens, lanes), bf16),
            jax.ShapeDtypeStruct((tokens, lanes), bf16),
        ),
        grid_spec=pltpu.PrefetchScalarGridSpec(
            num_scalar_prefetch=1,
            grid=(1,),
            in_specs=[
                whole((1, 2, tokens, lanes)),
                whole((2, tokens, lanes)),
                whole((2, tokens, lanes)),
                whole((tokens, lanes)),
            ],
            out_specs=(whole((2 * tokens, lanes)), whole((tokens, lanes))),
        ),
        compiler_params=params(),
        cost_estimate=cost(20 * tokens * lanes, 20 * tokens * lanes),
        name="gate_rows",
    )(order, blocks, up, down, filtered)


def backward_filter(order, grad_filtered, key_values, signal, spread_taps):
    tokens = grad_filtered.shape[0]
    taps = spread_taps.shape[0] // sublanes
    n_blocks = order.shape[0]
    size = tokens // n_blocks
    tiles = 8
    steps = taps // sublanes

    def body(order_ref, grad_ref, kv_ref, signal_ref, taps_ref, out_ref, moved, signal_grad, behind, gradient):
        for shift in range(sublanes):
            moved[shift, tokens - sublanes :, :] = jnp.zeros((taps + sublanes, lanes), f32)
            behind[shift, : taps + sublanes, :] = jnp.zeros((taps + sublanes, lanes), f32)
        moved[0, :tokens, :] = grad_ref[...].astype(f32)
        behind[0, taps:, :] = signal_ref[...].astype(f32)
        gradient[...] = grad_ref[...].astype(f32)
        for shift in range(1, sublanes):
            moved[shift, :tokens, :] = moved[0, shift : shift + tokens, :]
            behind[shift, taps:, :] = behind[0, taps - shift : taps - shift + tokens, :]

        def run(g, carry):
            start = pl.multiple_of(g * tiles * sublanes, tiles * sublanes)

            def load(shift, at):
                return moved[shift, pl.ds(start + (tiles - 1 - at) * sublanes, sublanes), :]

            def tap(shift, q):
                index = q * sublanes + shift
                return taps_ref[index * sublanes : (index + 1) * sublanes, :]

            sums = window_filter(load, tap, tiles, taps)
            for i in range(tiles):
                signal_grad[pl.ds(start + (tiles - 1 - i) * sublanes, sublanes), :] = sums[i]
            return carry

        lax.fori_loop(0, tokens // (tiles * sublanes), run, 0)

        def one_block(r, carry):
            start = pl.multiple_of(r * size, size)
            place = block_rows(order_ref, r, size)
            value = signal_grad[place, :]
            out_ref[pl.ds(start, size), :] = (value * kv_ref[1, place, :].astype(f32)).astype(bf16)
            out_ref[pl.ds(tokens + start, size), :] = (value * kv_ref[0, place, :].astype(f32)).astype(bf16)
            return carry

        lax.fori_loop(0, n_blocks, one_block, 0)

        for shift in range(sublanes):

            def sum_run(g, sums):
                start = pl.multiple_of(g * tiles * sublanes, tiles * sublanes)
                sums = list(sums)
                held = {}
                for i in range(tiles):
                    here = gradient[pl.ds(start + i * sublanes, sublanes), :]
                    for q in range(steps):
                        if i - q not in held:
                            held[i - q] = behind[shift, pl.ds(start + taps + (i - q) * sublanes, sublanes), :]
                        sums[q] = sums[q] + here * held[i - q]
                return tuple(sums)

            zero = tuple(jnp.zeros((sublanes, lanes), f32) for _ in range(steps))
            sums = lax.fori_loop(0, tokens // (tiles * sublanes), sum_run, zero)
            for q in range(steps):
                index = q * sublanes + shift
                signal_grad[index : index + 1, :] = jnp.sum(sums[q], axis=0, keepdims=True)
        out_ref[2 * tokens :, :] = signal_grad[:taps, :].astype(bf16)

    whole = lambda shape: pl.BlockSpec(shape, lambda g, order: (0,) * len(shape))
    return pl.pallas_call(
        body,
        out_shape=jax.ShapeDtypeStruct((2 * tokens + taps, lanes), bf16),
        grid_spec=pltpu.PrefetchScalarGridSpec(
            num_scalar_prefetch=1,
            grid=(1,),
            in_specs=[
                whole((tokens, lanes)),
                whole((2, tokens, lanes)),
                whole((tokens, lanes)),
                whole(spread_taps.shape),
            ],
            out_specs=whole((2 * tokens + taps, lanes)),
            scratch_shapes=[
                pltpu.VMEM((sublanes, tokens + taps, lanes), f32),
                pltpu.VMEM((tokens, lanes), f32),
                pltpu.VMEM((sublanes, tokens + taps, lanes), f32),
                pltpu.VMEM((tokens, lanes), f32),
            ],
        ),
        compiler_params=params(),
        cost_estimate=cost(800 * tokens * lanes * taps, 12 * tokens * lanes),
        name="backward_filter",
    )(order, grad_filtered, key_values, signal, spread_taps)


def merge_blocks(place, block, before, behind, tokens):
    matrices = block.shape[0] // tokens
    length = len(before) + 1
    rows = 256
    steps = tokens // rows

    def body(place_ref, *refs):
        out = refs[-1]
        own, ups, downs = refs[0], refs[1:length], refs[length : 2 * length - 1]
        line = place_ref[0]
        for offset in range(length):
            if offset == 0:
                value = own[...]
            else:
                value = downs[offset - 1][...] + ups[length - offset - 1][...]
            at = pl.multiple_of(lax.rem(line + offset, length) * lanes, lanes)
            out[0, :, pl.ds(at, lanes)] = value

    spec = pl.BlockSpec((rows, lanes), lambda which, g, place: (which * steps + g, 0))
    return pl.pallas_call(
        body,
        out_shape=jax.ShapeDtypeStruct((matrices, tokens, length * lanes), bf16),
        grid_spec=pltpu.PrefetchScalarGridSpec(
            num_scalar_prefetch=1,
            grid=(matrices, steps),
            in_specs=[spec] * (2 * length - 1),
            out_specs=pl.BlockSpec((1, rows, length * lanes), lambda which, g, place: (which, g, 0)),
        ),
        compiler_params=params(),
        cost_estimate=cost(tokens * lanes * 8, 2 * 2 * tokens * lanes * 11),
        name="merge_blocks",
    )(place, block, *before, *behind)


def merge_taps(place, block, before, behind, taps):
    length = len(before) + 1
    last = block.shape[0] // taps - 1

    def body(place_ref, *refs):
        out = refs[-1]
        own, ups, downs = refs[0], refs[1:length], refs[length : 2 * length - 1]
        line = place_ref[0]
        for offset in range(length):
            if offset == 0:
                value = own[...]
            else:
                value = downs[offset - 1][...] + ups[length - offset - 1][...]
            at = pl.multiple_of(lax.rem(line + offset, length) * lanes, lanes)
            out[pl.ds(at, lanes), :] = jnp.transpose(value.astype(f32)).astype(bf16)

    return pl.pallas_call(
        body,
        out_shape=jax.ShapeDtypeStruct((length * lanes, taps), bf16),
        grid_spec=pltpu.PrefetchScalarGridSpec(
            num_scalar_prefetch=1,
            grid=(1,),
            in_specs=[pl.BlockSpec((taps, lanes), lambda g, place: (last, 0))] * (2 * length - 1),
            out_specs=pl.BlockSpec((length * lanes, taps), lambda g, place: (0, 0)),
        ),
        compiler_params=params(),
        cost_estimate=cost(taps * lanes * 8, 2 * taps * lanes * 11),
        name="merge_taps",
    )(place, block, *before, *behind)


def project_back(place, merged, in_weight, given, indices, part):
    tokens, half = merged[0][0].shape[1:]
    rows = 256
    n = len(merged)
    steps = tokens // rows // 2

    def body(place_ref, *refs):
        out = refs[-1]
        dims = (((1,), (1,)), ((), ()))
        own = jnp.zeros((rows, half), f32)
        other = jnp.zeros((rows, half), f32)
        for k in range(n):
            value, kept, sent = refs[3 * k], refs[3 * k + 1], refs[3 * k + 2]
            value = value[...].reshape(rows, half)
            own += lax.dot_general(value, kept[...].reshape(half, half), dims, preferred_element_type=f32)
            other += lax.dot_general(value, sent[...].reshape(half, half), dims, preferred_element_type=f32)
        at = place_ref[1]
        out[:, pl.ds(pl.multiple_of(at * half, half), half)] = own.astype(bf16)
        out[:, pl.ds(pl.multiple_of((1 - at) * half, half), half)] = other.astype(bf16)

    operands, specs = [], []
    for (value, which), (sent, at), index in zip(merged, given, indices):
        operands += [value, in_weight, sent]
        specs += [
            pl.BlockSpec((1, rows, half), lambda g, place, which=which: (which, part * steps + g, 0)),
            pl.BlockSpec((1, half, half), lambda g, place, index=index: (index, 0, place[1])),
            pl.BlockSpec((1, half, half), lambda g, place, at=at: (at, 0, 0)),
        ]
    return pl.pallas_call(
        body,
        out_shape=jax.ShapeDtypeStruct((tokens // 2, 2 * half), bf16),
        grid_spec=pltpu.PrefetchScalarGridSpec(
            num_scalar_prefetch=1,
            grid=(steps,),
            in_specs=specs,
            out_specs=pl.BlockSpec((rows, 2 * half), lambda g, place: (g, 0)),
        ),
        compiler_params=params(),
        cost_estimate=cost(2 * n * tokens * half * half, 4 * tokens * half),
        name="project_back",
    )(place, *operands)


def project_out(place, merged, out_weight, given, at):
    tokens, half = merged.shape[1:]
    rows = 256

    def body(place_ref, value_ref, kept, sent, out):
        value = value_ref[...].reshape(rows, half)
        pair = place_ref[1]
        own = jnp.dot(value, kept[...], preferred_element_type=f32)
        other = jnp.dot(value, sent[...].reshape(half, half), preferred_element_type=f32)
        out[:, pl.ds(pl.multiple_of(pair * half, half), half)] = own.astype(bf16)
        out[:, pl.ds(pl.multiple_of((1 - pair) * half, half), half)] = other.astype(bf16)

    return pl.pallas_call(
        body,
        out_shape=jax.ShapeDtypeStruct((tokens, 2 * half), bf16),
        grid_spec=pltpu.PrefetchScalarGridSpec(
            num_scalar_prefetch=1,
            grid=(tokens // rows,),
            in_specs=[
                pl.BlockSpec((1, rows, half), lambda g, place: (0, g, 0)),
                pl.BlockSpec((half, half), lambda g, place: (place[1], 0)),
                pl.BlockSpec((1, half, half), lambda g, place: (at, 0, 0)),
            ],
            out_specs=pl.BlockSpec((rows, 2 * half), lambda g, place: (g, 0)),
        ),
        compiler_params=params(),
        cost_estimate=cost(4 * tokens * half * half, 8 * tokens * half),
        name="project_out",
    )(place, merged, out_weight, given)


def in_gradient(place, near, far, merged, which, index, total, running):
    tokens, half = merged.shape[1:]
    rows = 256
    steps = half // rows
    block = near.shape[:3] + (rows,)

    def body(place_ref, own, own_far, other, other_far, value_ref, *refs):
        kept, sent = refs[-2:]
        value = value_ref[...].reshape(tokens, half)
        dims = (((0,), (0,)), ((), ()))

        def product(one, two):
            rows_of = jnp.concatenate([one[...].reshape(tokens // 2, rows), two[...].reshape(tokens // 2, rows)], 0)
            return lax.dot_general(rows_of, value, dims, preferred_element_type=f32)

        kept[...] = product(own, own_far)[None]
        sent[...] = product(other, other_far).astype(bf16)

    more = [] if running is None else [running]
    own_spec = pl.BlockSpec(block, lambda g, place: (0, 0, 0, place[1] * steps + g))
    other_spec = pl.BlockSpec(block, lambda g, place: (0, 0, 0, (1 - place[1]) * steps + g))
    return pl.pallas_call(
        body,
        out_shape=(
            jax.ShapeDtypeStruct((total, half, 2 * half), f32),
            jax.ShapeDtypeStruct((half, half), bf16),
        ),
        grid_spec=pltpu.PrefetchScalarGridSpec(
            num_scalar_prefetch=1,
            grid=(steps,),
            in_specs=[own_spec, own_spec, other_spec, other_spec]
            + [pl.BlockSpec((1, tokens, half), lambda g, place: (which, 0, 0))]
            + [pl.BlockSpec(memory_space=pl.ANY)] * len(more),
            out_specs=(
                pl.BlockSpec((1, rows, half), lambda g, place: (index, g, place[1])),
                pl.BlockSpec((rows, half), lambda g, place: (g, 0)),
            ),
        ),
        input_output_aliases={6: 0} if more else {},
        compiler_params=params(),
        cost_estimate=cost(4 * tokens * half * half, 8 * tokens * half),
        name="in_gradient",
    )(place, near, far, near, far, merged, *more)


def out_gradient(place, merged, near, far):
    tokens, half = merged.shape[1:]
    rows = 256
    steps = half // rows
    block = near.shape[:3] + (half,)

    def body(place_ref, value_ref, own, own_far, other, other_far, kept, sent):
        value = value_ref[...].reshape(tokens, rows)
        dims = (((0,), (0,)), ((), ()))

        def in_order(one, two):
            return jnp.concatenate([ref[...].reshape(tokens // 2, half) for ref in (one, two)], 0)

        kept[...] = lax.dot_general(value, in_order(own, own_far), dims, preferred_element_type=f32)
        sent[...] = lax.dot_general(
            value, in_order(other, other_far), dims, preferred_element_type=f32
        ).astype(bf16)

    own_spec = pl.BlockSpec(block, lambda g, place: (0, 0, 0, place[1]))
    other_spec = pl.BlockSpec(block, lambda g, place: (0, 0, 0, 1 - place[1]))
    return pl.pallas_call(
        body,
        out_shape=(
            jax.ShapeDtypeStruct((2 * half, half), f32),
            jax.ShapeDtypeStruct((half, half), bf16),
        ),
        grid_spec=pltpu.PrefetchScalarGridSpec(
            num_scalar_prefetch=1,
            grid=(steps,),
            in_specs=[
                pl.BlockSpec((1, tokens, rows), lambda g, place: (0, 0, g)),
                own_spec,
                own_spec,
                other_spec,
                other_spec,
            ],
            out_specs=(
                pl.BlockSpec((rows, half), lambda g, place: (place[1] * steps + g, 0)),
                pl.BlockSpec((rows, half), lambda g, place: (g, 0)),
            ),
        ),
        compiler_params=params(),
        cost_estimate=cost(4 * tokens * half * half, 8 * tokens * half),
        name="out_gradient",
    )(place, merged, near, far, near, far)


def take_in_half(place, running, piece, index):
    half = piece.shape[0]

    def body(place_ref, piece_ref, running_ref, out):
        out[...] = piece_ref[...].astype(f32)[None]

    return pl.pallas_call(
        body,
        out_shape=jax.ShapeDtypeStruct(running.shape, f32),
        grid_spec=pltpu.PrefetchScalarGridSpec(
            num_scalar_prefetch=1,
            grid=(1,),
            in_specs=[
                pl.BlockSpec((half, half), lambda g, place: (0, 0)),
                pl.BlockSpec(memory_space=pl.ANY),
            ],
            out_specs=pl.BlockSpec((1, half, half), lambda g, place: (index, 0, 1 - place[1])),
        ),
        input_output_aliases={2: 0},
        compiler_params=params(),
        cost_estimate=cost(half * half, 6 * half * half),
        name="take_in_half",
    )(place, piece, running)


def take_out_half(place, running, piece):
    half = piece.shape[0]

    def body(place_ref, piece_ref, running_ref, out):
        out[...] = piece_ref[...].astype(f32)

    return pl.pallas_call(
        body,
        out_shape=jax.ShapeDtypeStruct(running.shape, f32),
        grid_spec=pltpu.PrefetchScalarGridSpec(
            num_scalar_prefetch=1,
            grid=(1,),
            in_specs=[
                pl.BlockSpec((half, half), lambda g, place: (0, 0)),
                pl.BlockSpec(memory_space=pl.ANY),
            ],
            out_specs=pl.BlockSpec((half, half), lambda g, place: (1 - place[1], 0)),
        ),
        input_output_aliases={2: 0},
        compiler_params=params(),
        cost_estimate=cost(half * half, 6 * half * half),
        name="take_out_half",
    )(place, piece, running)


def on_paired_mesh(tokens, in_weight, out_weight, filters, cotangent):
    taps = filters.shape[1]
    seq_at, fsdp_at = lax.axis_index("seq"), lax.axis_index("fsdp")
    line, pair = seq_at // 2, seq_at % 2
    place = jnp.stack([line, pair]).astype(jnp.int32)
    half_in, half_out = in_weight.shape[2] // 2, out_weight.shape[0] // 2
    width = tokens.shape[1]
    count = tokens.shape[0] * lax.axis_size("seq")
    relative = jnp.arange(8, dtype=jnp.int32)
    order = (
        2 * crossed(fsdp_at ^ (2 * (relative % 2) + relative // 4)) + (pair ^ (relative // 2 % 2))
    ).astype(jnp.int32)

    def sent_in(weight, i):
        return lax.dynamic_slice_in_dim(weight[i], (1 - pair) * half_in, half_in, 1)

    def gathered(own):
        return [own, flip(own, "fsdp", 2), flip(own, "seq", 1), flip_both(own)]

    given_kv = flip(jnp.stack([sent_in(in_weight, 1), sent_in(in_weight, 2)]), "seq", 1)
    x_own = trade_places(tokens, False)
    late_in, late_out, late_cot = after((in_weight, out_weight, cotangent), x_own)
    g_own = trade_places(late_cot, False)
    x_near = jnp.stack(gathered(x_own))
    sent_qo = jnp.stack(
        [sent_in(late_in, 0), lax.dynamic_slice_in_dim(late_out, (1 - pair) * half_out, half_out, 0)]
    )
    x_near, given_kv, sent_qo, g_own = lax.optimization_barrier((x_near, given_kv, sent_qo, g_own))
    x_near = x_near.reshape(2, 2, -1, width)
    x_far = flip(x_near, "fsdp", 1)
    given_qo = flip(sent_qo, "seq", 1)
    own_filters = lax.dynamic_slice_in_dim(filters, pair * half_in + line * lanes, lanes, 0)
    spread_taps = jnp.repeat(jnp.transpose(own_filters), sublanes, axis=0)

    kv_blocks = project_pair(
        place,
        ((x_near, x_far), in_weight, (given_kv, 0), False, 1),
        ((x_near, x_far), in_weight, (given_kv, 1), False, 2),
    )
    kv_up, kv_down = scatter_start(kv_blocks)
    kv_up, kv_down, given_qo = lax.optimization_barrier((kv_up, kv_down, given_qo))
    g_near = jnp.stack(gathered(after(g_own, kv_blocks))).reshape(2, 2, -1, width)
    kv_up, kv_down = scatter_next(kv_blocks, kv_up, kv_down, 2)
    g_near, kv_up, kv_down = lax.optimization_barrier((g_near, kv_up, kv_down))
    g_far = flip(g_near, "fsdp", 1)
    qg_blocks = project_pair(
        place,
        ((x_near, x_far), in_weight, (given_qo, 0), False, 0),
        ((g_near, g_far), out_weight, (given_qo, 1), True, 0),
    )
    kv_up, kv_down = scatter_next(kv_blocks, kv_up, kv_down, 3)
    qg_up, qg_down = scatter_start(qg_blocks)
    for step in (2, 3):
        qg_up, qg_down = scatter_next(qg_blocks, qg_up, qg_down, step)
    key_values, signal, filtered = forward_filter(order, kv_blocks, kv_up, kv_down, spread_taps)
    gated_rows, grad_filtered = gate_rows(order, qg_blocks, qg_up, qg_down, filtered)

    gated_before = [next_block(gated_rows, 1, 1)]
    gated_behind = [next_block(gated_rows, -1, 1)]
    grad_filtered = after(grad_filtered, gated_before[0], gated_behind[0])
    kv_grads = backward_filter(order, grad_filtered, key_values, signal, spread_taps)
    gated_before.append(next_block(gated_before[0], 1, 2))
    gated_behind.append(next_block(gated_behind[0], -1, 2))
    kv_grads, gated_before[1], gated_behind[1] = lax.optimization_barrier(
        (kv_grads, gated_before[1], gated_behind[1])
    )
    gated_before.append(next_block(gated_before[1], 1, 3))
    gated_behind.append(next_block(gated_behind[1], -1, 3))
    kv_before = [next_block(kv_grads, 1, 1)]
    kv_behind = [next_block(kv_grads, -1, 1)]
    kv_before.append(next_block(kv_before[0], 1, 2))
    kv_behind.append(next_block(kv_behind[0], -1, 2))

    total_in = in_weight.shape[0]
    first = merge_blocks(place, gated_rows, gated_before, gated_behind, count)
    out_kept, out_sent = out_gradient(place, first, g_near, g_far)
    out_given = flip(out_sent, "seq", 1)
    in_kept, q_sent = in_gradient(place, x_near, x_far, first, 1, 0, total_in, None)
    q_given = flip(q_sent, "seq", 1)
    mixed_part = project_out(place, after(first, out_sent), out_weight, given_qo, 1)
    last_up, last_down, out_given = lax.optimization_barrier(
        after((kv_before[1], kv_behind[1], out_given), q_sent, mixed_part)
    )
    kv_before.append(next_block(last_up, 1, 3))
    kv_behind.append(next_block(last_down, -1, 3))

    mixed_part = mixed_part.reshape(2, 2, 2, count // 8, width)
    mixed_part = added(mixed_part[0], flip(mixed_part[1], "fsdp", 1))
    kv_behind[2], kv_before[2], mixed_part, q_given = lax.optimization_barrier(
        (kv_behind[2], kv_before[2], mixed_part, q_given)
    )
    second = merge_blocks(place, kv_grads, kv_before, kv_behind, count)
    in_kept, k_sent = in_gradient(place, x_near, x_far, second, 0, 1, total_in, in_kept)
    k_given = flip(k_sent, "seq", 1)

    def back(part, value):
        return project_back(
            place,
            [(first, 1), (value, 0), (value, 1)],
            in_weight,
            [(given_qo, 0), (given_kv, 0), (given_kv, 1)],
            [0, 1, 2],
            part,
        )

    far_part = back(1, after(second, k_sent))
    near_part = back(0, after(second, far_part))
    parts = added(near_part, flip(far_part, "fsdp", 1)).reshape(4, count // 8, width)
    mixed_part = added(mixed_part[:, 0], flip(mixed_part[:, 1], "fsdp", 2))
    mixed_part = added(mixed_part[0], flip(mixed_part[1], "seq", 1))
    mixed_out = trade_places(mixed_part, True)
    total = parts[0].astype(f32) + flip(parts[1], "fsdp", 2).astype(f32)
    total += flip(parts[2], "seq", 1).astype(f32) + flip_both(parts[3]).astype(f32)
    in_kept, v_sent = in_gradient(place, x_near, x_far, after(second, parts), 1, 2, total_in, in_kept)
    half_taps = merge_taps(place, kv_grads, kv_before, kv_behind, taps)
    total, k_given, mixed_out = lax.optimization_barrier((total, k_given, mixed_out))
    v_given = flip(v_sent, "seq", 1)
    given_taps = flip(after(half_taps, v_sent), "seq", 1)
    grad_tokens = trade_places(total.astype(bf16), True)
    grad_filters = jnp.where(
        pair == 0,
        jnp.concatenate([half_taps, given_taps], 0),
        jnp.concatenate([given_taps, half_taps], 0),
    ).astype(f32)
    grad_out_weight = take_out_half(place, out_kept, out_given)
    for index, given in enumerate((q_given, k_given, v_given)):
        in_kept = take_in_half(place, in_kept, given, index)
    return (mixed_out, grad_tokens, in_kept, grad_out_weight, grad_filters)


def solution(mesh):
    placed = (
        P("seq", "fsdp"),
        P(None, "seq", "fsdp"),
        P("fsdp", "seq"),
        P("fsdp", None),
        P("seq", "fsdp"),
    )
    paired = (mesh.shape["seq"], mesh.shape["fsdp"]) == (8, 4)
    return jax.shard_map(
        on_paired_mesh if paired else on_any_mesh,
        mesh=mesh,
        in_specs=placed,
        out_specs=(
            P("seq", "fsdp"),
            P("seq", "fsdp"),
            P(None, "seq", "fsdp"),
            P("fsdp", "seq"),
            P("fsdp", None),
        ),
        check_vma=False,
    )
```

```python
import jax
import jax.numpy as jnp
from jax import lax
from jax.experimental import pallas as pl
from jax.experimental.pallas import tpu as pltpu
from jax.sharding import PartitionSpec as P

highest = lax.Precision.HIGHEST
bf16 = jnp.bfloat16
f32 = jnp.float32
lanes = 128
sublanes = 8
vmem_bytes = 48 * 1024 * 1024


def causal_filter(extended, filters):
    kernel = jnp.flip(jnp.transpose(filters), 0)[:, None, :]
    result = lax.conv_general_dilated(
        extended[None],
        kernel,
        (1,),
        "VALID",
        dimension_numbers=("NWC", "WIO", "NWC"),
        feature_group_count=filters.shape[0],
        precision=highest,
    )
    return result[0]


def reverse_filter(extended, filters):
    kernel = jnp.transpose(filters)[:, None, :]
    result = lax.conv_general_dilated(
        extended[None],
        kernel,
        (1,),
        "VALID",
        dimension_numbers=("NWC", "WIO", "NWC"),
        feature_group_count=filters.shape[0],
        precision=highest,
    )
    return result[0]


def filter_grad(extended, gradient):
    result = lax.conv_general_dilated(
        extended[None],
        gradient[:, None, :],
        (1,),
        "VALID",
        dimension_numbers=("NWC", "WIO", "NWC"),
        feature_group_count=gradient.shape[1],
        precision=highest,
    )
    return jnp.transpose(jnp.flip(result[0], 0))


def to_feature_rows(value):
    wide = lax.all_gather(value, "fsdp", axis=value.ndim - 1, tiled=True)
    return lax.all_to_all(wide, "seq", split_axis=wide.ndim - 1, concat_axis=wide.ndim - 2, tiled=True)


def to_token_rows(partial):
    swapped = lax.all_to_all(
        partial, "seq", split_axis=partial.ndim - 2, concat_axis=partial.ndim - 1, tiled=True
    )
    return lax.psum_scatter(swapped, "fsdp", scatter_dimension=partial.ndim - 1, tiled=True)


def on_any_mesh(tokens, in_weight, out_weight, filters, cotangent):
    taps = filters.shape[1]
    margin = taps - 1
    activations = to_feature_rows(jnp.stack([tokens, cotangent]))
    features, cot_rows = activations[0], activations[1]
    projected_part = jnp.einsum(
        "td,idc->itc", features, in_weight, preferred_element_type=jnp.float32
    ).astype(jnp.bfloat16)
    gated_part = lax.dot_general(
        cot_rows, out_weight, (((1,), (1,)), ((), ())), preferred_element_type=jnp.float32
    ).astype(jnp.bfloat16)
    summed = lax.psum_scatter(
        jnp.concatenate([projected_part, gated_part[None]], 0),
        "seq",
        scatter_dimension=2,
        tiled=True,
    ).astype(jnp.float32)
    queries, key_part, value_part, grad_gated = summed[0], summed[1], summed[2], summed[3]
    channels = queries.shape[1]
    own_filters = lax.dynamic_slice_in_dim(
        filters, lax.axis_index("seq") * channels, channels, 0
    )
    signal = (key_part * value_part).astype(jnp.bfloat16)
    extended = jnp.pad(signal, ((margin, 0), (0, 0))).astype(jnp.float32)
    filtered = causal_filter(extended, own_filters)
    gated = (queries * filtered).astype(jnp.bfloat16)
    grad_queries = grad_gated * filtered
    grad_filtered = (grad_gated * queries).astype(jnp.bfloat16)
    grad_signal = reverse_filter(
        jnp.pad(grad_filtered, ((0, margin), (0, 0))).astype(jnp.float32), own_filters
    )
    own_grad_filters = filter_grad(extended, grad_filtered.astype(jnp.float32))
    grad_projected = jnp.stack(
        [grad_queries, grad_signal * value_part, grad_signal * key_part]
    ).astype(jnp.bfloat16)
    rows = lax.all_gather(
        jnp.concatenate([grad_projected, gated[None]], 0), "seq", axis=2, tiled=True
    )
    grad_filters = lax.all_gather(own_grad_filters, "seq", axis=0, tiled=True)
    mixed_part = jnp.dot(rows[3], out_weight, preferred_element_type=jnp.float32)
    grad_part = jnp.einsum(
        "itc,idc->td", rows[:3], in_weight, preferred_element_type=jnp.float32
    )
    outward = to_token_rows(jnp.stack([mixed_part, grad_part]).astype(jnp.bfloat16))
    grad_in_weight = jnp.einsum(
        "td,itc->idc", features, rows[:3], preferred_element_type=jnp.float32
    )
    grad_out_weight = lax.dot_general(
        rows[3], cot_rows, (((0,), (0,)), ((), ())), preferred_element_type=jnp.float32
    )
    return (outward[0], outward[1], grad_in_weight, grad_out_weight, grad_filters)


def params(**more):
    return pltpu.CompilerParams(vmem_limit_bytes=vmem_bytes, **more)


def cost(flops, moved):
    return pl.CostEstimate(flops=flops, bytes_accessed=moved, transcendentals=0)


def flip(value, axis, bit):
    return lax.ppermute(value, axis, [(i, i ^ bit) for i in range(lax.axis_size(axis))])


def crossed(index):
    return 2 * (index % 2) + index // 2


def trade_places(value, back):
    size = lax.axis_size("fsdp")
    pairs = [
        ((2 * line + pair) * size + own, (2 * own + pair) * size + crossed(line))
        for line in range(size)
        for pair in range(2)
        for own in range(size)
    ]
    return lax.ppermute(value, ("seq", "fsdp"), [p[::-1] for p in pairs] if back else pairs)


def flip_both(value):
    size = lax.axis_size("fsdp")
    pairs = [
        (seq * size + own, (seq ^ 1) * size + (own ^ 2))
        for seq in range(lax.axis_size("seq"))
        for own in range(size)
    ]
    return lax.ppermute(value, ("seq", "fsdp"), pairs)


def after(values, *others):
    return lax.optimization_barrier((values, others))[0]


def along_line(value, by, holds):
    length = lax.axis_size("seq") // 2
    pairs = [
        (2 * i + pair, 2 * (i + by) + pair)
        for i in range(length)
        for pair in range(2)
        if 0 <= i + by < length and holds(i)
    ]
    return lax.ppermute(value, "seq", pairs)


def added(one, other):
    return (one.astype(f32) + other.astype(f32)).astype(bf16)


def scatter_step(blocks, up, down, step):
    length = blocks.shape[0]
    up_in = along_line(up, 1, lambda i: i <= step - 1)
    down_in = along_line(down, -1, lambda i: i >= length - step)
    return up_in, down_in


def scatter_start(blocks):
    return scatter_step(blocks, blocks[blocks.shape[0] - 1], blocks[1], 1)


def scatter_next(blocks, up_in, down_in, step):
    up = added(blocks[blocks.shape[0] - step], up_in)
    down = added(blocks[step], down_in)
    return scatter_step(blocks, up, down, step)


def next_block(block, by, step):
    length = lax.axis_size("seq") // 2
    if by > 0:
        return along_line(block, 1, lambda i: i >= step - 1)
    return along_line(block, -1, lambda i: i <= length - step)


def project_pair(place, first, second):
    near = first[0][0]
    tokens = 2 * near.shape[0] * near.shape[1] * near.shape[2]
    width = near.shape[3]
    half = width // 2
    rows = 2 * near.shape[2]
    count = half // lanes

    def body(place_ref, *refs):
        out = refs[-1]
        line = place_ref[0]
        is_near = pl.program_id(0) < 2
        for which in range(2):
            own, own_far, other, other_far, kept, given = refs[6 * which : 6 * which + 6]
            turned = (first, second)[which][3]
            dims = (((1,), (1,)), ((), ())) if turned else (((1,), (0,)), ((), ()))
            kept_value = kept[...].reshape(half, half)
            given_value = given[...].reshape(half, half)
            own_value = jnp.where(is_near, own[...], own_far[...]).reshape(rows, half)
            other_value = jnp.where(is_near, other[...], other_far[...]).reshape(rows, half)
            result = lax.dot_general(own_value, kept_value, dims, preferred_element_type=f32)
            result += lax.dot_general(other_value, given_value, dims, preferred_element_type=f32)
            result = result.astype(bf16)
            for j in range(count):
                out[lax.rem(j - line + count, count), which] = result[:, j * lanes : (j + 1) * lanes]

    operands, specs = [], []
    for (near, far), kept, (given, given_at), turned, index in (first, second):
        operands += [near, far, near, far, kept, given]
        for mine in (True, False):
            for is_far in (False, True):

                def index_of(g, place, mine=mine, is_far=is_far):
                    at = jnp.maximum(g - 2, 0) if is_far else jnp.minimum(g, 1)
                    return (at, 0, 0, place[1] if mine else 1 - place[1])

                specs.append(pl.BlockSpec((1, 2, rows // 2, half), index_of))
        if turned:
            specs.append(pl.BlockSpec((half, half), lambda g, place: (place[1], 0)))
        else:
            specs.append(pl.BlockSpec((1, half, half), lambda g, place, index=index: (index, 0, place[1])))
        specs.append(pl.BlockSpec((1, half, half), lambda g, place, at=given_at: (at, 0, 0)))
    return pl.pallas_call(
        body,
        out_shape=jax.ShapeDtypeStruct((count, 2, tokens, lanes), bf16),
        grid_spec=pltpu.PrefetchScalarGridSpec(
            num_scalar_prefetch=1,
            grid=(tokens // rows,),
            in_specs=specs,
            out_specs=pl.BlockSpec((count, 2, rows, lanes), lambda g, place: (0, 0, g, 0)),
        ),
        compiler_params=params(),
        cost_estimate=cost(4 * tokens * width * half, 8 * tokens * width),
        name="project_pair",
    )(place, *operands)


def block_rows(order, r, size):
    return pl.ds(pl.multiple_of(order[r] * size, size), size)


def window_filter(load, tap, tiles, reach):
    steps = range(reach // sublanes)
    sums = [jnp.zeros((sublanes, lanes), f32) for _ in range(tiles)]
    for shift in range(sublanes):
        held = {}
        for q in steps:
            weight = tap(shift, q)
            for i in range(tiles):
                if i - q not in held:
                    held[i - q] = load(shift, i - q)
                sums[i] = sums[i] + weight * held[i - q]
    return sums


def own_sum(blocks, up, down, which, rows):
    return (
        blocks[0, which, rows, :].astype(f32)
        + up[which, rows, :].astype(f32)
        + down[which, rows, :].astype(f32)
    ).astype(bf16)


def forward_filter(order, blocks, up, down, spread_taps):
    tokens = up.shape[1]
    taps = spread_taps.shape[0] // sublanes
    n_blocks = order.shape[0]
    size = tokens // n_blocks
    tiles = 8

    def body(order_ref, blocks_ref, up_ref, down_ref, taps_ref, kv_ref, signal_ref, filtered_ref, moved):
        for shift in range(sublanes):
            moved[shift, : taps + sublanes, :] = jnp.zeros((taps + sublanes, lanes), f32)

        def one_block(r, carry):
            rows = pl.ds(pl.multiple_of(r * size, size), size)
            place = block_rows(order_ref, r, size)
            key_part = own_sum(blocks_ref, up_ref, down_ref, 0, rows)
            value_part = own_sum(blocks_ref, up_ref, down_ref, 1, rows)
            kv_ref[0, place, :] = key_part
            kv_ref[1, place, :] = value_part
            product = (key_part.astype(f32) * value_part.astype(f32)).astype(bf16)
            signal_ref[place, :] = product
            moved[0, pl.ds(pl.multiple_of(taps + order_ref[r] * size, size), size), :] = product.astype(f32)
            return carry

        lax.fori_loop(0, n_blocks, one_block, 0)
        for shift in range(1, sublanes):
            moved[shift, taps : taps + tokens, :] = moved[0, taps - shift : taps - shift + tokens, :]

        def run(g, carry):
            start = pl.multiple_of(g * tiles * sublanes, tiles * sublanes)

            def load(shift, at):
                return moved[shift, pl.ds(start + taps + at * sublanes, sublanes), :]

            def tap(shift, q):
                index = q * sublanes + shift
                return taps_ref[index * sublanes : (index + 1) * sublanes, :]

            sums = window_filter(load, tap, tiles, taps)
            for i in range(tiles):
                filtered_ref[pl.ds(start + i * sublanes, sublanes), :] = sums[i]
            return carry

        lax.fori_loop(0, tokens // (tiles * sublanes), run, 0)

    whole = lambda shape: pl.BlockSpec(shape, lambda g, order: (0,) * len(shape))
    return pl.pallas_call(
        body,
        out_shape=(
            jax.ShapeDtypeStruct((2, tokens, lanes), bf16),
            jax.ShapeDtypeStruct((tokens, lanes), bf16),
            jax.ShapeDtypeStruct((tokens, lanes), f32),
        ),
        grid_spec=pltpu.PrefetchScalarGridSpec(
            num_scalar_prefetch=1,
            grid=(1,),
            in_specs=[
                whole((1, 2, tokens, lanes)),
                whole((2, tokens, lanes)),
                whole((2, tokens, lanes)),
                whole(spread_taps.shape),
            ],
            out_specs=(
                whole((2, tokens, lanes)),
                whole((tokens, lanes)),
                whole((tokens, lanes)),
            ),
            scratch_shapes=[pltpu.VMEM((sublanes, taps + tokens, lanes), f32)],
        ),
        compiler_params=params(),
        cost_estimate=cost(400 * tokens * lanes * taps, 12 * tokens * lanes),
        name="forward_filter",
    )(order, blocks, up, down, spread_taps)


def gate_rows(order, blocks, up, down, filtered):
    tokens = up.shape[1]
    n_blocks = order.shape[0]
    size = tokens // n_blocks

    def body(order_ref, blocks_ref, up_ref, down_ref, filtered_ref, out_ref, grad_ref):
        def one_block(r, carry):
            rows = pl.ds(pl.multiple_of(r * size, size), size)
            place = block_rows(order_ref, r, size)
            queries = own_sum(blocks_ref, up_ref, down_ref, 0, rows).astype(f32)
            grad_gated = (
                blocks_ref[0, 1, rows, :].astype(f32)
                + up_ref[1, rows, :].astype(f32)
                + down_ref[1, rows, :].astype(f32)
            )
            kept = filtered_ref[place, :]
            out_ref[rows, :] = (queries * kept).astype(bf16)
            later = pl.ds(pl.multiple_of(tokens + r * size, size), size)
            out_ref[later, :] = (grad_gated * kept).astype(bf16)
            grad_ref[place, :] = (grad_gated * queries).astype(bf16)
            return carry

        lax.fori_loop(0, n_blocks, one_block, 0)

    whole = lambda shape: pl.BlockSpec(shape, lambda g, order: (0,) * len(shape))
    return pl.pallas_call(
        body,
        out_shape=(
            jax.ShapeDtypeStruct((2 * tokens, lanes), bf16),
            jax.ShapeDtypeStruct((tokens, lanes), bf16),
        ),
        grid_spec=pltpu.PrefetchScalarGridSpec(
            num_scalar_prefetch=1,
            grid=(1,),
            in_specs=[
                whole((1, 2, tokens, lanes)),
                whole((2, tokens, lanes)),
                whole((2, tokens, lanes)),
                whole((tokens, lanes)),
            ],
            out_specs=(whole((2 * tokens, lanes)), whole((tokens, lanes))),
        ),
        compiler_params=params(),
        cost_estimate=cost(20 * tokens * lanes, 20 * tokens * lanes),
        name="gate_rows",
    )(order, blocks, up, down, filtered)


def backward_filter(order, grad_filtered, key_values, signal, spread_taps):
    tokens = grad_filtered.shape[0]
    taps = spread_taps.shape[0] // sublanes
    n_blocks = order.shape[0]
    size = tokens // n_blocks
    tiles = 8
    steps = taps // sublanes

    def body(order_ref, grad_ref, kv_ref, signal_ref, taps_ref, out_ref, moved, signal_grad, behind, gradient):
        for shift in range(sublanes):
            moved[shift, tokens - sublanes :, :] = jnp.zeros((taps + sublanes, lanes), f32)
            behind[shift, : taps + sublanes, :] = jnp.zeros((taps + sublanes, lanes), f32)
        moved[0, :tokens, :] = grad_ref[...].astype(f32)
        behind[0, taps:, :] = signal_ref[...].astype(f32)
        gradient[...] = grad_ref[...].astype(f32)
        for shift in range(1, sublanes):
            moved[shift, :tokens, :] = moved[0, shift : shift + tokens, :]
            behind[shift, taps:, :] = behind[0, taps - shift : taps - shift + tokens, :]

        def run(g, carry):
            start = pl.multiple_of(g * tiles * sublanes, tiles * sublanes)

            def load(shift, at):
                return moved[shift, pl.ds(start + (tiles - 1 - at) * sublanes, sublanes), :]

            def tap(shift, q):
                index = q * sublanes + shift
                return taps_ref[index * sublanes : (index + 1) * sublanes, :]

            sums = window_filter(load, tap, tiles, taps)
            for i in range(tiles):
                signal_grad[pl.ds(start + (tiles - 1 - i) * sublanes, sublanes), :] = sums[i]
            return carry

        lax.fori_loop(0, tokens // (tiles * sublanes), run, 0)

        def one_block(r, carry):
            start = pl.multiple_of(r * size, size)
            place = block_rows(order_ref, r, size)
            value = signal_grad[place, :]
            out_ref[pl.ds(start, size), :] = (value * kv_ref[1, place, :].astype(f32)).astype(bf16)
            out_ref[pl.ds(tokens + start, size), :] = (value * kv_ref[0, place, :].astype(f32)).astype(bf16)
            return carry

        lax.fori_loop(0, n_blocks, one_block, 0)

        for shift in range(sublanes):

            def sum_run(g, sums):
                start = pl.multiple_of(g * tiles * sublanes, tiles * sublanes)
                sums = list(sums)
                held = {}
                for i in range(tiles):
                    here = gradient[pl.ds(start + i * sublanes, sublanes), :]
                    for q in range(steps):
                        if i - q not in held:
                            held[i - q] = behind[shift, pl.ds(start + taps + (i - q) * sublanes, sublanes), :]
                        sums[q] = sums[q] + here * held[i - q]
                return tuple(sums)

            zero = tuple(jnp.zeros((sublanes, lanes), f32) for _ in range(steps))
            sums = lax.fori_loop(0, tokens // (tiles * sublanes), sum_run, zero)
            for q in range(steps):
                index = q * sublanes + shift
                signal_grad[index : index + 1, :] = jnp.sum(sums[q], axis=0, keepdims=True)
        out_ref[2 * tokens :, :] = signal_grad[:taps, :].astype(bf16)

    whole = lambda shape: pl.BlockSpec(shape, lambda g, order: (0,) * len(shape))
    return pl.pallas_call(
        body,
        out_shape=jax.ShapeDtypeStruct((2 * tokens + taps, lanes), bf16),
        grid_spec=pltpu.PrefetchScalarGridSpec(
            num_scalar_prefetch=1,
            grid=(1,),
            in_specs=[
                whole((tokens, lanes)),
                whole((2, tokens, lanes)),
                whole((tokens, lanes)),
                whole(spread_taps.shape),
            ],
            out_specs=whole((2 * tokens + taps, lanes)),
            scratch_shapes=[
                pltpu.VMEM((sublanes, tokens + taps, lanes), f32),
                pltpu.VMEM((tokens, lanes), f32),
                pltpu.VMEM((sublanes, tokens + taps, lanes), f32),
                pltpu.VMEM((tokens, lanes), f32),
            ],
        ),
        compiler_params=params(),
        cost_estimate=cost(800 * tokens * lanes * taps, 12 * tokens * lanes),
        name="backward_filter",
    )(order, grad_filtered, key_values, signal, spread_taps)


def merge_blocks(place, block, before, behind, tokens):
    matrices = block.shape[0] // tokens
    length = len(before) + 1
    rows = 256
    steps = tokens // rows

    def body(place_ref, *refs):
        out = refs[-1]
        own, ups, downs = refs[0], refs[1:length], refs[length : 2 * length - 1]
        line = place_ref[0]
        for offset in range(length):
            if offset == 0:
                value = own[...]
            else:
                value = downs[offset - 1][...] + ups[length - offset - 1][...]
            at = pl.multiple_of(lax.rem(line + offset, length) * lanes, lanes)
            out[0, :, pl.ds(at, lanes)] = value

    spec = pl.BlockSpec((rows, lanes), lambda which, g, place: (which * steps + g, 0))
    return pl.pallas_call(
        body,
        out_shape=jax.ShapeDtypeStruct((matrices, tokens, length * lanes), bf16),
        grid_spec=pltpu.PrefetchScalarGridSpec(
            num_scalar_prefetch=1,
            grid=(matrices, steps),
            in_specs=[spec] * (2 * length - 1),
            out_specs=pl.BlockSpec((1, rows, length * lanes), lambda which, g, place: (which, g, 0)),
        ),
        compiler_params=params(),
        cost_estimate=cost(tokens * lanes * 8, 2 * 2 * tokens * lanes * 11),
        name="merge_blocks",
    )(place, block, *before, *behind)


def merge_taps(place, block, before, behind, taps):
    length = len(before) + 1
    last = block.shape[0] // taps - 1

    def body(place_ref, *refs):
        out = refs[-1]
        own, ups, downs = refs[0], refs[1:length], refs[length : 2 * length - 1]
        line = place_ref[0]
        for offset in range(length):
            if offset == 0:
                value = own[...]
            else:
                value = downs[offset - 1][...] + ups[length - offset - 1][...]
            at = pl.multiple_of(lax.rem(line + offset, length) * lanes, lanes)
            out[pl.ds(at, lanes), :] = jnp.transpose(value.astype(f32)).astype(bf16)

    return pl.pallas_call(
        body,
        out_shape=jax.ShapeDtypeStruct((length * lanes, taps), bf16),
        grid_spec=pltpu.PrefetchScalarGridSpec(
            num_scalar_prefetch=1,
            grid=(1,),
            in_specs=[pl.BlockSpec((taps, lanes), lambda g, place: (last, 0))] * (2 * length - 1),
            out_specs=pl.BlockSpec((length * lanes, taps), lambda g, place: (0, 0)),
        ),
        compiler_params=params(),
        cost_estimate=cost(taps * lanes * 8, 2 * taps * lanes * 11),
        name="merge_taps",
    )(place, block, *before, *behind)


def project_back(place, merged, in_weight, given, indices, part):
    tokens, half = merged[0][0].shape[1:]
    rows = 256
    n = len(merged)
    steps = tokens // rows // 2

    def body(place_ref, *refs):
        out = refs[-1]
        dims = (((1,), (1,)), ((), ()))
        own = jnp.zeros((rows, half), f32)
        other = jnp.zeros((rows, half), f32)
        for k in range(n):
            value, kept, sent = refs[3 * k], refs[3 * k + 1], refs[3 * k + 2]
            value = value[...].reshape(rows, half)
            own += lax.dot_general(value, kept[...].reshape(half, half), dims, preferred_element_type=f32)
            other += lax.dot_general(value, sent[...].reshape(half, half), dims, preferred_element_type=f32)
        at = place_ref[1]
        out[:, pl.ds(pl.multiple_of(at * half, half), half)] = own.astype(bf16)
        out[:, pl.ds(pl.multiple_of((1 - at) * half, half), half)] = other.astype(bf16)

    operands, specs = [], []
    for (value, which), (sent, at), index in zip(merged, given, indices):
        operands += [value, in_weight, sent]
        specs += [
            pl.BlockSpec((1, rows, half), lambda g, place, which=which: (which, part * steps + g, 0)),
            pl.BlockSpec((1, half, half), lambda g, place, index=index: (index, 0, place[1])),
            pl.BlockSpec((1, half, half), lambda g, place, at=at: (at, 0, 0)),
        ]
    return pl.pallas_call(
        body,
        out_shape=jax.ShapeDtypeStruct((tokens // 2, 2 * half), bf16),
        grid_spec=pltpu.PrefetchScalarGridSpec(
            num_scalar_prefetch=1,
            grid=(steps,),
            in_specs=specs,
            out_specs=pl.BlockSpec((rows, 2 * half), lambda g, place: (g, 0)),
        ),
        compiler_params=params(),
        cost_estimate=cost(2 * n * tokens * half * half, 4 * tokens * half),
        name="project_back",
    )(place, *operands)


def project_out(place, merged, out_weight, given, at):
    tokens, half = merged.shape[1:]
    rows = 256

    def body(place_ref, value_ref, kept, sent, out):
        value = value_ref[...].reshape(rows, half)
        pair = place_ref[1]
        own = jnp.dot(value, kept[...], preferred_element_type=f32)
        other = jnp.dot(value, sent[...].reshape(half, half), preferred_element_type=f32)
        out[:, pl.ds(pl.multiple_of(pair * half, half), half)] = own.astype(bf16)
        out[:, pl.ds(pl.multiple_of((1 - pair) * half, half), half)] = other.astype(bf16)

    return pl.pallas_call(
        body,
        out_shape=jax.ShapeDtypeStruct((tokens, 2 * half), bf16),
        grid_spec=pltpu.PrefetchScalarGridSpec(
            num_scalar_prefetch=1,
            grid=(tokens // rows,),
            in_specs=[
                pl.BlockSpec((1, rows, half), lambda g, place: (0, g, 0)),
                pl.BlockSpec((half, half), lambda g, place: (place[1], 0)),
                pl.BlockSpec((1, half, half), lambda g, place: (at, 0, 0)),
            ],
            out_specs=pl.BlockSpec((rows, 2 * half), lambda g, place: (g, 0)),
        ),
        compiler_params=params(),
        cost_estimate=cost(4 * tokens * half * half, 8 * tokens * half),
        name="project_out",
    )(place, merged, out_weight, given)


def in_gradient(place, near, far, merged, which, index, total, running):
    tokens, half = merged.shape[1:]
    rows = 256
    steps = half // rows
    block = near.shape[:3] + (rows,)

    def body(place_ref, own, own_far, other, other_far, value_ref, *refs):
        kept, sent = refs[-2:]
        value = value_ref[...].reshape(tokens, half)
        dims = (((0,), (0,)), ((), ()))

        def product(one, two):
            rows_of = jnp.concatenate([one[...].reshape(tokens // 2, rows), two[...].reshape(tokens // 2, rows)], 0)
            return lax.dot_general(rows_of, value, dims, preferred_element_type=f32)

        kept[...] = product(own, own_far)[None]
        sent[...] = product(other, other_far).astype(bf16)

    more = [] if running is None else [running]
    own_spec = pl.BlockSpec(block, lambda g, place: (0, 0, 0, place[1] * steps + g))
    other_spec = pl.BlockSpec(block, lambda g, place: (0, 0, 0, (1 - place[1]) * steps + g))
    return pl.pallas_call(
        body,
        out_shape=(
            jax.ShapeDtypeStruct((total, half, 2 * half), f32),
            jax.ShapeDtypeStruct((half, half), bf16),
        ),
        grid_spec=pltpu.PrefetchScalarGridSpec(
            num_scalar_prefetch=1,
            grid=(steps,),
            in_specs=[own_spec, own_spec, other_spec, other_spec]
            + [pl.BlockSpec((1, tokens, half), lambda g, place: (which, 0, 0))]
            + [pl.BlockSpec(memory_space=pl.ANY)] * len(more),
            out_specs=(
                pl.BlockSpec((1, rows, half), lambda g, place: (index, g, place[1])),
                pl.BlockSpec((rows, half), lambda g, place: (g, 0)),
            ),
        ),
        input_output_aliases={6: 0} if more else {},
        compiler_params=params(),
        cost_estimate=cost(4 * tokens * half * half, 8 * tokens * half),
        name="in_gradient",
    )(place, near, far, near, far, merged, *more)


def out_gradient(place, merged, near, far):
    tokens, half = merged.shape[1:]
    rows = 256
    steps = half // rows
    block = near.shape[:3] + (half,)

    def body(place_ref, value_ref, own, own_far, other, other_far, kept, sent):
        value = value_ref[...].reshape(tokens, rows)
        dims = (((0,), (0,)), ((), ()))

        def in_order(one, two):
            return jnp.concatenate([ref[...].reshape(tokens // 2, half) for ref in (one, two)], 0)

        kept[...] = lax.dot_general(value, in_order(own, own_far), dims, preferred_element_type=f32)
        sent[...] = lax.dot_general(
            value, in_order(other, other_far), dims, preferred_element_type=f32
        ).astype(bf16)

    own_spec = pl.BlockSpec(block, lambda g, place: (0, 0, 0, place[1]))
    other_spec = pl.BlockSpec(block, lambda g, place: (0, 0, 0, 1 - place[1]))
    return pl.pallas_call(
        body,
        out_shape=(
            jax.ShapeDtypeStruct((2 * half, half), f32),
            jax.ShapeDtypeStruct((half, half), bf16),
        ),
        grid_spec=pltpu.PrefetchScalarGridSpec(
            num_scalar_prefetch=1,
            grid=(steps,),
            in_specs=[
                pl.BlockSpec((1, tokens, rows), lambda g, place: (0, 0, g)),
                own_spec,
                own_spec,
                other_spec,
                other_spec,
            ],
            out_specs=(
                pl.BlockSpec((rows, half), lambda g, place: (place[1] * steps + g, 0)),
                pl.BlockSpec((rows, half), lambda g, place: (g, 0)),
            ),
        ),
        compiler_params=params(),
        cost_estimate=cost(4 * tokens * half * half, 8 * tokens * half),
        name="out_gradient",
    )(place, merged, near, far, near, far)


def take_in_half(place, running, piece, index):
    half = piece.shape[0]

    def body(place_ref, piece_ref, running_ref, out):
        out[...] = piece_ref[...].astype(f32)[None]

    return pl.pallas_call(
        body,
        out_shape=jax.ShapeDtypeStruct(running.shape, f32),
        grid_spec=pltpu.PrefetchScalarGridSpec(
            num_scalar_prefetch=1,
            grid=(1,),
            in_specs=[
                pl.BlockSpec((half, half), lambda g, place: (0, 0)),
                pl.BlockSpec(memory_space=pl.ANY),
            ],
            out_specs=pl.BlockSpec((1, half, half), lambda g, place: (index, 0, 1 - place[1])),
        ),
        input_output_aliases={2: 0},
        compiler_params=params(),
        cost_estimate=cost(half * half, 6 * half * half),
        name="take_in_half",
    )(place, piece, running)


def take_out_half(place, running, piece):
    half = piece.shape[0]

    def body(place_ref, piece_ref, running_ref, out):
        out[...] = piece_ref[...].astype(f32)

    return pl.pallas_call(
        body,
        out_shape=jax.ShapeDtypeStruct(running.shape, f32),
        grid_spec=pltpu.PrefetchScalarGridSpec(
            num_scalar_prefetch=1,
            grid=(1,),
            in_specs=[
                pl.BlockSpec((half, half), lambda g, place: (0, 0)),
                pl.BlockSpec(memory_space=pl.ANY),
            ],
            out_specs=pl.BlockSpec((half, half), lambda g, place: (1 - place[1], 0)),
        ),
        input_output_aliases={2: 0},
        compiler_params=params(),
        cost_estimate=cost(half * half, 6 * half * half),
        name="take_out_half",
    )(place, piece, running)


def on_paired_mesh(tokens, in_weight, out_weight, filters, cotangent):
    taps = filters.shape[1]
    seq_at, fsdp_at = lax.axis_index("seq"), lax.axis_index("fsdp")
    line, pair = seq_at // 2, seq_at % 2
    place = jnp.stack([line, pair]).astype(jnp.int32)
    half_in, half_out = in_weight.shape[2] // 2, out_weight.shape[0] // 2
    width = tokens.shape[1]
    count = tokens.shape[0] * lax.axis_size("seq")
    relative = jnp.arange(8, dtype=jnp.int32)
    order = (
        2 * crossed(fsdp_at ^ (2 * (relative % 2) + relative // 4)) + (pair ^ (relative // 2 % 2))
    ).astype(jnp.int32)

    def sent_in(weight, i):
        return lax.dynamic_slice_in_dim(weight[i], (1 - pair) * half_in, half_in, 1)

    def gathered(own):
        return [own, flip(own, "fsdp", 2), flip(own, "seq", 1), flip_both(own)]

    given_kv = flip(jnp.stack([sent_in(in_weight, 1), sent_in(in_weight, 2)]), "seq", 1)
    x_own = trade_places(tokens, False)
    late_in, late_out, late_cot = after((in_weight, out_weight, cotangent), x_own)
    g_own = trade_places(late_cot, False)
    x_near = jnp.stack(gathered(x_own))
    sent_qo = jnp.stack(
        [sent_in(late_in, 0), lax.dynamic_slice_in_dim(late_out, (1 - pair) * half_out, half_out, 0)]
    )
    x_near, given_kv, sent_qo, g_own = lax.optimization_barrier((x_near, given_kv, sent_qo, g_own))
    x_near = x_near.reshape(2, 2, -1, width)
    x_far = flip(x_near, "fsdp", 1)
    given_qo = flip(sent_qo, "seq", 1)
    own_filters = lax.dynamic_slice_in_dim(filters, pair * half_in + line * lanes, lanes, 0)
    spread_taps = jnp.repeat(jnp.transpose(own_filters), sublanes, axis=0)

    kv_blocks = project_pair(
        place,
        ((x_near, x_far), in_weight, (given_kv, 0), False, 1),
        ((x_near, x_far), in_weight, (given_kv, 1), False, 2),
    )
    kv_up, kv_down = scatter_start(kv_blocks)
    g_near = jnp.stack(gathered(g_own)).reshape(2, 2, -1, width)
    kv_up, kv_down, given_qo, g_near = lax.optimization_barrier((kv_up, kv_down, given_qo, g_near))
    kv_up, kv_down = scatter_next(kv_blocks, kv_up, kv_down, 2)
    g_far = flip(g_near, "fsdp", 1)
    qg_blocks = project_pair(
        place,
        ((x_near, x_far), in_weight, (given_qo, 0), False, 0),
        ((g_near, g_far), out_weight, (given_qo, 1), True, 0),
    )
    kv_up, kv_down = scatter_next(kv_blocks, kv_up, kv_down, 3)
    qg_up, qg_down = scatter_start(qg_blocks)
    for step in (2, 3):
        qg_up, qg_down = scatter_next(qg_blocks, qg_up, qg_down, step)
    key_values, signal, filtered = forward_filter(order, kv_blocks, kv_up, kv_down, spread_taps)
    gated_rows, grad_filtered = gate_rows(order, qg_blocks, qg_up, qg_down, filtered)

    gated_before = [next_block(gated_rows, 1, 1)]
    gated_behind = [next_block(gated_rows, -1, 1)]
    grad_filtered = after(grad_filtered, gated_before[0], gated_behind[0])
    kv_grads = backward_filter(order, grad_filtered, key_values, signal, spread_taps)
    gated_before.append(next_block(gated_before[0], 1, 2))
    gated_behind.append(next_block(gated_behind[0], -1, 2))
    kv_grads, gated_before[1], gated_behind[1] = lax.optimization_barrier(
        (kv_grads, gated_before[1], gated_behind[1])
    )
    gated_before.append(next_block(gated_before[1], 1, 3))
    gated_behind.append(next_block(gated_behind[1], -1, 3))
    kv_before = [next_block(kv_grads, 1, 1)]
    kv_behind = [next_block(kv_grads, -1, 1)]
    kv_before.append(next_block(kv_before[0], 1, 2))
    kv_behind.append(next_block(kv_behind[0], -1, 2))

    total_in = in_weight.shape[0]
    first = merge_blocks(place, gated_rows, gated_before, gated_behind, count)
    out_kept, out_sent = out_gradient(place, first, g_near, g_far)
    out_given = flip(out_sent, "seq", 1)
    in_kept, q_sent = in_gradient(place, x_near, x_far, first, 1, 0, total_in, None)
    q_given = flip(q_sent, "seq", 1)
    mixed_part = project_out(place, after(first, out_sent), out_weight, given_qo, 1)
    last_up, last_down, out_given = lax.optimization_barrier(
        after((kv_before[1], kv_behind[1], out_given), q_sent, mixed_part)
    )
    kv_before.append(next_block(last_up, 1, 3))
    kv_behind.append(next_block(last_down, -1, 3))

    mixed_part = mixed_part.reshape(2, 2, 2, count // 8, width)
    mixed_part = added(mixed_part[0], flip(mixed_part[1], "fsdp", 1))
    kv_behind[2], kv_before[2], mixed_part, q_given = lax.optimization_barrier(
        (kv_behind[2], kv_before[2], mixed_part, q_given)
    )
    second = merge_blocks(place, kv_grads, kv_before, kv_behind, count)
    in_kept, k_sent = in_gradient(place, x_near, x_far, second, 0, 1, total_in, in_kept)
    k_given = flip(k_sent, "seq", 1)

    def back(part, value):
        return project_back(
            place,
            [(first, 1), (value, 0), (value, 1)],
            in_weight,
            [(given_qo, 0), (given_kv, 0), (given_kv, 1)],
            [0, 1, 2],
            part,
        )

    far_part = back(1, after(second, k_sent))
    near_part = back(0, after(second, far_part))
    parts = added(near_part, flip(far_part, "fsdp", 1)).reshape(4, count // 8, width)
    mixed_part = added(mixed_part[:, 0], flip(mixed_part[:, 1], "fsdp", 2))
    mixed_part = added(mixed_part[0], flip(mixed_part[1], "seq", 1))
    mixed_out = trade_places(mixed_part, True)
    total = parts[0].astype(f32) + flip(parts[1], "fsdp", 2).astype(f32)
    total += flip(parts[2], "seq", 1).astype(f32) + flip_both(parts[3]).astype(f32)
    in_kept, v_sent = in_gradient(place, x_near, x_far, after(second, parts), 1, 2, total_in, in_kept)
    half_taps = merge_taps(place, kv_grads, kv_before, kv_behind, taps)
    total, k_given, mixed_out = lax.optimization_barrier((total, k_given, mixed_out))
    v_given = flip(v_sent, "seq", 1)
    given_taps = flip(after(half_taps, v_sent), "seq", 1)
    grad_tokens = trade_places(total.astype(bf16), True)
    grad_filters = jnp.where(
        pair == 0,
        jnp.concatenate([half_taps, given_taps], 0),
        jnp.concatenate([given_taps, half_taps], 0),
    ).astype(f32)
    grad_out_weight = take_out_half(place, out_kept, out_given)
    for index, given in enumerate((q_given, k_given, v_given)):
        in_kept = take_in_half(place, in_kept, given, index)
    return (mixed_out, grad_tokens, in_kept, grad_out_weight, grad_filters)


def solution(mesh):
    placed = (
        P("seq", "fsdp"),
        P(None, "seq", "fsdp"),
        P("fsdp", "seq"),
        P("fsdp", None),
        P("seq", "fsdp"),
    )
    paired = (mesh.shape["seq"], mesh.shape["fsdp"]) == (8, 4)
    return jax.shard_map(
        on_paired_mesh if paired else on_any_mesh,
        mesh=mesh,
        in_specs=placed,
        out_specs=(
            P("seq", "fsdp"),
            P("seq", "fsdp"),
            P(None, "seq", "fsdp"),
            P("fsdp", "seq"),
            P("fsdp", None),
        ),
        check_vma=False,
    )
```

```python
import jax
import jax.numpy as jnp
from jax import lax
from jax.experimental import pallas as pl
from jax.experimental.pallas import tpu as pltpu
from jax.sharding import PartitionSpec as P

highest = lax.Precision.HIGHEST
bf16 = jnp.bfloat16
f32 = jnp.float32
lanes = 128
sublanes = 8
vmem_bytes = 48 * 1024 * 1024


def causal_filter(extended, filters):
    kernel = jnp.flip(jnp.transpose(filters), 0)[:, None, :]
    result = lax.conv_general_dilated(
        extended[None],
        kernel,
        (1,),
        "VALID",
        dimension_numbers=("NWC", "WIO", "NWC"),
        feature_group_count=filters.shape[0],
        precision=highest,
    )
    return result[0]


def reverse_filter(extended, filters):
    kernel = jnp.transpose(filters)[:, None, :]
    result = lax.conv_general_dilated(
        extended[None],
        kernel,
        (1,),
        "VALID",
        dimension_numbers=("NWC", "WIO", "NWC"),
        feature_group_count=filters.shape[0],
        precision=highest,
    )
    return result[0]


def filter_grad(extended, gradient):
    result = lax.conv_general_dilated(
        extended[None],
        gradient[:, None, :],
        (1,),
        "VALID",
        dimension_numbers=("NWC", "WIO", "NWC"),
        feature_group_count=gradient.shape[1],
        precision=highest,
    )
    return jnp.transpose(jnp.flip(result[0], 0))


def to_feature_rows(value):
    wide = lax.all_gather(value, "fsdp", axis=value.ndim - 1, tiled=True)
    return lax.all_to_all(wide, "seq", split_axis=wide.ndim - 1, concat_axis=wide.ndim - 2, tiled=True)


def to_token_rows(partial):
    swapped = lax.all_to_all(
        partial, "seq", split_axis=partial.ndim - 2, concat_axis=partial.ndim - 1, tiled=True
    )
    return lax.psum_scatter(swapped, "fsdp", scatter_dimension=partial.ndim - 1, tiled=True)


def on_any_mesh(tokens, in_weight, out_weight, filters, cotangent):
    taps = filters.shape[1]
    margin = taps - 1
    activations = to_feature_rows(jnp.stack([tokens, cotangent]))
    features, cot_rows = activations[0], activations[1]
    projected_part = jnp.einsum(
        "td,idc->itc", features, in_weight, preferred_element_type=jnp.float32
    ).astype(jnp.bfloat16)
    gated_part = lax.dot_general(
        cot_rows, out_weight, (((1,), (1,)), ((), ())), preferred_element_type=jnp.float32
    ).astype(jnp.bfloat16)
    summed = lax.psum_scatter(
        jnp.concatenate([projected_part, gated_part[None]], 0),
        "seq",
        scatter_dimension=2,
        tiled=True,
    ).astype(jnp.float32)
    queries, key_part, value_part, grad_gated = summed[0], summed[1], summed[2], summed[3]
    channels = queries.shape[1]
    own_filters = lax.dynamic_slice_in_dim(
        filters, lax.axis_index("seq") * channels, channels, 0
    )
    signal = (key_part * value_part).astype(jnp.bfloat16)
    extended = jnp.pad(signal, ((margin, 0), (0, 0))).astype(jnp.float32)
    filtered = causal_filter(extended, own_filters)
    gated = (queries * filtered).astype(jnp.bfloat16)
    grad_queries = grad_gated * filtered
    grad_filtered = (grad_gated * queries).astype(jnp.bfloat16)
    grad_signal = reverse_filter(
        jnp.pad(grad_filtered, ((0, margin), (0, 0))).astype(jnp.float32), own_filters
    )
    own_grad_filters = filter_grad(extended, grad_filtered.astype(jnp.float32))
    grad_projected = jnp.stack(
        [grad_queries, grad_signal * value_part, grad_signal * key_part]
    ).astype(jnp.bfloat16)
    rows = lax.all_gather(
        jnp.concatenate([grad_projected, gated[None]], 0), "seq", axis=2, tiled=True
    )
    grad_filters = lax.all_gather(own_grad_filters, "seq", axis=0, tiled=True)
    mixed_part = jnp.dot(rows[3], out_weight, preferred_element_type=jnp.float32)
    grad_part = jnp.einsum(
        "itc,idc->td", rows[:3], in_weight, preferred_element_type=jnp.float32
    )
    outward = to_token_rows(jnp.stack([mixed_part, grad_part]).astype(jnp.bfloat16))
    grad_in_weight = jnp.einsum(
        "td,itc->idc", features, rows[:3], preferred_element_type=jnp.float32
    )
    grad_out_weight = lax.dot_general(
        rows[3], cot_rows, (((0,), (0,)), ((), ())), preferred_element_type=jnp.float32
    )
    return (outward[0], outward[1], grad_in_weight, grad_out_weight, grad_filters)


def params(**more):
    return pltpu.CompilerParams(vmem_limit_bytes=vmem_bytes, **more)


def cost(flops, moved):
    return pl.CostEstimate(flops=flops, bytes_accessed=moved, transcendentals=0)


def flip(value, axis, bit):
    return lax.ppermute(value, axis, [(i, i ^ bit) for i in range(lax.axis_size(axis))])


def crossed(index):
    return 2 * (index % 2) + index // 2


def trade_places(value, back):
    size = lax.axis_size("fsdp")
    pairs = [
        ((2 * line + pair) * size + own, (2 * own + pair) * size + crossed(line))
        for line in range(size)
        for pair in range(2)
        for own in range(size)
    ]
    return lax.ppermute(value, ("seq", "fsdp"), [p[::-1] for p in pairs] if back else pairs)


def flip_both(value):
    size = lax.axis_size("fsdp")
    pairs = [
        (seq * size + own, (seq ^ 1) * size + (own ^ 2))
        for seq in range(lax.axis_size("seq"))
        for own in range(size)
    ]
    return lax.ppermute(value, ("seq", "fsdp"), pairs)


def after(values, *others):
    return lax.optimization_barrier((values, others))[0]


def along_line(value, by, holds):
    length = lax.axis_size("seq") // 2
    pairs = [
        (2 * i + pair, 2 * (i + by) + pair)
        for i in range(length)
        for pair in range(2)
        if 0 <= i + by < length and holds(i)
    ]
    return lax.ppermute(value, "seq", pairs)


def added(one, other):
    return (one.astype(f32) + other.astype(f32)).astype(bf16)


def scatter_step(blocks, up, down, step):
    length = blocks.shape[0]
    up_in = along_line(up, 1, lambda i: i <= step - 1)
    down_in = along_line(down, -1, lambda i: i >= length - step)
    return up_in, down_in


def scatter_start(blocks):
    return scatter_step(blocks, blocks[blocks.shape[0] - 1], blocks[1], 1)


def scatter_next(blocks, up_in, down_in, step):
    up = added(blocks[blocks.shape[0] - step], up_in)
    down = added(blocks[step], down_in)
    return scatter_step(blocks, up, down, step)


def around(value, by):
    size = lax.axis_size("seq")
    return lax.ppermute(value, "seq", [(i, (i + 2 * by) % size) for i in range(size)])


def both_ways(before, behind):
    return [[behind[k], before[-1 - k]] for k in range(len(before))]


def next_block(block, by, step):
    length = lax.axis_size("seq") // 2
    if by > 0:
        return along_line(block, 1, lambda i: i >= step - 1)
    return along_line(block, -1, lambda i: i <= length - step)


def project_pair(place, first, second):
    near = first[0][0]
    tokens = 2 * near.shape[0] * near.shape[1] * near.shape[2]
    width = near.shape[3]
    half = width // 2
    rows = 2 * near.shape[2]
    count = half // lanes

    def body(place_ref, *refs):
        out = refs[-1]
        line = place_ref[0]
        is_near = pl.program_id(0) < 2
        for which in range(2):
            own, own_far, other, other_far, kept, given = refs[6 * which : 6 * which + 6]
            turned = (first, second)[which][3]
            dims = (((1,), (1,)), ((), ())) if turned else (((1,), (0,)), ((), ()))
            kept_value = kept[...].reshape(half, half)
            given_value = given[...].reshape(half, half)
            own_value = jnp.where(is_near, own[...], own_far[...]).reshape(rows, half)
            other_value = jnp.where(is_near, other[...], other_far[...]).reshape(rows, half)
            result = lax.dot_general(own_value, kept_value, dims, preferred_element_type=f32)
            result += lax.dot_general(other_value, given_value, dims, preferred_element_type=f32)
            result = result.astype(bf16)
            for j in range(count):
                out[lax.rem(j - line + count, count), which] = result[:, j * lanes : (j + 1) * lanes]

    operands, specs = [], []
    for (near, far), kept, (given, given_at), turned, index in (first, second):
        operands += [near, far, near, far, kept, given]
        for mine in (True, False):
            for is_far in (False, True):

                def index_of(g, place, mine=mine, is_far=is_far):
                    at = jnp.maximum(g - 2, 0) if is_far else jnp.minimum(g, 1)
                    return (at, 0, 0, place[1] if mine else 1 - place[1])

                specs.append(pl.BlockSpec((1, 2, rows // 2, half), index_of))
        if turned:
            specs.append(pl.BlockSpec((half, half), lambda g, place: (place[1], 0)))
        else:
            specs.append(pl.BlockSpec((1, half, half), lambda g, place, index=index: (index, 0, place[1])))
        specs.append(pl.BlockSpec((1, half, half), lambda g, place, at=given_at: (at, 0, 0)))
    return pl.pallas_call(
        body,
        out_shape=jax.ShapeDtypeStruct((count, 2, tokens, lanes), bf16),
        grid_spec=pltpu.PrefetchScalarGridSpec(
            num_scalar_prefetch=1,
            grid=(tokens // rows,),
            in_specs=specs,
            out_specs=pl.BlockSpec((count, 2, rows, lanes), lambda g, place: (0, 0, g, 0)),
        ),
        compiler_params=params(),
        cost_estimate=cost(4 * tokens * width * half, 8 * tokens * width),
        name="project_pair",
    )(place, *operands)


def block_rows(order, r, size):
    return pl.ds(pl.multiple_of(order[r] * size, size), size)


def window_filter(load, tap, tiles, reach):
    steps = range(reach // sublanes)
    sums = [jnp.zeros((sublanes, lanes), f32) for _ in range(tiles)]
    for shift in range(sublanes):
        held = {}
        for q in steps:
            weight = tap(shift, q)
            for i in range(tiles):
                if i - q not in held:
                    held[i - q] = load(shift, i - q)
                sums[i] = sums[i] + weight * held[i - q]
    return sums


def own_sum(blocks, received, which, rows):
    total = blocks[0, which, rows, :].astype(f32)
    for term in received:
        total += term[which, rows, :].astype(f32)
    return total


def forward_filter(order, blocks, received, spread_taps):
    tokens = blocks.shape[2]
    count = len(received)
    taps = spread_taps.shape[0] // sublanes
    n_blocks = order.shape[0]
    size = tokens // n_blocks
    tiles = 8

    def body(order_ref, blocks_ref, *refs):
        terms = refs[:count]
        taps_ref, kv_ref, signal_ref, filtered_ref, moved = refs[count:]
        for shift in range(sublanes):
            moved[shift, : taps + sublanes, :] = jnp.zeros((taps + sublanes, lanes), f32)

        def one_block(r, carry):
            rows = pl.ds(pl.multiple_of(r * size, size), size)
            place = block_rows(order_ref, r, size)
            key_part = own_sum(blocks_ref, terms, 0, rows).astype(bf16)
            value_part = own_sum(blocks_ref, terms, 1, rows).astype(bf16)
            kv_ref[0, place, :] = key_part
            kv_ref[1, place, :] = value_part
            product = (key_part.astype(f32) * value_part.astype(f32)).astype(bf16)
            signal_ref[place, :] = product
            moved[0, pl.ds(pl.multiple_of(taps + order_ref[r] * size, size), size), :] = product.astype(f32)
            return carry

        lax.fori_loop(0, n_blocks, one_block, 0)
        for shift in range(1, sublanes):
            moved[shift, taps : taps + tokens, :] = moved[0, taps - shift : taps - shift + tokens, :]

        def run(g, carry):
            start = pl.multiple_of(g * tiles * sublanes, tiles * sublanes)

            def load(shift, at):
                return moved[shift, pl.ds(start + taps + at * sublanes, sublanes), :]

            def tap(shift, q):
                index = q * sublanes + shift
                return taps_ref[index * sublanes : (index + 1) * sublanes, :]

            sums = window_filter(load, tap, tiles, taps)
            for i in range(tiles):
                filtered_ref[pl.ds(start + i * sublanes, sublanes), :] = sums[i]
            return carry

        lax.fori_loop(0, tokens // (tiles * sublanes), run, 0)

    whole = lambda shape: pl.BlockSpec(shape, lambda g, order: (0,) * len(shape))
    return pl.pallas_call(
        body,
        out_shape=(
            jax.ShapeDtypeStruct((2, tokens, lanes), bf16),
            jax.ShapeDtypeStruct((tokens, lanes), bf16),
            jax.ShapeDtypeStruct((tokens, lanes), f32),
        ),
        grid_spec=pltpu.PrefetchScalarGridSpec(
            num_scalar_prefetch=1,
            grid=(1,),
            in_specs=[
                whole((1, 2, tokens, lanes)),
                *[whole((2, tokens, lanes))] * count,
                whole(spread_taps.shape),
            ],
            out_specs=(
                whole((2, tokens, lanes)),
                whole((tokens, lanes)),
                whole((tokens, lanes)),
            ),
            scratch_shapes=[pltpu.VMEM((sublanes, taps + tokens, lanes), f32)],
        ),
        compiler_params=params(),
        cost_estimate=cost(400 * tokens * lanes * taps, 12 * tokens * lanes),
        name="forward_filter",
    )(order, blocks, *received, spread_taps)


def gate_rows(order, blocks, received, filtered):
    tokens = blocks.shape[2]
    count = len(received)
    n_blocks = order.shape[0]
    size = tokens // n_blocks

    def body(order_ref, blocks_ref, *refs):
        terms = refs[:count]
        filtered_ref, out_ref, grad_ref = refs[count:]

        def one_block(r, carry):
            rows = pl.ds(pl.multiple_of(r * size, size), size)
            place = block_rows(order_ref, r, size)
            queries = own_sum(blocks_ref, terms, 0, rows).astype(bf16).astype(f32)
            grad_gated = own_sum(blocks_ref, terms, 1, rows)
            kept = filtered_ref[place, :]
            out_ref[rows, :] = (queries * kept).astype(bf16)
            later = pl.ds(pl.multiple_of(tokens + r * size, size), size)
            out_ref[later, :] = (grad_gated * kept).astype(bf16)
            grad_ref[place, :] = (grad_gated * queries).astype(bf16)
            return carry

        lax.fori_loop(0, n_blocks, one_block, 0)

    whole = lambda shape: pl.BlockSpec(shape, lambda g, order: (0,) * len(shape))
    return pl.pallas_call(
        body,
        out_shape=(
            jax.ShapeDtypeStruct((2 * tokens, lanes), bf16),
            jax.ShapeDtypeStruct((tokens, lanes), bf16),
        ),
        grid_spec=pltpu.PrefetchScalarGridSpec(
            num_scalar_prefetch=1,
            grid=(1,),
            in_specs=[
                whole((1, 2, tokens, lanes)),
                *[whole((2, tokens, lanes))] * count,
                whole((tokens, lanes)),
            ],
            out_specs=(whole((2 * tokens, lanes)), whole((tokens, lanes))),
        ),
        compiler_params=params(),
        cost_estimate=cost(20 * tokens * lanes, 20 * tokens * lanes),
        name="gate_rows",
    )(order, blocks, *received, filtered)


def backward_filter(order, grad_filtered, key_values, signal, spread_taps):
    tokens = grad_filtered.shape[0]
    taps = spread_taps.shape[0] // sublanes
    n_blocks = order.shape[0]
    size = tokens // n_blocks
    tiles = 8
    steps = taps // sublanes

    def body(order_ref, grad_ref, kv_ref, signal_ref, taps_ref, out_ref, moved, signal_grad, behind, gradient):
        for shift in range(sublanes):
            moved[shift, tokens - sublanes :, :] = jnp.zeros((taps + sublanes, lanes), f32)
            behind[shift, : taps + sublanes, :] = jnp.zeros((taps + sublanes, lanes), f32)
        moved[0, :tokens, :] = grad_ref[...].astype(f32)
        behind[0, taps:, :] = signal_ref[...].astype(f32)
        gradient[...] = grad_ref[...].astype(f32)
        for shift in range(1, sublanes):
            moved[shift, :tokens, :] = moved[0, shift : shift + tokens, :]
            behind[shift, taps:, :] = behind[0, taps - shift : taps - shift + tokens, :]

        def run(g, carry):
            start = pl.multiple_of(g * tiles * sublanes, tiles * sublanes)

            def load(shift, at):
                return moved[shift, pl.ds(start + (tiles - 1 - at) * sublanes, sublanes), :]

            def tap(shift, q):
                index = q * sublanes + shift
                return taps_ref[index * sublanes : (index + 1) * sublanes, :]

            sums = window_filter(load, tap, tiles, taps)
            for i in range(tiles):
                signal_grad[pl.ds(start + (tiles - 1 - i) * sublanes, sublanes), :] = sums[i]
            return carry

        lax.fori_loop(0, tokens // (tiles * sublanes), run, 0)

        def one_block(r, carry):
            start = pl.multiple_of(r * size, size)
            place = block_rows(order_ref, r, size)
            value = signal_grad[place, :]
            out_ref[pl.ds(start, size), :] = (value * kv_ref[1, place, :].astype(f32)).astype(bf16)
            out_ref[pl.ds(tokens + start, size), :] = (value * kv_ref[0, place, :].astype(f32)).astype(bf16)
            return carry

        lax.fori_loop(0, n_blocks, one_block, 0)

        for shift in range(sublanes):

            def sum_run(g, sums):
                start = pl.multiple_of(g * tiles * sublanes, tiles * sublanes)
                sums = list(sums)
                held = {}
                for i in range(tiles):
                    here = gradient[pl.ds(start + i * sublanes, sublanes), :]
                    for q in range(steps):
                        if i - q not in held:
                            held[i - q] = behind[shift, pl.ds(start + taps + (i - q) * sublanes, sublanes), :]
                        sums[q] = sums[q] + here * held[i - q]
                return tuple(sums)

            zero = tuple(jnp.zeros((sublanes, lanes), f32) for _ in range(steps))
            sums = lax.fori_loop(0, tokens // (tiles * sublanes), sum_run, zero)
            for q in range(steps):
                index = q * sublanes + shift
                signal_grad[index : index + 1, :] = jnp.sum(sums[q], axis=0, keepdims=True)
        out_ref[2 * tokens :, :] = signal_grad[:taps, :].astype(bf16)

    whole = lambda shape: pl.BlockSpec(shape, lambda g, order: (0,) * len(shape))
    return pl.pallas_call(
        body,
        out_shape=jax.ShapeDtypeStruct((2 * tokens + taps, lanes), bf16),
        grid_spec=pltpu.PrefetchScalarGridSpec(
            num_scalar_prefetch=1,
            grid=(1,),
            in_specs=[
                whole((tokens, lanes)),
                whole((2, tokens, lanes)),
                whole((tokens, lanes)),
                whole(spread_taps.shape),
            ],
            out_specs=whole((2 * tokens + taps, lanes)),
            scratch_shapes=[
                pltpu.VMEM((sublanes, tokens + taps, lanes), f32),
                pltpu.VMEM((tokens, lanes), f32),
                pltpu.VMEM((sublanes, tokens + taps, lanes), f32),
                pltpu.VMEM((tokens, lanes), f32),
            ],
        ),
        compiler_params=params(),
        cost_estimate=cost(800 * tokens * lanes * taps, 12 * tokens * lanes),
        name="backward_filter",
    )(order, grad_filtered, key_values, signal, spread_taps)


def merge_blocks(place, block, others, tokens):
    matrices = block.shape[0] // tokens
    length = len(others) + 1
    sizes = [len(other) for other in others]
    rows = 256
    steps = tokens // rows

    def body(place_ref, *refs):
        out = refs[-1]
        own, rest = refs[0], list(refs[1:-1])
        line = place_ref[0]
        for offset in range(length):
            if offset == 0:
                value = own[...]
            else:
                value = rest.pop(0)[...]
                for _ in range(sizes[offset - 1] - 1):
                    value += rest.pop(0)[...]
            at = pl.multiple_of(lax.rem(line + offset, length) * lanes, lanes)
            out[0, :, pl.ds(at, lanes)] = value

    spec = pl.BlockSpec((rows, lanes), lambda which, g, place: (which * steps + g, 0))
    return pl.pallas_call(
        body,
        out_shape=jax.ShapeDtypeStruct((matrices, tokens, length * lanes), bf16),
        grid_spec=pltpu.PrefetchScalarGridSpec(
            num_scalar_prefetch=1,
            grid=(matrices, steps),
            in_specs=[spec] * (1 + sum(sizes)),
            out_specs=pl.BlockSpec((1, rows, length * lanes), lambda which, g, place: (which, g, 0)),
        ),
        compiler_params=params(),
        cost_estimate=cost(tokens * lanes * 8, 2 * 2 * tokens * lanes * 11),
        name="merge_blocks",
    )(place, block, *[term for other in others for term in other])


def merge_taps(place, block, others, taps):
    length = len(others) + 1
    sizes = [len(other) for other in others]
    last = block.shape[0] // taps - 1

    def body(place_ref, *refs):
        out = refs[-1]
        own, rest = refs[0], list(refs[1:-1])
        line = place_ref[0]
        for offset in range(length):
            if offset == 0:
                value = own[...]
            else:
                value = rest.pop(0)[...]
                for _ in range(sizes[offset - 1] - 1):
                    value += rest.pop(0)[...]
            at = pl.multiple_of(lax.rem(line + offset, length) * lanes, lanes)
            out[pl.ds(at, lanes), :] = jnp.transpose(value.astype(f32)).astype(bf16)

    return pl.pallas_call(
        body,
        out_shape=jax.ShapeDtypeStruct((length * lanes, taps), bf16),
        grid_spec=pltpu.PrefetchScalarGridSpec(
            num_scalar_prefetch=1,
            grid=(1,),
            in_specs=[pl.BlockSpec((taps, lanes), lambda g, place: (last, 0))] * (1 + sum(sizes)),
            out_specs=pl.BlockSpec((length * lanes, taps), lambda g, place: (0, 0)),
        ),
        compiler_params=params(),
        cost_estimate=cost(taps * lanes * 8, 2 * taps * lanes * 11),
        name="merge_taps",
    )(place, block, *[term for other in others for term in other])


def project_back(place, merged, in_weight, given, indices, part):
    tokens, half = merged[0][0].shape[1:]
    rows = 256
    n = len(merged)
    steps = tokens // rows // 2

    def body(place_ref, *refs):
        out = refs[-1]
        dims = (((1,), (1,)), ((), ()))
        own = jnp.zeros((rows, half), f32)
        other = jnp.zeros((rows, half), f32)
        for k in range(n):
            value, kept, sent = refs[3 * k], refs[3 * k + 1], refs[3 * k + 2]
            value = value[...].reshape(rows, half)
            own += lax.dot_general(value, kept[...].reshape(half, half), dims, preferred_element_type=f32)
            other += lax.dot_general(value, sent[...].reshape(half, half), dims, preferred_element_type=f32)
        at = place_ref[1]
        out[:, pl.ds(pl.multiple_of(at * half, half), half)] = own.astype(bf16)
        out[:, pl.ds(pl.multiple_of((1 - at) * half, half), half)] = other.astype(bf16)

    operands, specs = [], []
    for (value, which), (sent, at), index in zip(merged, given, indices):
        operands += [value, in_weight, sent]
        specs += [
            pl.BlockSpec((1, rows, half), lambda g, place, which=which: (which, part * steps + g, 0)),
            pl.BlockSpec((1, half, half), lambda g, place, index=index: (index, 0, place[1])),
            pl.BlockSpec((1, half, half), lambda g, place, at=at: (at, 0, 0)),
        ]
    return pl.pallas_call(
        body,
        out_shape=jax.ShapeDtypeStruct((tokens // 2, 2 * half), bf16),
        grid_spec=pltpu.PrefetchScalarGridSpec(
            num_scalar_prefetch=1,
            grid=(steps,),
            in_specs=specs,
            out_specs=pl.BlockSpec((rows, 2 * half), lambda g, place: (g, 0)),
        ),
        compiler_params=params(),
        cost_estimate=cost(2 * n * tokens * half * half, 4 * tokens * half),
        name="project_back",
    )(place, *operands)


def project_out(place, merged, out_weight, given, at):
    tokens, half = merged.shape[1:]
    rows = 256

    def body(place_ref, value_ref, kept, sent, out):
        value = value_ref[...].reshape(rows, half)
        pair = place_ref[1]
        own = jnp.dot(value, kept[...], preferred_element_type=f32)
        other = jnp.dot(value, sent[...].reshape(half, half), preferred_element_type=f32)
        out[:, pl.ds(pl.multiple_of(pair * half, half), half)] = own.astype(bf16)
        out[:, pl.ds(pl.multiple_of((1 - pair) * half, half), half)] = other.astype(bf16)

    return pl.pallas_call(
        body,
        out_shape=jax.ShapeDtypeStruct((tokens, 2 * half), bf16),
        grid_spec=pltpu.PrefetchScalarGridSpec(
            num_scalar_prefetch=1,
            grid=(tokens // rows,),
            in_specs=[
                pl.BlockSpec((1, rows, half), lambda g, place: (0, g, 0)),
                pl.BlockSpec((half, half), lambda g, place: (place[1], 0)),
                pl.BlockSpec((1, half, half), lambda g, place: (at, 0, 0)),
            ],
            out_specs=pl.BlockSpec((rows, 2 * half), lambda g, place: (g, 0)),
        ),
        compiler_params=params(),
        cost_estimate=cost(4 * tokens * half * half, 8 * tokens * half),
        name="project_out",
    )(place, merged, out_weight, given)


def in_gradient(place, near, far, merged, which, index, total, running):
    tokens, half = merged.shape[1:]
    rows = 256
    steps = half // rows
    block = near.shape[:3] + (rows,)

    def body(place_ref, own, own_far, other, other_far, value_ref, *refs):
        kept, sent = refs[-2:]
        value = value_ref[...].reshape(tokens, half)
        dims = (((0,), (0,)), ((), ()))

        def product(one, two):
            rows_of = jnp.concatenate([one[...].reshape(tokens // 2, rows), two[...].reshape(tokens // 2, rows)], 0)
            return lax.dot_general(rows_of, value, dims, preferred_element_type=f32)

        kept[...] = product(own, own_far)[None]
        sent[...] = product(other, other_far).astype(bf16)

    more = [] if running is None else [running]
    own_spec = pl.BlockSpec(block, lambda g, place: (0, 0, 0, place[1] * steps + g))
    other_spec = pl.BlockSpec(block, lambda g, place: (0, 0, 0, (1 - place[1]) * steps + g))
    return pl.pallas_call(
        body,
        out_shape=(
            jax.ShapeDtypeStruct((total, half, 2 * half), f32),
            jax.ShapeDtypeStruct((half, half), bf16),
        ),
        grid_spec=pltpu.PrefetchScalarGridSpec(
            num_scalar_prefetch=1,
            grid=(steps,),
            in_specs=[own_spec, own_spec, other_spec, other_spec]
            + [pl.BlockSpec((1, tokens, half), lambda g, place: (which, 0, 0))]
            + [pl.BlockSpec(memory_space=pl.ANY)] * len(more),
            out_specs=(
                pl.BlockSpec((1, rows, half), lambda g, place: (index, g, place[1])),
                pl.BlockSpec((rows, half), lambda g, place: (g, 0)),
            ),
        ),
        input_output_aliases={6: 0} if more else {},
        compiler_params=params(),
        cost_estimate=cost(4 * tokens * half * half, 8 * tokens * half),
        name="in_gradient",
    )(place, near, far, near, far, merged, *more)


def out_gradient(place, merged, near, far):
    tokens, half = merged.shape[1:]
    rows = 256
    steps = half // rows
    block = near.shape[:3] + (half,)

    def body(place_ref, value_ref, own, own_far, other, other_far, kept, sent):
        value = value_ref[...].reshape(tokens, rows)
        dims = (((0,), (0,)), ((), ()))

        def in_order(one, two):
            return jnp.concatenate([ref[...].reshape(tokens // 2, half) for ref in (one, two)], 0)

        kept[...] = lax.dot_general(value, in_order(own, own_far), dims, preferred_element_type=f32)
        sent[...] = lax.dot_general(
            value, in_order(other, other_far), dims, preferred_element_type=f32
        ).astype(bf16)

    own_spec = pl.BlockSpec(block, lambda g, place: (0, 0, 0, place[1]))
    other_spec = pl.BlockSpec(block, lambda g, place: (0, 0, 0, 1 - place[1]))
    return pl.pallas_call(
        body,
        out_shape=(
            jax.ShapeDtypeStruct((2 * half, half), f32),
            jax.ShapeDtypeStruct((half, half), bf16),
        ),
        grid_spec=pltpu.PrefetchScalarGridSpec(
            num_scalar_prefetch=1,
            grid=(steps,),
            in_specs=[
                pl.BlockSpec((1, tokens, rows), lambda g, place: (0, 0, g)),
                own_spec,
                own_spec,
                other_spec,
                other_spec,
            ],
            out_specs=(
                pl.BlockSpec((rows, half), lambda g, place: (place[1] * steps + g, 0)),
                pl.BlockSpec((rows, half), lambda g, place: (g, 0)),
            ),
        ),
        compiler_params=params(),
        cost_estimate=cost(4 * tokens * half * half, 8 * tokens * half),
        name="out_gradient",
    )(place, merged, near, far, near, far)


def take_in_half(place, running, piece, index):
    half = piece.shape[0]

    def body(place_ref, piece_ref, running_ref, out):
        out[...] = piece_ref[...].astype(f32)[None]

    return pl.pallas_call(
        body,
        out_shape=jax.ShapeDtypeStruct(running.shape, f32),
        grid_spec=pltpu.PrefetchScalarGridSpec(
            num_scalar_prefetch=1,
            grid=(1,),
            in_specs=[
                pl.BlockSpec((half, half), lambda g, place: (0, 0)),
                pl.BlockSpec(memory_space=pl.ANY),
            ],
            out_specs=pl.BlockSpec((1, half, half), lambda g, place: (index, 0, 1 - place[1])),
        ),
        input_output_aliases={2: 0},
        compiler_params=params(),
        cost_estimate=cost(half * half, 6 * half * half),
        name="take_in_half",
    )(place, piece, running)


def take_out_half(place, running, piece):
    half = piece.shape[0]

    def body(place_ref, piece_ref, running_ref, out):
        out[...] = piece_ref[...].astype(f32)

    return pl.pallas_call(
        body,
        out_shape=jax.ShapeDtypeStruct(running.shape, f32),
        grid_spec=pltpu.PrefetchScalarGridSpec(
            num_scalar_prefetch=1,
            grid=(1,),
            in_specs=[
                pl.BlockSpec((half, half), lambda g, place: (0, 0)),
                pl.BlockSpec(memory_space=pl.ANY),
            ],
            out_specs=pl.BlockSpec((half, half), lambda g, place: (1 - place[1], 0)),
        ),
        input_output_aliases={2: 0},
        compiler_params=params(),
        cost_estimate=cost(half * half, 6 * half * half),
        name="take_out_half",
    )(place, piece, running)


def on_paired_mesh(tokens, in_weight, out_weight, filters, cotangent):
    taps = filters.shape[1]
    seq_at, fsdp_at = lax.axis_index("seq"), lax.axis_index("fsdp")
    line, pair = seq_at // 2, seq_at % 2
    place = jnp.stack([line, pair]).astype(jnp.int32)
    half_in, half_out = in_weight.shape[2] // 2, out_weight.shape[0] // 2
    width = tokens.shape[1]
    count = tokens.shape[0] * lax.axis_size("seq")
    relative = jnp.arange(8, dtype=jnp.int32)
    order = (
        2 * crossed(fsdp_at ^ (2 * (relative % 2) + relative // 4)) + (pair ^ (relative // 2 % 2))
    ).astype(jnp.int32)

    def sent_in(weight, i):
        return lax.dynamic_slice_in_dim(weight[i], (1 - pair) * half_in, half_in, 1)

    def gathered(own):
        return [own, flip(own, "fsdp", 2), flip(own, "seq", 1), flip_both(own)]

    given_kv = flip(jnp.stack([sent_in(in_weight, 1), sent_in(in_weight, 2)]), "seq", 1)
    x_own = trade_places(tokens, False)
    late_in, late_out, late_cot = after((in_weight, out_weight, cotangent), x_own)
    g_own = trade_places(late_cot, False)
    x_near = jnp.stack(gathered(x_own))
    sent_qo = jnp.stack(
        [sent_in(late_in, 0), lax.dynamic_slice_in_dim(late_out, (1 - pair) * half_out, half_out, 0)]
    )
    x_near, given_kv, sent_qo, g_own = lax.optimization_barrier((x_near, given_kv, sent_qo, g_own))
    x_near = x_near.reshape(2, 2, -1, width)
    x_far = flip(x_near, "fsdp", 1)
    given_qo = flip(sent_qo, "seq", 1)
    own_filters = lax.dynamic_slice_in_dim(filters, pair * half_in + line * lanes, lanes, 0)
    spread_taps = jnp.repeat(jnp.transpose(own_filters), sublanes, axis=0)

    kv_blocks = project_pair(
        place,
        ((x_near, x_far), in_weight, (given_kv, 0), False, 1),
        ((x_near, x_far), in_weight, (given_kv, 1), False, 2),
    )
    kv_up, kv_down = scatter_start(kv_blocks)
    g_near = jnp.stack(gathered(g_own)).reshape(2, 2, -1, width)
    kv_up, kv_down, given_qo, g_near = lax.optimization_barrier((kv_up, kv_down, given_qo, g_near))
    kv_up, kv_down = scatter_next(kv_blocks, kv_up, kv_down, 2)
    g_far = flip(g_near, "fsdp", 1)
    qg_blocks = project_pair(
        place,
        ((x_near, x_far), in_weight, (given_qo, 0), False, 0),
        ((g_near, g_far), out_weight, (given_qo, 1), True, 0),
    )
    kv_up, kv_down = scatter_next(kv_blocks, kv_up, kv_down, 3)
    qg_up, qg_down = scatter_start(qg_blocks)
    for step in (2, 3):
        qg_up, qg_down = scatter_next(qg_blocks, qg_up, qg_down, step)
    key_values, signal, filtered = forward_filter(order, kv_blocks, [kv_up, kv_down], spread_taps)
    gated_rows, grad_filtered = gate_rows(order, qg_blocks, [qg_up, qg_down], filtered)

    gated_others = [[around(gated_rows, -k)] for k in range(1, 4)]
    kv_grads = backward_filter(order, grad_filtered, key_values, signal, spread_taps)
    kv_before = [next_block(kv_grads, 1, 1)]
    kv_behind = [next_block(kv_grads, -1, 1)]
    kv_before.append(next_block(kv_before[0], 1, 2))
    kv_behind.append(next_block(kv_behind[0], -1, 2))

    total_in = in_weight.shape[0]
    first = merge_blocks(place, gated_rows, gated_others, count)
    out_kept, out_sent = out_gradient(place, first, g_near, g_far)
    out_given = flip(out_sent, "seq", 1)
    in_kept, q_sent = in_gradient(place, x_near, x_far, first, 1, 0, total_in, None)
    q_given = flip(q_sent, "seq", 1)
    mixed_part = project_out(place, after(first, out_sent), out_weight, given_qo, 1)
    last_up, last_down, out_given = lax.optimization_barrier(
        after((kv_before[1], kv_behind[1], out_given), q_sent, mixed_part)
    )
    kv_before.append(next_block(last_up, 1, 3))
    kv_behind.append(next_block(last_down, -1, 3))

    mixed_part = mixed_part.reshape(2, 2, 2, count // 8, width)
    mixed_part = added(mixed_part[0], flip(mixed_part[1], "fsdp", 1))
    kv_behind[2], kv_before[2], mixed_part, q_given = lax.optimization_barrier(
        (kv_behind[2], kv_before[2], mixed_part, q_given)
    )
    second = merge_blocks(place, kv_grads, both_ways(kv_before, kv_behind), count)
    in_kept, k_sent = in_gradient(place, x_near, x_far, second, 0, 1, total_in, in_kept)
    k_given = flip(k_sent, "seq", 1)

    def back(part, value):
        return project_back(
            place,
            [(first, 1), (value, 0), (value, 1)],
            in_weight,
            [(given_qo, 0), (given_kv, 0), (given_kv, 1)],
            [0, 1, 2],
            part,
        )

    far_part = back(1, after(second, k_sent))
    near_part = back(0, after(second, far_part))
    parts = added(near_part, flip(far_part, "fsdp", 1)).reshape(4, count // 8, width)
    mixed_part = added(mixed_part[:, 0], flip(mixed_part[:, 1], "fsdp", 2))
    mixed_part = added(mixed_part[0], flip(mixed_part[1], "seq", 1))
    mixed_out = trade_places(mixed_part, True)
    total = parts[0].astype(f32) + flip(parts[1], "fsdp", 2).astype(f32)
    total += flip(parts[2], "seq", 1).astype(f32) + flip_both(parts[3]).astype(f32)
    in_kept, v_sent = in_gradient(place, x_near, x_far, after(second, parts), 1, 2, total_in, in_kept)
    half_taps = merge_taps(place, kv_grads, both_ways(kv_before, kv_behind), taps)
    total, k_given, mixed_out = lax.optimization_barrier((total, k_given, mixed_out))
    v_given = flip(v_sent, "seq", 1)
    given_taps = flip(after(half_taps, v_sent), "seq", 1)
    grad_tokens = trade_places(total.astype(bf16), True)
    grad_filters = jnp.where(
        pair == 0,
        jnp.concatenate([half_taps, given_taps], 0),
        jnp.concatenate([given_taps, half_taps], 0),
    ).astype(f32)
    grad_out_weight = take_out_half(place, out_kept, out_given)
    for index, given in enumerate((q_given, k_given, v_given)):
        in_kept = take_in_half(place, in_kept, given, index)
    return (mixed_out, grad_tokens, in_kept, grad_out_weight, grad_filters)


def solution(mesh):
    placed = (
        P("seq", "fsdp"),
        P(None, "seq", "fsdp"),
        P("fsdp", "seq"),
        P("fsdp", None),
        P("seq", "fsdp"),
    )
    paired = (mesh.shape["seq"], mesh.shape["fsdp"]) == (8, 4)
    return jax.shard_map(
        on_paired_mesh if paired else on_any_mesh,
        mesh=mesh,
        in_specs=placed,
        out_specs=(
            P("seq", "fsdp"),
            P("seq", "fsdp"),
            P(None, "seq", "fsdp"),
            P("fsdp", "seq"),
            P("fsdp", None),
        ),
        check_vma=False,
    )
```

```python
import jax
import jax.numpy as jnp
from jax import lax
from jax.experimental import pallas as pl
from jax.experimental.pallas import tpu as pltpu
from jax.sharding import PartitionSpec as P

highest = lax.Precision.HIGHEST
bf16 = jnp.bfloat16
f32 = jnp.float32
lanes = 128
sublanes = 8
vmem_bytes = 24 * 1024 * 1024


def causal_filter(extended, filters):
    kernel = jnp.flip(jnp.transpose(filters), 0)[:, None, :]
    result = lax.conv_general_dilated(
        extended[None],
        kernel,
        (1,),
        "VALID",
        dimension_numbers=("NWC", "WIO", "NWC"),
        feature_group_count=filters.shape[0],
        precision=highest,
    )
    return result[0]


def reverse_filter(extended, filters):
    kernel = jnp.transpose(filters)[:, None, :]
    result = lax.conv_general_dilated(
        extended[None],
        kernel,
        (1,),
        "VALID",
        dimension_numbers=("NWC", "WIO", "NWC"),
        feature_group_count=filters.shape[0],
        precision=highest,
    )
    return result[0]


def filter_grad(extended, gradient):
    result = lax.conv_general_dilated(
        extended[None],
        gradient[:, None, :],
        (1,),
        "VALID",
        dimension_numbers=("NWC", "WIO", "NWC"),
        feature_group_count=gradient.shape[1],
        precision=highest,
    )
    return jnp.transpose(jnp.flip(result[0], 0))


def to_feature_rows(value):
    wide = lax.all_gather(value, "fsdp", axis=value.ndim - 1, tiled=True)
    return lax.all_to_all(wide, "seq", split_axis=wide.ndim - 1, concat_axis=wide.ndim - 2, tiled=True)


def to_token_rows(partial):
    swapped = lax.all_to_all(
        partial, "seq", split_axis=partial.ndim - 2, concat_axis=partial.ndim - 1, tiled=True
    )
    return lax.psum_scatter(swapped, "fsdp", scatter_dimension=partial.ndim - 1, tiled=True)


def on_any_mesh(tokens, in_weight, out_weight, filters, cotangent):
    taps = filters.shape[1]
    margin = taps - 1
    activations = to_feature_rows(jnp.stack([tokens, cotangent]))
    features, cot_rows = activations[0], activations[1]
    projected_part = jnp.einsum(
        "td,idc->itc", features, in_weight, preferred_element_type=jnp.float32
    ).astype(jnp.bfloat16)
    gated_part = lax.dot_general(
        cot_rows, out_weight, (((1,), (1,)), ((), ())), preferred_element_type=jnp.float32
    ).astype(jnp.bfloat16)
    summed = lax.psum_scatter(
        jnp.concatenate([projected_part, gated_part[None]], 0),
        "seq",
        scatter_dimension=2,
        tiled=True,
    ).astype(jnp.float32)
    queries, key_part, value_part, grad_gated = summed[0], summed[1], summed[2], summed[3]
    channels = queries.shape[1]
    own_filters = lax.dynamic_slice_in_dim(
        filters, lax.axis_index("seq") * channels, channels, 0
    )
    signal = (key_part * value_part).astype(jnp.bfloat16)
    extended = jnp.pad(signal, ((margin, 0), (0, 0))).astype(jnp.float32)
    filtered = causal_filter(extended, own_filters)
    gated = (queries * filtered).astype(jnp.bfloat16)
    grad_queries = grad_gated * filtered
    grad_filtered = (grad_gated * queries).astype(jnp.bfloat16)
    grad_signal = reverse_filter(
        jnp.pad(grad_filtered, ((0, margin), (0, 0))).astype(jnp.float32), own_filters
    )
    own_grad_filters = filter_grad(extended, grad_filtered.astype(jnp.float32))
    grad_projected = jnp.stack(
        [grad_queries, grad_signal * value_part, grad_signal * key_part]
    ).astype(jnp.bfloat16)
    rows = lax.all_gather(
        jnp.concatenate([grad_projected, gated[None]], 0), "seq", axis=2, tiled=True
    )
    grad_filters = lax.all_gather(own_grad_filters, "seq", axis=0, tiled=True)
    mixed_part = jnp.dot(rows[3], out_weight, preferred_element_type=jnp.float32)
    grad_part = jnp.einsum(
        "itc,idc->td", rows[:3], in_weight, preferred_element_type=jnp.float32
    )
    outward = to_token_rows(jnp.stack([mixed_part, grad_part]).astype(jnp.bfloat16))
    grad_in_weight = jnp.einsum(
        "td,itc->idc", features, rows[:3], preferred_element_type=jnp.float32
    )
    grad_out_weight = lax.dot_general(
        rows[3], cot_rows, (((0,), (0,)), ((), ())), preferred_element_type=jnp.float32
    )
    return (outward[0], outward[1], grad_in_weight, grad_out_weight, grad_filters)


def params(**more):
    return pltpu.CompilerParams(vmem_limit_bytes=vmem_bytes, **more)


def cost(flops, moved):
    return pl.CostEstimate(flops=flops, bytes_accessed=moved, transcendentals=0)


def flip(value, axis, bit):
    return lax.ppermute(value, axis, [(i, i ^ bit) for i in range(lax.axis_size(axis))])


def crossed(index):
    return 2 * (index % 2) + index // 2


def trade_places(value, back):
    size = lax.axis_size("fsdp")
    pairs = [
        ((2 * line + pair) * size + own, (2 * own + pair) * size + crossed(line))
        for line in range(size)
        for pair in range(2)
        for own in range(size)
    ]
    return lax.ppermute(value, ("seq", "fsdp"), [p[::-1] for p in pairs] if back else pairs)


def flip_both(value):
    size = lax.axis_size("fsdp")
    pairs = [
        (seq * size + own, (seq ^ 1) * size + (own ^ 2))
        for seq in range(lax.axis_size("seq"))
        for own in range(size)
    ]
    return lax.ppermute(value, ("seq", "fsdp"), pairs)


def after(values, *others):
    return lax.optimization_barrier((values, others))[0]


def along_line(value, by, holds):
    length = lax.axis_size("seq") // 2
    pairs = [
        (2 * i + pair, 2 * (i + by) + pair)
        for i in range(length)
        for pair in range(2)
        if 0 <= i + by < length and holds(i)
    ]
    return lax.ppermute(value, "seq", pairs)


def added(one, other):
    return (one.astype(f32) + other.astype(f32)).astype(bf16)


def scatter_step(blocks, up, down, step):
    length = blocks.shape[0]
    up_in = along_line(up, 1, lambda i: i <= step - 1)
    down_in = along_line(down, -1, lambda i: i >= length - step)
    return up_in, down_in


def scatter_start(blocks):
    return scatter_step(blocks, blocks[blocks.shape[0] - 1], blocks[1], 1)


def scatter_next(blocks, up_in, down_in, step):
    up = added(blocks[blocks.shape[0] - step], up_in)
    down = added(blocks[step], down_in)
    return scatter_step(blocks, up, down, step)


def around(value, by):
    size = lax.axis_size("seq")
    return lax.ppermute(value, "seq", [(i, (i + 2 * by) % size) for i in range(size)])


def both_ways(before, behind):
    return [[behind[k], before[-1 - k]] for k in range(len(before))]


def next_block(block, by, step):
    length = lax.axis_size("seq") // 2
    if by > 0:
        return along_line(block, 1, lambda i: i >= step - 1)
    return along_line(block, -1, lambda i: i <= length - step)


def project_pair(place, first, second):
    near = first[0][0]
    tokens = 2 * near.shape[0] * near.shape[1] * near.shape[2]
    width = near.shape[3]
    half = width // 2
    rows = 2 * near.shape[2]
    count = half // lanes

    def body(place_ref, *refs):
        out = refs[-1]
        line = place_ref[0]
        is_near = pl.program_id(0) < 2
        for which in range(2):
            own, own_far, other, other_far, kept, given = refs[6 * which : 6 * which + 6]
            turned = (first, second)[which][3]
            dims = (((1,), (1,)), ((), ())) if turned else (((1,), (0,)), ((), ()))
            kept_value = kept[...].reshape(half, half)
            given_value = given[...].reshape(half, half)
            own_value = jnp.where(is_near, own[...], own_far[...]).reshape(rows, half)
            other_value = jnp.where(is_near, other[...], other_far[...]).reshape(rows, half)
            result = lax.dot_general(own_value, kept_value, dims, preferred_element_type=f32)
            result += lax.dot_general(other_value, given_value, dims, preferred_element_type=f32)
            result = result.astype(bf16)
            for j in range(count):
                out[lax.rem(j - line + count, count), which] = result[:, j * lanes : (j + 1) * lanes]

    operands, specs = [], []
    for (near, far), kept, (given, given_at), turned, index in (first, second):
        operands += [near, far, near, far, kept, given]
        for mine in (True, False):
            for is_far in (False, True):

                def index_of(g, place, mine=mine, is_far=is_far):
                    at = jnp.maximum(g - 2, 0) if is_far else jnp.minimum(g, 1)
                    return (at, 0, 0, place[1] if mine else 1 - place[1])

                specs.append(pl.BlockSpec((1, 2, rows // 2, half), index_of))
        if turned:
            specs.append(pl.BlockSpec((half, half), lambda g, place: (place[1], 0)))
        else:
            specs.append(pl.BlockSpec((1, half, half), lambda g, place, index=index: (index, 0, place[1])))
        specs.append(pl.BlockSpec((1, half, half), lambda g, place, at=given_at: (at, 0, 0)))
    return pl.pallas_call(
        body,
        out_shape=jax.ShapeDtypeStruct((count, 2, tokens, lanes), bf16),
        grid_spec=pltpu.PrefetchScalarGridSpec(
            num_scalar_prefetch=1,
            grid=(tokens // rows,),
            in_specs=specs,
            out_specs=pl.BlockSpec((count, 2, rows, lanes), lambda g, place: (0, 0, g, 0)),
        ),
        compiler_params=params(),
        cost_estimate=cost(4 * tokens * width * half, 8 * tokens * width),
        name="project_pair",
    )(place, *operands)


def block_rows(order, r, size):
    return pl.ds(pl.multiple_of(order[r] * size, size), size)


def window_filter(load, tap, tiles, reach):
    steps = range(reach // sublanes)
    sums = [jnp.zeros((sublanes, lanes), f32) for _ in range(tiles)]
    for shift in range(sublanes):
        held = {}
        for q in steps:
            weight = tap(shift, q)
            for i in range(tiles):
                if i - q not in held:
                    held[i - q] = load(shift, i - q)
                sums[i] = sums[i] + weight * held[i - q]
    return sums


def own_sum(blocks, received, which, rows):
    total = blocks[0, which, rows, :].astype(f32)
    for term in received:
        total += term[which, rows, :].astype(f32)
    return total


def forward_filter(order, blocks, received, spread_taps):
    tokens = blocks.shape[2]
    count = len(received)
    taps = spread_taps.shape[0] // sublanes
    n_blocks = order.shape[0]
    size = tokens // n_blocks
    tiles = 8

    def body(order_ref, blocks_ref, *refs):
        terms = refs[:count]
        taps_ref, kv_ref, signal_ref, filtered_ref, moved = refs[count:]
        for shift in range(sublanes):
            moved[shift, : taps + sublanes, :] = jnp.zeros((taps + sublanes, lanes), f32)

        def one_block(r, carry):
            rows = pl.ds(pl.multiple_of(r * size, size), size)
            place = block_rows(order_ref, r, size)
            key_part = own_sum(blocks_ref, terms, 0, rows).astype(bf16)
            value_part = own_sum(blocks_ref, terms, 1, rows).astype(bf16)
            kv_ref[0, place, :] = key_part
            kv_ref[1, place, :] = value_part
            product = (key_part.astype(f32) * value_part.astype(f32)).astype(bf16)
            signal_ref[place, :] = product
            moved[0, pl.ds(pl.multiple_of(taps + order_ref[r] * size, size), size), :] = product.astype(f32)
            return carry

        lax.fori_loop(0, n_blocks, one_block, 0)
        for shift in range(1, sublanes):
            moved[shift, taps : taps + tokens, :] = moved[0, taps - shift : taps - shift + tokens, :]

        def run(g, carry):
            start = pl.multiple_of(g * tiles * sublanes, tiles * sublanes)

            def load(shift, at):
                return moved[shift, pl.ds(start + taps + at * sublanes, sublanes), :]

            def tap(shift, q):
                index = q * sublanes + shift
                return taps_ref[index * sublanes : (index + 1) * sublanes, :]

            sums = window_filter(load, tap, tiles, taps)
            for i in range(tiles):
                filtered_ref[pl.ds(start + i * sublanes, sublanes), :] = sums[i]
            return carry

        lax.fori_loop(0, tokens // (tiles * sublanes), run, 0)

    whole = lambda shape: pl.BlockSpec(shape, lambda g, order: (0,) * len(shape))
    return pl.pallas_call(
        body,
        out_shape=(
            jax.ShapeDtypeStruct((2, tokens, lanes), bf16),
            jax.ShapeDtypeStruct((tokens, lanes), bf16),
            jax.ShapeDtypeStruct((tokens, lanes), f32),
        ),
        grid_spec=pltpu.PrefetchScalarGridSpec(
            num_scalar_prefetch=1,
            grid=(1,),
            in_specs=[
                whole((1, 2, tokens, lanes)),
                *[whole((2, tokens, lanes))] * count,
                whole(spread_taps.shape),
            ],
            out_specs=(
                whole((2, tokens, lanes)),
                whole((tokens, lanes)),
                whole((tokens, lanes)),
            ),
            scratch_shapes=[pltpu.VMEM((sublanes, taps + tokens, lanes), f32)],
        ),
        compiler_params=params(),
        cost_estimate=cost(400 * tokens * lanes * taps, 12 * tokens * lanes),
        name="forward_filter",
    )(order, blocks, *received, spread_taps)


def gate_rows(order, blocks, received, filtered):
    tokens = blocks.shape[2]
    count = len(received)
    n_blocks = order.shape[0]
    size = tokens // n_blocks

    def body(order_ref, blocks_ref, *refs):
        terms = refs[:count]
        filtered_ref, out_ref, grad_ref = refs[count:]

        def one_block(r, carry):
            rows = pl.ds(pl.multiple_of(r * size, size), size)
            place = block_rows(order_ref, r, size)
            queries = own_sum(blocks_ref, terms, 0, rows).astype(bf16).astype(f32)
            grad_gated = own_sum(blocks_ref, terms, 1, rows)
            kept = filtered_ref[place, :]
            out_ref[rows, :] = (queries * kept).astype(bf16)
            later = pl.ds(pl.multiple_of(tokens + r * size, size), size)
            out_ref[later, :] = (grad_gated * kept).astype(bf16)
            grad_ref[place, :] = (grad_gated * queries).astype(bf16)
            return carry

        lax.fori_loop(0, n_blocks, one_block, 0)

    whole = lambda shape: pl.BlockSpec(shape, lambda g, order: (0,) * len(shape))
    return pl.pallas_call(
        body,
        out_shape=(
            jax.ShapeDtypeStruct((2 * tokens, lanes), bf16),
            jax.ShapeDtypeStruct((tokens, lanes), bf16),
        ),
        grid_spec=pltpu.PrefetchScalarGridSpec(
            num_scalar_prefetch=1,
            grid=(1,),
            in_specs=[
                whole((1, 2, tokens, lanes)),
                *[whole((2, tokens, lanes))] * count,
                whole((tokens, lanes)),
            ],
            out_specs=(whole((2 * tokens, lanes)), whole((tokens, lanes))),
        ),
        compiler_params=params(),
        cost_estimate=cost(20 * tokens * lanes, 20 * tokens * lanes),
        name="gate_rows",
    )(order, blocks, *received, filtered)


def backward_filter(order, grad_filtered, key_values, signal, spread_taps):
    tokens = grad_filtered.shape[0]
    taps = spread_taps.shape[0] // sublanes
    n_blocks = order.shape[0]
    size = tokens // n_blocks
    tiles = 8
    steps = taps // sublanes

    def body(order_ref, grad_ref, kv_ref, signal_ref, taps_ref, out_ref, moved, signal_grad, behind, gradient):
        for shift in range(sublanes):
            moved[shift, tokens - sublanes :, :] = jnp.zeros((taps + sublanes, lanes), f32)
            behind[shift, : taps + sublanes, :] = jnp.zeros((taps + sublanes, lanes), f32)
        moved[0, :tokens, :] = grad_ref[...].astype(f32)
        behind[0, taps:, :] = signal_ref[...].astype(f32)
        gradient[...] = grad_ref[...].astype(f32)
        for shift in range(1, sublanes):
            moved[shift, :tokens, :] = moved[0, shift : shift + tokens, :]
            behind[shift, taps:, :] = behind[0, taps - shift : taps - shift + tokens, :]

        def run(g, carry):
            start = pl.multiple_of(g * tiles * sublanes, tiles * sublanes)

            def load(shift, at):
                return moved[shift, pl.ds(start + (tiles - 1 - at) * sublanes, sublanes), :]

            def tap(shift, q):
                index = q * sublanes + shift
                return taps_ref[index * sublanes : (index + 1) * sublanes, :]

            sums = window_filter(load, tap, tiles, taps)
            for i in range(tiles):
                signal_grad[pl.ds(start + (tiles - 1 - i) * sublanes, sublanes), :] = sums[i]
            return carry

        lax.fori_loop(0, tokens // (tiles * sublanes), run, 0)

        def one_block(r, carry):
            start = pl.multiple_of(r * size, size)
            place = block_rows(order_ref, r, size)
            value = signal_grad[place, :]
            out_ref[pl.ds(start, size), :] = (value * kv_ref[1, place, :].astype(f32)).astype(bf16)
            out_ref[pl.ds(tokens + start, size), :] = (value * kv_ref[0, place, :].astype(f32)).astype(bf16)
            return carry

        lax.fori_loop(0, n_blocks, one_block, 0)

        for shift in range(sublanes):

            def sum_run(g, sums):
                start = pl.multiple_of(g * tiles * sublanes, tiles * sublanes)
                sums = list(sums)
                held = {}
                for i in range(tiles):
                    here = gradient[pl.ds(start + i * sublanes, sublanes), :]
                    for q in range(steps):
                        if i - q not in held:
                            held[i - q] = behind[shift, pl.ds(start + taps + (i - q) * sublanes, sublanes), :]
                        sums[q] = sums[q] + here * held[i - q]
                return tuple(sums)

            zero = tuple(jnp.zeros((sublanes, lanes), f32) for _ in range(steps))
            sums = lax.fori_loop(0, tokens // (tiles * sublanes), sum_run, zero)
            for q in range(steps):
                index = q * sublanes + shift
                signal_grad[index : index + 1, :] = jnp.sum(sums[q], axis=0, keepdims=True)
        out_ref[2 * tokens :, :] = signal_grad[:taps, :].astype(bf16)

    whole = lambda shape: pl.BlockSpec(shape, lambda g, order: (0,) * len(shape))
    return pl.pallas_call(
        body,
        out_shape=jax.ShapeDtypeStruct((2 * tokens + taps, lanes), bf16),
        grid_spec=pltpu.PrefetchScalarGridSpec(
            num_scalar_prefetch=1,
            grid=(1,),
            in_specs=[
                whole((tokens, lanes)),
                whole((2, tokens, lanes)),
                whole((tokens, lanes)),
                whole(spread_taps.shape),
            ],
            out_specs=whole((2 * tokens + taps, lanes)),
            scratch_shapes=[
                pltpu.VMEM((sublanes, tokens + taps, lanes), f32),
                pltpu.VMEM((tokens, lanes), f32),
                pltpu.VMEM((sublanes, tokens + taps, lanes), f32),
                pltpu.VMEM((tokens, lanes), f32),
            ],
        ),
        compiler_params=params(),
        cost_estimate=cost(800 * tokens * lanes * taps, 12 * tokens * lanes),
        name="backward_filter",
    )(order, grad_filtered, key_values, signal, spread_taps)


def merge_blocks(place, block, others, tokens):
    matrices = block.shape[0] // tokens
    length = len(others) + 1
    sizes = [len(other) for other in others]
    rows = 256
    steps = tokens // rows

    def body(place_ref, *refs):
        out = refs[-1]
        own, rest = refs[0], list(refs[1:-1])
        line = place_ref[0]
        for offset in range(length):
            if offset == 0:
                value = own[...]
            else:
                value = rest.pop(0)[...]
                for _ in range(sizes[offset - 1] - 1):
                    value += rest.pop(0)[...]
            at = pl.multiple_of(lax.rem(line + offset, length) * lanes, lanes)
            out[0, :, pl.ds(at, lanes)] = value

    spec = pl.BlockSpec((rows, lanes), lambda which, g, place: (which * steps + g, 0))
    return pl.pallas_call(
        body,
        out_shape=jax.ShapeDtypeStruct((matrices, tokens, length * lanes), bf16),
        grid_spec=pltpu.PrefetchScalarGridSpec(
            num_scalar_prefetch=1,
            grid=(matrices, steps),
            in_specs=[spec] * (1 + sum(sizes)),
            out_specs=pl.BlockSpec((1, rows, length * lanes), lambda which, g, place: (which, g, 0)),
        ),
        compiler_params=params(),
        cost_estimate=cost(tokens * lanes * 8, 2 * 2 * tokens * lanes * 11),
        name="merge_blocks",
    )(place, block, *[term for other in others for term in other])


def merge_taps(place, block, others, taps):
    length = len(others) + 1
    sizes = [len(other) for other in others]
    last = block.shape[0] // taps - 1

    def body(place_ref, *refs):
        out = refs[-1]
        own, rest = refs[0], list(refs[1:-1])
        line = place_ref[0]
        for offset in range(length):
            if offset == 0:
                value = own[...]
            else:
                value = rest.pop(0)[...]
                for _ in range(sizes[offset - 1] - 1):
                    value += rest.pop(0)[...]
            at = pl.multiple_of(lax.rem(line + offset, length) * lanes, lanes)
            out[pl.ds(at, lanes), :] = jnp.transpose(value.astype(f32)).astype(bf16)

    return pl.pallas_call(
        body,
        out_shape=jax.ShapeDtypeStruct((length * lanes, taps), bf16),
        grid_spec=pltpu.PrefetchScalarGridSpec(
            num_scalar_prefetch=1,
            grid=(1,),
            in_specs=[pl.BlockSpec((taps, lanes), lambda g, place: (last, 0))] * (1 + sum(sizes)),
            out_specs=pl.BlockSpec((length * lanes, taps), lambda g, place: (0, 0)),
        ),
        compiler_params=params(),
        cost_estimate=cost(taps * lanes * 8, 2 * taps * lanes * 11),
        name="merge_taps",
    )(place, block, *[term for other in others for term in other])


def project_back(place, merged, in_weight, given, indices, part):
    tokens, half = merged[0][0].shape[1:]
    rows = 256
    n = len(merged)
    steps = tokens // rows // 2

    def body(place_ref, *refs):
        out = refs[-1]
        dims = (((1,), (1,)), ((), ()))
        own = jnp.zeros((rows, half), f32)
        other = jnp.zeros((rows, half), f32)
        for k in range(n):
            value, kept, sent = refs[3 * k], refs[3 * k + 1], refs[3 * k + 2]
            value = value[...].reshape(rows, half)
            own += lax.dot_general(value, kept[...].reshape(half, half), dims, preferred_element_type=f32)
            other += lax.dot_general(value, sent[...].reshape(half, half), dims, preferred_element_type=f32)
        at = place_ref[1]
        out[:, pl.ds(pl.multiple_of(at * half, half), half)] = own.astype(bf16)
        out[:, pl.ds(pl.multiple_of((1 - at) * half, half), half)] = other.astype(bf16)

    operands, specs = [], []
    for (value, which), (sent, at), index in zip(merged, given, indices):
        operands += [value, in_weight, sent]
        specs += [
            pl.BlockSpec((1, rows, half), lambda g, place, which=which: (which, part * steps + g, 0)),
            pl.BlockSpec((1, half, half), lambda g, place, index=index: (index, 0, place[1])),
            pl.BlockSpec((1, half, half), lambda g, place, at=at: (at, 0, 0)),
        ]
    return pl.pallas_call(
        body,
        out_shape=jax.ShapeDtypeStruct((tokens // 2, 2 * half), bf16),
        grid_spec=pltpu.PrefetchScalarGridSpec(
            num_scalar_prefetch=1,
            grid=(steps,),
            in_specs=specs,
            out_specs=pl.BlockSpec((rows, 2 * half), lambda g, place: (g, 0)),
        ),
        compiler_params=params(),
        cost_estimate=cost(2 * n * tokens * half * half, 4 * tokens * half),
        name="project_back",
    )(place, *operands)


def project_out(place, merged, out_weight, given, at):
    tokens, half = merged.shape[1:]
    rows = 256

    def body(place_ref, value_ref, kept, sent, out):
        value = value_ref[...].reshape(rows, half)
        pair = place_ref[1]
        own = jnp.dot(value, kept[...], preferred_element_type=f32)
        other = jnp.dot(value, sent[...].reshape(half, half), preferred_element_type=f32)
        out[:, pl.ds(pl.multiple_of(pair * half, half), half)] = own.astype(bf16)
        out[:, pl.ds(pl.multiple_of((1 - pair) * half, half), half)] = other.astype(bf16)

    return pl.pallas_call(
        body,
        out_shape=jax.ShapeDtypeStruct((tokens, 2 * half), bf16),
        grid_spec=pltpu.PrefetchScalarGridSpec(
            num_scalar_prefetch=1,
            grid=(tokens // rows,),
            in_specs=[
                pl.BlockSpec((1, rows, half), lambda g, place: (0, g, 0)),
                pl.BlockSpec((half, half), lambda g, place: (place[1], 0)),
                pl.BlockSpec((1, half, half), lambda g, place: (at, 0, 0)),
            ],
            out_specs=pl.BlockSpec((rows, 2 * half), lambda g, place: (g, 0)),
        ),
        compiler_params=params(),
        cost_estimate=cost(4 * tokens * half * half, 8 * tokens * half),
        name="project_out",
    )(place, merged, out_weight, given)


def in_gradient(place, near, far, merged, which, index, total, running):
    tokens, half = merged.shape[1:]
    rows = 256
    steps = half // rows
    block = near.shape[:3] + (rows,)

    def body(place_ref, own, own_far, other, other_far, value_ref, *refs):
        kept, sent = refs[-2:]
        value = value_ref[...].reshape(tokens, half)
        dims = (((0,), (0,)), ((), ()))

        def product(one, two):
            rows_of = jnp.concatenate([one[...].reshape(tokens // 2, rows), two[...].reshape(tokens // 2, rows)], 0)
            return lax.dot_general(rows_of, value, dims, preferred_element_type=f32)

        kept[...] = product(own, own_far)[None]
        sent[...] = product(other, other_far).astype(bf16)

    more = [] if running is None else [running]
    own_spec = pl.BlockSpec(block, lambda g, place: (0, 0, 0, place[1] * steps + g))
    other_spec = pl.BlockSpec(block, lambda g, place: (0, 0, 0, (1 - place[1]) * steps + g))
    return pl.pallas_call(
        body,
        out_shape=(
            jax.ShapeDtypeStruct((total, half, 2 * half), f32),
            jax.ShapeDtypeStruct((half, half), bf16),
        ),
        grid_spec=pltpu.PrefetchScalarGridSpec(
            num_scalar_prefetch=1,
            grid=(steps,),
            in_specs=[own_spec, own_spec, other_spec, other_spec]
            + [pl.BlockSpec((1, tokens, half), lambda g, place: (which, 0, 0))]
            + [pl.BlockSpec(memory_space=pl.ANY)] * len(more),
            out_specs=(
                pl.BlockSpec((1, rows, half), lambda g, place: (index, g, place[1])),
                pl.BlockSpec((rows, half), lambda g, place: (g, 0)),
            ),
        ),
        input_output_aliases={6: 0} if more else {},
        compiler_params=params(),
        cost_estimate=cost(4 * tokens * half * half, 8 * tokens * half),
        name="in_gradient",
    )(place, near, far, near, far, merged, *more)


def out_gradient(place, merged, near, far):
    tokens, half = merged.shape[1:]
    rows = 256
    steps = half // rows
    block = near.shape[:3] + (half,)

    def body(place_ref, value_ref, own, own_far, other, other_far, kept, sent):
        value = value_ref[...].reshape(tokens, rows)
        dims = (((0,), (0,)), ((), ()))

        def in_order(one, two):
            return jnp.concatenate([ref[...].reshape(tokens // 2, half) for ref in (one, two)], 0)

        kept[...] = lax.dot_general(value, in_order(own, own_far), dims, preferred_element_type=f32)
        sent[...] = lax.dot_general(
            value, in_order(other, other_far), dims, preferred_element_type=f32
        ).astype(bf16)

    own_spec = pl.BlockSpec(block, lambda g, place: (0, 0, 0, place[1]))
    other_spec = pl.BlockSpec(block, lambda g, place: (0, 0, 0, 1 - place[1]))
    return pl.pallas_call(
        body,
        out_shape=(
            jax.ShapeDtypeStruct((2 * half, half), f32),
            jax.ShapeDtypeStruct((half, half), bf16),
        ),
        grid_spec=pltpu.PrefetchScalarGridSpec(
            num_scalar_prefetch=1,
            grid=(steps,),
            in_specs=[
                pl.BlockSpec((1, tokens, rows), lambda g, place: (0, 0, g)),
                own_spec,
                own_spec,
                other_spec,
                other_spec,
            ],
            out_specs=(
                pl.BlockSpec((rows, half), lambda g, place: (place[1] * steps + g, 0)),
                pl.BlockSpec((rows, half), lambda g, place: (g, 0)),
            ),
        ),
        compiler_params=params(),
        cost_estimate=cost(4 * tokens * half * half, 8 * tokens * half),
        name="out_gradient",
    )(place, merged, near, far, near, far)


def take_in_half(place, running, piece, index):
    half = piece.shape[0]

    def body(place_ref, piece_ref, running_ref, out):
        out[...] = piece_ref[...].astype(f32)[None]

    return pl.pallas_call(
        body,
        out_shape=jax.ShapeDtypeStruct(running.shape, f32),
        grid_spec=pltpu.PrefetchScalarGridSpec(
            num_scalar_prefetch=1,
            grid=(1,),
            in_specs=[
                pl.BlockSpec((half, half), lambda g, place: (0, 0)),
                pl.BlockSpec(memory_space=pl.ANY),
            ],
            out_specs=pl.BlockSpec((1, half, half), lambda g, place: (index, 0, 1 - place[1])),
        ),
        input_output_aliases={2: 0},
        compiler_params=params(),
        cost_estimate=cost(half * half, 6 * half * half),
        name="take_in_half",
    )(place, piece, running)


def take_out_half(place, running, piece):
    half = piece.shape[0]

    def body(place_ref, piece_ref, running_ref, out):
        out[...] = piece_ref[...].astype(f32)

    return pl.pallas_call(
        body,
        out_shape=jax.ShapeDtypeStruct(running.shape, f32),
        grid_spec=pltpu.PrefetchScalarGridSpec(
            num_scalar_prefetch=1,
            grid=(1,),
            in_specs=[
                pl.BlockSpec((half, half), lambda g, place: (0, 0)),
                pl.BlockSpec(memory_space=pl.ANY),
            ],
            out_specs=pl.BlockSpec((half, half), lambda g, place: (1 - place[1], 0)),
        ),
        input_output_aliases={2: 0},
        compiler_params=params(),
        cost_estimate=cost(half * half, 6 * half * half),
        name="take_out_half",
    )(place, piece, running)


def on_paired_mesh(tokens, in_weight, out_weight, filters, cotangent):
    taps = filters.shape[1]
    seq_at, fsdp_at = lax.axis_index("seq"), lax.axis_index("fsdp")
    line, pair = seq_at // 2, seq_at % 2
    place = jnp.stack([line, pair]).astype(jnp.int32)
    half_in, half_out = in_weight.shape[2] // 2, out_weight.shape[0] // 2
    width = tokens.shape[1]
    count = tokens.shape[0] * lax.axis_size("seq")
    relative = jnp.arange(8, dtype=jnp.int32)
    order = (
        2 * crossed(fsdp_at ^ (2 * (relative % 2) + relative // 4)) + (pair ^ (relative // 2 % 2))
    ).astype(jnp.int32)

    def sent_in(weight, i):
        return lax.dynamic_slice_in_dim(weight[i], (1 - pair) * half_in, half_in, 1)

    def gathered(own):
        return [own, flip(own, "fsdp", 2), flip(own, "seq", 1), flip_both(own)]

    given_kv = flip(jnp.stack([sent_in(in_weight, 1), sent_in(in_weight, 2)]), "seq", 1)
    x_own = trade_places(tokens, False)
    late_in, late_out, late_cot = after((in_weight, out_weight, cotangent), x_own)
    g_own = trade_places(late_cot, False)
    x_near = jnp.stack(gathered(x_own))
    sent_qo = jnp.stack(
        [sent_in(late_in, 0), lax.dynamic_slice_in_dim(late_out, (1 - pair) * half_out, half_out, 0)]
    )
    x_near, given_kv, sent_qo, g_own = lax.optimization_barrier((x_near, given_kv, sent_qo, g_own))
    x_near = x_near.reshape(2, 2, -1, width)
    x_far = flip(x_near, "fsdp", 1)
    given_qo = flip(sent_qo, "seq", 1)
    own_filters = lax.dynamic_slice_in_dim(filters, pair * half_in + line * lanes, lanes, 0)
    spread_taps = jnp.repeat(jnp.transpose(own_filters), sublanes, axis=0)

    kv_blocks = project_pair(
        place,
        ((x_near, x_far), in_weight, (given_kv, 0), False, 1),
        ((x_near, x_far), in_weight, (given_kv, 1), False, 2),
    )
    kv_up, kv_down = scatter_start(kv_blocks)
    g_near = jnp.stack(gathered(g_own)).reshape(2, 2, -1, width)
    kv_up, kv_down, given_qo, g_near = lax.optimization_barrier((kv_up, kv_down, given_qo, g_near))
    kv_up, kv_down = scatter_next(kv_blocks, kv_up, kv_down, 2)
    g_far = flip(g_near, "fsdp", 1)
    qg_blocks = project_pair(
        place,
        ((x_near, x_far), in_weight, (given_qo, 0), False, 0),
        ((g_near, g_far), out_weight, (given_qo, 1), True, 0),
    )
    kv_up, kv_down = scatter_next(kv_blocks, kv_up, kv_down, 3)
    qg_up, qg_down = scatter_start(qg_blocks)
    for step in (2, 3):
        qg_up, qg_down = scatter_next(qg_blocks, qg_up, qg_down, step)
    key_values, signal, filtered = forward_filter(order, kv_blocks, [kv_up, kv_down], spread_taps)
    gated_rows, grad_filtered = gate_rows(order, qg_blocks, [qg_up, qg_down], filtered)

    gated_others = [[around(gated_rows, -k)] for k in range(1, 4)]
    kv_grads = backward_filter(order, grad_filtered, key_values, signal, spread_taps)
    kv_before = [next_block(kv_grads, 1, 1)]
    kv_behind = [next_block(kv_grads, -1, 1)]
    kv_before.append(next_block(kv_before[0], 1, 2))
    kv_behind.append(next_block(kv_behind[0], -1, 2))

    total_in = in_weight.shape[0]
    first = merge_blocks(place, gated_rows, gated_others, count)
    out_kept, out_sent = out_gradient(place, first, g_near, g_far)
    out_given = flip(out_sent, "seq", 1)
    in_kept, q_sent = in_gradient(place, x_near, x_far, first, 1, 0, total_in, None)
    q_given = flip(q_sent, "seq", 1)
    mixed_part = project_out(place, after(first, out_sent), out_weight, given_qo, 1)
    last_up, last_down, out_given = lax.optimization_barrier(
        after((kv_before[1], kv_behind[1], out_given), q_sent, mixed_part)
    )
    kv_before.append(next_block(last_up, 1, 3))
    kv_behind.append(next_block(last_down, -1, 3))

    mixed_part = mixed_part.reshape(2, 2, 2, count // 8, width)
    mixed_part = added(mixed_part[0], flip(mixed_part[1], "fsdp", 1))
    kv_behind[2], kv_before[2], mixed_part, q_given = lax.optimization_barrier(
        (kv_behind[2], kv_before[2], mixed_part, q_given)
    )
    second = merge_blocks(place, kv_grads, both_ways(kv_before, kv_behind), count)
    in_kept, k_sent = in_gradient(place, x_near, x_far, second, 0, 1, total_in, in_kept)
    k_given = flip(k_sent, "seq", 1)

    def back(part, value):
        return project_back(
            place,
            [(first, 1), (value, 0), (value, 1)],
            in_weight,
            [(given_qo, 0), (given_kv, 0), (given_kv, 1)],
            [0, 1, 2],
            part,
        )

    far_part = back(1, after(second, k_sent))
    near_part = back(0, after(second, far_part))
    parts = added(near_part, flip(far_part, "fsdp", 1)).reshape(4, count // 8, width)
    mixed_part = added(mixed_part[:, 0], flip(mixed_part[:, 1], "fsdp", 2))
    mixed_part = added(mixed_part[0], flip(mixed_part[1], "seq", 1))
    mixed_out = trade_places(mixed_part, True)
    total = parts[0].astype(f32) + flip(parts[1], "fsdp", 2).astype(f32)
    total += flip(parts[2], "seq", 1).astype(f32) + flip_both(parts[3]).astype(f32)
    in_kept, v_sent = in_gradient(place, x_near, x_far, after(second, parts), 1, 2, total_in, in_kept)
    half_taps = merge_taps(place, kv_grads, both_ways(kv_before, kv_behind), taps)
    total, k_given, mixed_out = lax.optimization_barrier((total, k_given, mixed_out))
    v_given = flip(v_sent, "seq", 1)
    given_taps = flip(after(half_taps, v_sent), "seq", 1)
    grad_tokens = trade_places(total.astype(bf16), True)
    grad_filters = jnp.where(
        pair == 0,
        jnp.concatenate([half_taps, given_taps], 0),
        jnp.concatenate([given_taps, half_taps], 0),
    ).astype(f32)
    grad_out_weight = take_out_half(place, out_kept, out_given)
    for index, given in enumerate((q_given, k_given, v_given)):
        in_kept = take_in_half(place, in_kept, given, index)
    return (mixed_out, grad_tokens, in_kept, grad_out_weight, grad_filters)


def solution(mesh):
    placed = (
        P("seq", "fsdp"),
        P(None, "seq", "fsdp"),
        P("fsdp", "seq"),
        P("fsdp", None),
        P("seq", "fsdp"),
    )
    paired = (mesh.shape["seq"], mesh.shape["fsdp"]) == (8, 4)
    return jax.shard_map(
        on_paired_mesh if paired else on_any_mesh,
        mesh=mesh,
        in_specs=placed,
        out_specs=(
            P("seq", "fsdp"),
            P("seq", "fsdp"),
            P(None, "seq", "fsdp"),
            P("fsdp", "seq"),
            P("fsdp", None),
        ),
        check_vma=False,
    )
```

```python
import jax
import jax.numpy as jnp
from jax import lax
from jax.experimental import pallas as pl
from jax.experimental.pallas import tpu as pltpu
from jax.sharding import PartitionSpec as P

highest = lax.Precision.HIGHEST
bf16 = jnp.bfloat16
f32 = jnp.float32
lanes = 128
sublanes = 8
vmem_bytes = 24 * 1024 * 1024


def causal_filter(extended, filters):
    kernel = jnp.flip(jnp.transpose(filters), 0)[:, None, :]
    result = lax.conv_general_dilated(
        extended[None],
        kernel,
        (1,),
        "VALID",
        dimension_numbers=("NWC", "WIO", "NWC"),
        feature_group_count=filters.shape[0],
        precision=highest,
    )
    return result[0]


def reverse_filter(extended, filters):
    kernel = jnp.transpose(filters)[:, None, :]
    result = lax.conv_general_dilated(
        extended[None],
        kernel,
        (1,),
        "VALID",
        dimension_numbers=("NWC", "WIO", "NWC"),
        feature_group_count=filters.shape[0],
        precision=highest,
    )
    return result[0]


def filter_grad(extended, gradient):
    result = lax.conv_general_dilated(
        extended[None],
        gradient[:, None, :],
        (1,),
        "VALID",
        dimension_numbers=("NWC", "WIO", "NWC"),
        feature_group_count=gradient.shape[1],
        precision=highest,
    )
    return jnp.transpose(jnp.flip(result[0], 0))


def to_feature_rows(value):
    wide = lax.all_gather(value, "fsdp", axis=value.ndim - 1, tiled=True)
    return lax.all_to_all(wide, "seq", split_axis=wide.ndim - 1, concat_axis=wide.ndim - 2, tiled=True)


def to_token_rows(partial):
    swapped = lax.all_to_all(
        partial, "seq", split_axis=partial.ndim - 2, concat_axis=partial.ndim - 1, tiled=True
    )
    return lax.psum_scatter(swapped, "fsdp", scatter_dimension=partial.ndim - 1, tiled=True)


def on_any_mesh(tokens, in_weight, out_weight, filters, cotangent):
    taps = filters.shape[1]
    margin = taps - 1
    activations = to_feature_rows(jnp.stack([tokens, cotangent]))
    features, cot_rows = activations[0], activations[1]
    projected_part = jnp.einsum(
        "td,idc->itc", features, in_weight, preferred_element_type=jnp.float32
    ).astype(jnp.bfloat16)
    gated_part = lax.dot_general(
        cot_rows, out_weight, (((1,), (1,)), ((), ())), preferred_element_type=jnp.float32
    ).astype(jnp.bfloat16)
    summed = lax.psum_scatter(
        jnp.concatenate([projected_part, gated_part[None]], 0),
        "seq",
        scatter_dimension=2,
        tiled=True,
    ).astype(jnp.float32)
    queries, key_part, value_part, grad_gated = summed[0], summed[1], summed[2], summed[3]
    channels = queries.shape[1]
    own_filters = lax.dynamic_slice_in_dim(
        filters, lax.axis_index("seq") * channels, channels, 0
    )
    signal = (key_part * value_part).astype(jnp.bfloat16)
    extended = jnp.pad(signal, ((margin, 0), (0, 0))).astype(jnp.float32)
    filtered = causal_filter(extended, own_filters)
    gated = (queries * filtered).astype(jnp.bfloat16)
    grad_queries = grad_gated * filtered
    grad_filtered = (grad_gated * queries).astype(jnp.bfloat16)
    grad_signal = reverse_filter(
        jnp.pad(grad_filtered, ((0, margin), (0, 0))).astype(jnp.float32), own_filters
    )
    own_grad_filters = filter_grad(extended, grad_filtered.astype(jnp.float32))
    grad_projected = jnp.stack(
        [grad_queries, grad_signal * value_part, grad_signal * key_part]
    ).astype(jnp.bfloat16)
    rows = lax.all_gather(
        jnp.concatenate([grad_projected, gated[None]], 0), "seq", axis=2, tiled=True
    )
    grad_filters = lax.all_gather(own_grad_filters, "seq", axis=0, tiled=True)
    mixed_part = jnp.dot(rows[3], out_weight, preferred_element_type=jnp.float32)
    grad_part = jnp.einsum(
        "itc,idc->td", rows[:3], in_weight, preferred_element_type=jnp.float32
    )
    outward = to_token_rows(jnp.stack([mixed_part, grad_part]).astype(jnp.bfloat16))
    grad_in_weight = jnp.einsum(
        "td,itc->idc", features, rows[:3], preferred_element_type=jnp.float32
    )
    grad_out_weight = lax.dot_general(
        rows[3], cot_rows, (((0,), (0,)), ((), ())), preferred_element_type=jnp.float32
    )
    return (outward[0], outward[1], grad_in_weight, grad_out_weight, grad_filters)


def params(**more):
    return pltpu.CompilerParams(vmem_limit_bytes=vmem_bytes, **more)


def cost(flops, moved):
    return pl.CostEstimate(flops=flops, bytes_accessed=moved, transcendentals=0)


def flip(value, axis, bit):
    return lax.ppermute(value, axis, [(i, i ^ bit) for i in range(lax.axis_size(axis))])


def crossed(index):
    return 2 * (index % 2) + index // 2


def trade_places(value, back):
    size = lax.axis_size("fsdp")
    pairs = [
        ((2 * line + pair) * size + own, (2 * own + pair) * size + crossed(line))
        for line in range(size)
        for pair in range(2)
        for own in range(size)
    ]
    return lax.ppermute(value, ("seq", "fsdp"), [p[::-1] for p in pairs] if back else pairs)


def flip_both(value):
    size = lax.axis_size("fsdp")
    pairs = [
        (seq * size + own, (seq ^ 1) * size + (own ^ 2))
        for seq in range(lax.axis_size("seq"))
        for own in range(size)
    ]
    return lax.ppermute(value, ("seq", "fsdp"), pairs)


def after(values, *others):
    return lax.optimization_barrier((values, others))[0]


def along_line(value, by, holds):
    length = lax.axis_size("seq") // 2
    pairs = [
        (2 * i + pair, 2 * (i + by) + pair)
        for i in range(length)
        for pair in range(2)
        if 0 <= i + by < length and holds(i)
    ]
    return lax.ppermute(value, "seq", pairs)


def added(one, other):
    return (one.astype(f32) + other.astype(f32)).astype(bf16)


def scatter_step(blocks, up, down, step):
    length = blocks.shape[0]
    up_in = along_line(up, 1, lambda i: i <= step - 1)
    down_in = along_line(down, -1, lambda i: i >= length - step)
    return up_in, down_in


def scatter_start(blocks):
    return scatter_step(blocks, blocks[blocks.shape[0] - 1], blocks[1], 1)


def scatter_next(blocks, up_in, down_in, step):
    up = added(blocks[blocks.shape[0] - step], up_in)
    down = added(blocks[step], down_in)
    return scatter_step(blocks, up, down, step)


def around(value, by):
    size = lax.axis_size("seq")
    return lax.ppermute(value, "seq", [(i, (i + 2 * by) % size) for i in range(size)])


def both_ways(before, behind):
    return [[behind[k], before[-1 - k]] for k in range(len(before))]


def next_block(block, by, step):
    length = lax.axis_size("seq") // 2
    if by > 0:
        return along_line(block, 1, lambda i: i >= step - 1)
    return along_line(block, -1, lambda i: i <= length - step)


def project_pair(place, first, second):
    near = first[0][0]
    tokens = 2 * near.shape[0] * near.shape[1] * near.shape[2]
    width = near.shape[3]
    half = width // 2
    rows = 2 * near.shape[2]
    count = half // lanes

    def body(place_ref, *refs):
        out = refs[-1]
        line = place_ref[0]
        is_near = pl.program_id(0) < 2
        for which in range(2):
            own, own_far, other, other_far, kept, given = refs[6 * which : 6 * which + 6]
            turned = (first, second)[which][3]
            dims = (((1,), (1,)), ((), ())) if turned else (((1,), (0,)), ((), ()))
            kept_value = kept[...].reshape(half, half)
            given_value = given[...].reshape(half, half)
            own_value = jnp.where(is_near, own[...], own_far[...]).reshape(rows, half)
            other_value = jnp.where(is_near, other[...], other_far[...]).reshape(rows, half)
            result = lax.dot_general(own_value, kept_value, dims, preferred_element_type=f32)
            result += lax.dot_general(other_value, given_value, dims, preferred_element_type=f32)
            result = result.astype(bf16)
            for j in range(count):
                out[lax.rem(j - line + count, count), which] = result[:, j * lanes : (j + 1) * lanes]

    operands, specs = [], []
    for (near, far), kept, (given, given_at), turned, index in (first, second):
        operands += [near, far, near, far, kept, given]
        for mine in (True, False):
            for is_far in (False, True):

                def index_of(g, place, mine=mine, is_far=is_far):
                    at = jnp.maximum(g - 2, 0) if is_far else jnp.minimum(g, 1)
                    return (at, 0, 0, place[1] if mine else 1 - place[1])

                specs.append(pl.BlockSpec((1, 2, rows // 2, half), index_of))
        if turned:
            specs.append(pl.BlockSpec((half, half), lambda g, place: (place[1], 0)))
        else:
            specs.append(pl.BlockSpec((1, half, half), lambda g, place, index=index: (index, 0, place[1])))
        specs.append(pl.BlockSpec((1, half, half), lambda g, place, at=given_at: (at, 0, 0)))
    return pl.pallas_call(
        body,
        out_shape=jax.ShapeDtypeStruct((count, 2, tokens, lanes), bf16),
        grid_spec=pltpu.PrefetchScalarGridSpec(
            num_scalar_prefetch=1,
            grid=(tokens // rows,),
            in_specs=specs,
            out_specs=pl.BlockSpec((count, 2, rows, lanes), lambda g, place: (0, 0, g, 0)),
        ),
        compiler_params=params(),
        cost_estimate=cost(4 * tokens * width * half, 8 * tokens * width),
        name="project_pair",
    )(place, *operands)


def block_rows(order, r, size):
    return pl.ds(pl.multiple_of(order[r] * size, size), size)


def window_filter(load, tap, tiles, reach):
    steps = range(reach // sublanes)
    sums = [jnp.zeros((sublanes, lanes), f32) for _ in range(tiles)]
    for shift in range(sublanes):
        held = {}
        for q in steps:
            weight = tap(shift, q)
            for i in range(tiles):
                if i - q not in held:
                    held[i - q] = load(shift, i - q)
                sums[i] = sums[i] + weight * held[i - q]
    return sums


def own_sum(blocks, received, which, rows):
    total = blocks[0, which, rows, :].astype(f32)
    for term in received:
        total += term[which, rows, :].astype(f32)
    return total


def forward_filter(order, blocks, received, spread_taps):
    tokens = blocks.shape[2]
    count = len(received)
    taps = spread_taps.shape[0] // sublanes
    n_blocks = order.shape[0]
    size = tokens // n_blocks
    tiles = 8

    def body(order_ref, blocks_ref, *refs):
        terms = refs[:count]
        taps_ref, kv_ref, signal_ref, filtered_ref, moved = refs[count:]
        for shift in range(sublanes):
            moved[shift, : taps + sublanes, :] = jnp.zeros((taps + sublanes, lanes), f32)

        def one_block(r, carry):
            rows = pl.ds(pl.multiple_of(r * size, size), size)
            place = block_rows(order_ref, r, size)
            key_part = own_sum(blocks_ref, terms, 0, rows).astype(bf16)
            value_part = own_sum(blocks_ref, terms, 1, rows).astype(bf16)
            kv_ref[0, place, :] = key_part
            kv_ref[1, place, :] = value_part
            product = (key_part.astype(f32) * value_part.astype(f32)).astype(bf16)
            signal_ref[place, :] = product
            moved[0, pl.ds(pl.multiple_of(taps + order_ref[r] * size, size), size), :] = product.astype(f32)
            return carry

        lax.fori_loop(0, n_blocks, one_block, 0)
        for shift in range(1, sublanes):
            moved[shift, taps : taps + tokens, :] = moved[0, taps - shift : taps - shift + tokens, :]

        def run(g, carry):
            start = pl.multiple_of(g * tiles * sublanes, tiles * sublanes)

            def load(shift, at):
                return moved[shift, pl.ds(start + taps + at * sublanes, sublanes), :]

            def tap(shift, q):
                index = q * sublanes + shift
                return taps_ref[index * sublanes : (index + 1) * sublanes, :]

            sums = window_filter(load, tap, tiles, taps)
            for i in range(tiles):
                filtered_ref[pl.ds(start + i * sublanes, sublanes), :] = sums[i]
            return carry

        lax.fori_loop(0, tokens // (tiles * sublanes), run, 0)

    whole = lambda shape: pl.BlockSpec(shape, lambda g, order: (0,) * len(shape))
    return pl.pallas_call(
        body,
        out_shape=(
            jax.ShapeDtypeStruct((2, tokens, lanes), bf16),
            jax.ShapeDtypeStruct((tokens, lanes), bf16),
            jax.ShapeDtypeStruct((tokens, lanes), f32),
        ),
        grid_spec=pltpu.PrefetchScalarGridSpec(
            num_scalar_prefetch=1,
            grid=(1,),
            in_specs=[
                whole((1, 2, tokens, lanes)),
                *[whole((2, tokens, lanes))] * count,
                whole(spread_taps.shape),
            ],
            out_specs=(
                whole((2, tokens, lanes)),
                whole((tokens, lanes)),
                whole((tokens, lanes)),
            ),
            scratch_shapes=[pltpu.VMEM((sublanes, taps + tokens, lanes), f32)],
        ),
        compiler_params=params(),
        cost_estimate=cost(400 * tokens * lanes * taps, 12 * tokens * lanes),
        name="forward_filter",
    )(order, blocks, *received, spread_taps)


def gate_rows(order, blocks, received, filtered):
    tokens = blocks.shape[2]
    count = len(received)
    n_blocks = order.shape[0]
    size = tokens // n_blocks

    def body(order_ref, blocks_ref, *refs):
        terms = refs[:count]
        filtered_ref, out_ref, grad_ref = refs[count:]

        def one_block(r, carry):
            rows = pl.ds(pl.multiple_of(r * size, size), size)
            place = block_rows(order_ref, r, size)
            queries = own_sum(blocks_ref, terms, 0, rows).astype(bf16).astype(f32)
            grad_gated = own_sum(blocks_ref, terms, 1, rows)
            kept = filtered_ref[place, :]
            out_ref[rows, :] = (queries * kept).astype(bf16)
            later = pl.ds(pl.multiple_of(tokens + r * size, size), size)
            out_ref[later, :] = (grad_gated * kept).astype(bf16)
            grad_ref[place, :] = (grad_gated * queries).astype(bf16)
            return carry

        lax.fori_loop(0, n_blocks, one_block, 0)

    whole = lambda shape: pl.BlockSpec(shape, lambda g, order: (0,) * len(shape))
    return pl.pallas_call(
        body,
        out_shape=(
            jax.ShapeDtypeStruct((2 * tokens, lanes), bf16),
            jax.ShapeDtypeStruct((tokens, lanes), bf16),
        ),
        grid_spec=pltpu.PrefetchScalarGridSpec(
            num_scalar_prefetch=1,
            grid=(1,),
            in_specs=[
                whole((1, 2, tokens, lanes)),
                *[whole((2, tokens, lanes))] * count,
                whole((tokens, lanes)),
            ],
            out_specs=(whole((2 * tokens, lanes)), whole((tokens, lanes))),
        ),
        compiler_params=params(),
        cost_estimate=cost(20 * tokens * lanes, 20 * tokens * lanes),
        name="gate_rows",
    )(order, blocks, *received, filtered)


def backward_filter(order, grad_filtered, key_values, signal, spread_taps):
    tokens = grad_filtered.shape[0]
    taps = spread_taps.shape[0] // sublanes
    n_blocks = order.shape[0]
    size = tokens // n_blocks
    tiles = 8
    steps = taps // sublanes

    def body(order_ref, grad_ref, kv_ref, signal_ref, taps_ref, out_ref, moved, signal_grad, behind, gradient):
        for shift in range(sublanes):
            moved[shift, tokens - sublanes :, :] = jnp.zeros((taps + sublanes, lanes), f32)
            behind[shift, : taps + sublanes, :] = jnp.zeros((taps + sublanes, lanes), f32)
        moved[0, :tokens, :] = grad_ref[...].astype(f32)
        behind[0, taps:, :] = signal_ref[...].astype(f32)
        gradient[...] = grad_ref[...].astype(f32)
        for shift in range(1, sublanes):
            moved[shift, :tokens, :] = moved[0, shift : shift + tokens, :]
            behind[shift, taps:, :] = behind[0, taps - shift : taps - shift + tokens, :]

        def run(g, carry):
            start = pl.multiple_of(g * tiles * sublanes, tiles * sublanes)

            def load(shift, at):
                return moved[shift, pl.ds(start + (tiles - 1 - at) * sublanes, sublanes), :]

            def tap(shift, q):
                index = q * sublanes + shift
                return taps_ref[index * sublanes : (index + 1) * sublanes, :]

            sums = window_filter(load, tap, tiles, taps)
            for i in range(tiles):
                signal_grad[pl.ds(start + (tiles - 1 - i) * sublanes, sublanes), :] = sums[i]
            return carry

        lax.fori_loop(0, tokens // (tiles * sublanes), run, 0)

        def one_block(r, carry):
            start = pl.multiple_of(r * size, size)
            place = block_rows(order_ref, r, size)
            value = signal_grad[place, :]
            out_ref[pl.ds(start, size), :] = (value * kv_ref[1, place, :].astype(f32)).astype(bf16)
            out_ref[pl.ds(tokens + start, size), :] = (value * kv_ref[0, place, :].astype(f32)).astype(bf16)
            return carry

        lax.fori_loop(0, n_blocks, one_block, 0)

        for shift in range(sublanes):

            def sum_run(g, sums):
                start = pl.multiple_of(g * tiles * sublanes, tiles * sublanes)
                sums = list(sums)
                held = {}
                for i in range(tiles):
                    here = gradient[pl.ds(start + i * sublanes, sublanes), :]
                    for q in range(steps):
                        if i - q not in held:
                            held[i - q] = behind[shift, pl.ds(start + taps + (i - q) * sublanes, sublanes), :]
                        sums[q] = sums[q] + here * held[i - q]
                return tuple(sums)

            zero = tuple(jnp.zeros((sublanes, lanes), f32) for _ in range(steps))
            sums = lax.fori_loop(0, tokens // (tiles * sublanes), sum_run, zero)
            for q in range(steps):
                index = q * sublanes + shift
                signal_grad[index : index + 1, :] = jnp.sum(sums[q], axis=0, keepdims=True)
        out_ref[2 * tokens :, :] = signal_grad[:taps, :].astype(bf16)

    whole = lambda shape: pl.BlockSpec(shape, lambda g, order: (0,) * len(shape))
    return pl.pallas_call(
        body,
        out_shape=jax.ShapeDtypeStruct((2 * tokens + taps, lanes), bf16),
        grid_spec=pltpu.PrefetchScalarGridSpec(
            num_scalar_prefetch=1,
            grid=(1,),
            in_specs=[
                whole((tokens, lanes)),
                whole((2, tokens, lanes)),
                whole((tokens, lanes)),
                whole(spread_taps.shape),
            ],
            out_specs=whole((2 * tokens + taps, lanes)),
            scratch_shapes=[
                pltpu.VMEM((sublanes, tokens + taps, lanes), f32),
                pltpu.VMEM((tokens, lanes), f32),
                pltpu.VMEM((sublanes, tokens + taps, lanes), f32),
                pltpu.VMEM((tokens, lanes), f32),
            ],
        ),
        compiler_params=params(),
        cost_estimate=cost(800 * tokens * lanes * taps, 12 * tokens * lanes),
        name="backward_filter",
    )(order, grad_filtered, key_values, signal, spread_taps)


def merge_blocks(place, block, others, tokens):
    matrices = block.shape[0] // tokens
    length = len(others) + 1
    sizes = [len(other) for other in others]
    rows = 256
    steps = tokens // rows

    def body(place_ref, *refs):
        out = refs[-1]
        own, rest = refs[0], list(refs[1:-1])
        line = place_ref[0]
        for offset in range(length):
            if offset == 0:
                value = own[...]
            else:
                value = rest.pop(0)[...]
                for _ in range(sizes[offset - 1] - 1):
                    value += rest.pop(0)[...]
            at = pl.multiple_of(lax.rem(line + offset, length) * lanes, lanes)
            out[0, :, pl.ds(at, lanes)] = value

    spec = pl.BlockSpec((rows, lanes), lambda which, g, place: (which * steps + g, 0))
    return pl.pallas_call(
        body,
        out_shape=jax.ShapeDtypeStruct((matrices, tokens, length * lanes), bf16),
        grid_spec=pltpu.PrefetchScalarGridSpec(
            num_scalar_prefetch=1,
            grid=(matrices, steps),
            in_specs=[spec] * (1 + sum(sizes)),
            out_specs=pl.BlockSpec((1, rows, length * lanes), lambda which, g, place: (which, g, 0)),
        ),
        compiler_params=params(),
        cost_estimate=cost(tokens * lanes * 8, 2 * 2 * tokens * lanes * 11),
        name="merge_blocks",
    )(place, block, *[term for other in others for term in other])


def merge_taps(place, block, others, taps):
    length = len(others) + 1
    sizes = [len(other) for other in others]
    last = block.shape[0] // taps - 1

    def body(place_ref, *refs):
        out = refs[-1]
        own, rest = refs[0], list(refs[1:-1])
        line = place_ref[0]
        for offset in range(length):
            if offset == 0:
                value = own[...]
            else:
                value = rest.pop(0)[...]
                for _ in range(sizes[offset - 1] - 1):
                    value += rest.pop(0)[...]
            at = pl.multiple_of(lax.rem(line + offset, length) * lanes, lanes)
            out[pl.ds(at, lanes), :] = jnp.transpose(value.astype(f32)).astype(bf16)

    return pl.pallas_call(
        body,
        out_shape=jax.ShapeDtypeStruct((length * lanes, taps), bf16),
        grid_spec=pltpu.PrefetchScalarGridSpec(
            num_scalar_prefetch=1,
            grid=(1,),
            in_specs=[pl.BlockSpec((taps, lanes), lambda g, place: (last, 0))] * (1 + sum(sizes)),
            out_specs=pl.BlockSpec((length * lanes, taps), lambda g, place: (0, 0)),
        ),
        compiler_params=params(),
        cost_estimate=cost(taps * lanes * 8, 2 * taps * lanes * 11),
        name="merge_taps",
    )(place, block, *[term for other in others for term in other])


def project_back(place, merged, in_weight, given, indices, part):
    tokens, half = merged[0][0].shape[1:]
    rows = 256
    n = len(merged)
    steps = tokens // rows // 2

    def body(place_ref, *refs):
        out = refs[-1]
        dims = (((1,), (1,)), ((), ()))
        own = jnp.zeros((rows, half), f32)
        other = jnp.zeros((rows, half), f32)
        for k in range(n):
            value, kept, sent = refs[3 * k], refs[3 * k + 1], refs[3 * k + 2]
            value = value[...].reshape(rows, half)
            own += lax.dot_general(value, kept[...].reshape(half, half), dims, preferred_element_type=f32)
            other += lax.dot_general(value, sent[...].reshape(half, half), dims, preferred_element_type=f32)
        at = place_ref[1]
        out[:, pl.ds(pl.multiple_of(at * half, half), half)] = own.astype(bf16)
        out[:, pl.ds(pl.multiple_of((1 - at) * half, half), half)] = other.astype(bf16)

    operands, specs = [], []
    for (value, which), (sent, at), index in zip(merged, given, indices):
        operands += [value, in_weight, sent]
        specs += [
            pl.BlockSpec((1, rows, half), lambda g, place, which=which: (which, part * steps + g, 0)),
            pl.BlockSpec((1, half, half), lambda g, place, index=index: (index, 0, place[1])),
            pl.BlockSpec((1, half, half), lambda g, place, at=at: (at, 0, 0)),
        ]
    return pl.pallas_call(
        body,
        out_shape=jax.ShapeDtypeStruct((tokens // 2, 2 * half), bf16),
        grid_spec=pltpu.PrefetchScalarGridSpec(
            num_scalar_prefetch=1,
            grid=(steps,),
            in_specs=specs,
            out_specs=pl.BlockSpec((rows, 2 * half), lambda g, place: (g, 0)),
        ),
        compiler_params=params(),
        cost_estimate=cost(2 * n * tokens * half * half, 4 * tokens * half),
        name="project_back",
    )(place, *operands)


def project_out(place, merged, out_weight, given, at):
    tokens, half = merged.shape[1:]
    rows = 256

    def body(place_ref, value_ref, kept, sent, out):
        value = value_ref[...].reshape(rows, half)
        pair = place_ref[1]
        own = jnp.dot(value, kept[...], preferred_element_type=f32)
        other = jnp.dot(value, sent[...].reshape(half, half), preferred_element_type=f32)
        out[:, pl.ds(pl.multiple_of(pair * half, half), half)] = own.astype(bf16)
        out[:, pl.ds(pl.multiple_of((1 - pair) * half, half), half)] = other.astype(bf16)

    return pl.pallas_call(
        body,
        out_shape=jax.ShapeDtypeStruct((tokens, 2 * half), bf16),
        grid_spec=pltpu.PrefetchScalarGridSpec(
            num_scalar_prefetch=1,
            grid=(tokens // rows,),
            in_specs=[
                pl.BlockSpec((1, rows, half), lambda g, place: (0, g, 0)),
                pl.BlockSpec((half, half), lambda g, place: (place[1], 0)),
                pl.BlockSpec((1, half, half), lambda g, place: (at, 0, 0)),
            ],
            out_specs=pl.BlockSpec((rows, 2 * half), lambda g, place: (g, 0)),
        ),
        compiler_params=params(),
        cost_estimate=cost(4 * tokens * half * half, 8 * tokens * half),
        name="project_out",
    )(place, merged, out_weight, given)


def in_gradient(place, near, far, merged, which, index, total, running):
    tokens, half = merged.shape[1:]
    rows = 256
    steps = half // rows
    block = near.shape[:3] + (rows,)

    def body(place_ref, own, own_far, other, other_far, value_ref, *refs):
        kept, sent = refs[-2:]
        value = value_ref[...].reshape(tokens, half)
        dims = (((0,), (0,)), ((), ()))

        def product(one, two):
            rows_of = jnp.concatenate([one[...].reshape(tokens // 2, rows), two[...].reshape(tokens // 2, rows)], 0)
            return lax.dot_general(rows_of, value, dims, preferred_element_type=f32)

        kept[...] = product(own, own_far)[None]
        sent[...] = product(other, other_far).astype(bf16)

    more = [] if running is None else [running]
    own_spec = pl.BlockSpec(block, lambda g, place: (0, 0, 0, place[1] * steps + g))
    other_spec = pl.BlockSpec(block, lambda g, place: (0, 0, 0, (1 - place[1]) * steps + g))
    return pl.pallas_call(
        body,
        out_shape=(
            jax.ShapeDtypeStruct((total, half, 2 * half), f32),
            jax.ShapeDtypeStruct((half, half), bf16),
        ),
        grid_spec=pltpu.PrefetchScalarGridSpec(
            num_scalar_prefetch=1,
            grid=(steps,),
            in_specs=[own_spec, own_spec, other_spec, other_spec]
            + [pl.BlockSpec((1, tokens, half), lambda g, place: (which, 0, 0))]
            + [pl.BlockSpec(memory_space=pl.ANY)] * len(more),
            out_specs=(
                pl.BlockSpec((1, rows, half), lambda g, place: (index, g, place[1])),
                pl.BlockSpec((rows, half), lambda g, place: (g, 0)),
            ),
        ),
        input_output_aliases={6: 0} if more else {},
        compiler_params=params(),
        cost_estimate=cost(4 * tokens * half * half, 8 * tokens * half),
        name="in_gradient",
    )(place, near, far, near, far, merged, *more)


def out_gradient(place, merged, near, far):
    tokens, half = merged.shape[1:]
    rows = 256
    steps = half // rows
    block = near.shape[:3] + (half,)

    def body(place_ref, value_ref, own, own_far, other, other_far, kept, sent):
        value = value_ref[...].reshape(tokens, rows)
        dims = (((0,), (0,)), ((), ()))

        def in_order(one, two):
            return jnp.concatenate([ref[...].reshape(tokens // 2, half) for ref in (one, two)], 0)

        kept[...] = lax.dot_general(value, in_order(own, own_far), dims, preferred_element_type=f32)
        sent[...] = lax.dot_general(
            value, in_order(other, other_far), dims, preferred_element_type=f32
        ).astype(bf16)

    own_spec = pl.BlockSpec(block, lambda g, place: (0, 0, 0, place[1]))
    other_spec = pl.BlockSpec(block, lambda g, place: (0, 0, 0, 1 - place[1]))
    return pl.pallas_call(
        body,
        out_shape=(
            jax.ShapeDtypeStruct((2 * half, half), f32),
            jax.ShapeDtypeStruct((half, half), bf16),
        ),
        grid_spec=pltpu.PrefetchScalarGridSpec(
            num_scalar_prefetch=1,
            grid=(steps,),
            in_specs=[
                pl.BlockSpec((1, tokens, rows), lambda g, place: (0, 0, g)),
                own_spec,
                own_spec,
                other_spec,
                other_spec,
            ],
            out_specs=(
                pl.BlockSpec((rows, half), lambda g, place: (place[1] * steps + g, 0)),
                pl.BlockSpec((rows, half), lambda g, place: (g, 0)),
            ),
        ),
        compiler_params=params(),
        cost_estimate=cost(4 * tokens * half * half, 8 * tokens * half),
        name="out_gradient",
    )(place, merged, near, far, near, far)


def take_in_half(place, running, piece, index):
    half = piece.shape[0]

    def body(place_ref, piece_ref, running_ref, out):
        out[...] = piece_ref[...].astype(f32)[None]

    return pl.pallas_call(
        body,
        out_shape=jax.ShapeDtypeStruct(running.shape, f32),
        grid_spec=pltpu.PrefetchScalarGridSpec(
            num_scalar_prefetch=1,
            grid=(1,),
            in_specs=[
                pl.BlockSpec((half, half), lambda g, place: (0, 0)),
                pl.BlockSpec(memory_space=pl.ANY),
            ],
            out_specs=pl.BlockSpec((1, half, half), lambda g, place: (index, 0, 1 - place[1])),
        ),
        input_output_aliases={2: 0},
        compiler_params=params(),
        cost_estimate=cost(half * half, 6 * half * half),
        name="take_in_half",
    )(place, piece, running)


def take_out_half(place, running, piece):
    half = piece.shape[0]

    def body(place_ref, piece_ref, running_ref, out):
        out[...] = piece_ref[...].astype(f32)

    return pl.pallas_call(
        body,
        out_shape=jax.ShapeDtypeStruct(running.shape, f32),
        grid_spec=pltpu.PrefetchScalarGridSpec(
            num_scalar_prefetch=1,
            grid=(1,),
            in_specs=[
                pl.BlockSpec((half, half), lambda g, place: (0, 0)),
                pl.BlockSpec(memory_space=pl.ANY),
            ],
            out_specs=pl.BlockSpec((half, half), lambda g, place: (1 - place[1], 0)),
        ),
        input_output_aliases={2: 0},
        compiler_params=params(),
        cost_estimate=cost(half * half, 6 * half * half),
        name="take_out_half",
    )(place, piece, running)


def on_paired_mesh(tokens, in_weight, out_weight, filters, cotangent):
    taps = filters.shape[1]
    seq_at, fsdp_at = lax.axis_index("seq"), lax.axis_index("fsdp")
    line, pair = seq_at // 2, seq_at % 2
    place = jnp.stack([line, pair]).astype(jnp.int32)
    half_in, half_out = in_weight.shape[2] // 2, out_weight.shape[0] // 2
    width = tokens.shape[1]
    count = tokens.shape[0] * lax.axis_size("seq")
    relative = jnp.arange(8, dtype=jnp.int32)
    order = (
        2 * crossed(fsdp_at ^ (2 * (relative % 2) + relative // 4)) + (pair ^ (relative // 2 % 2))
    ).astype(jnp.int32)

    def sent_in(weight, i):
        return lax.dynamic_slice_in_dim(weight[i], (1 - pair) * half_in, half_in, 1)

    def gathered(own):
        return [own, flip(own, "fsdp", 2), flip(own, "seq", 1), flip_both(own)]

    given_kv = flip(jnp.stack([sent_in(in_weight, 1), sent_in(in_weight, 2)]), "seq", 1)
    x_own = trade_places(tokens, False)
    late_in, late_out, late_cot = after((in_weight, out_weight, cotangent), x_own)
    g_own = trade_places(late_cot, False)
    x_near = jnp.stack(gathered(x_own))
    sent_qo = jnp.stack(
        [sent_in(late_in, 0), lax.dynamic_slice_in_dim(late_out, (1 - pair) * half_out, half_out, 0)]
    )
    x_near, given_kv, sent_qo, g_own = lax.optimization_barrier((x_near, given_kv, sent_qo, g_own))
    x_near = x_near.reshape(2, 2, -1, width)
    x_far = flip(x_near, "fsdp", 1)
    given_qo = flip(sent_qo, "seq", 1)
    own_filters = lax.dynamic_slice_in_dim(filters, pair * half_in + line * lanes, lanes, 0)
    spread_taps = jnp.repeat(jnp.transpose(own_filters), sublanes, axis=0)

    kv_blocks = project_pair(
        place,
        ((x_near, x_far), in_weight, (given_kv, 0), False, 1),
        ((x_near, x_far), in_weight, (given_kv, 1), False, 2),
    )
    kv_up, kv_down = scatter_start(kv_blocks)
    g_near = jnp.stack(gathered(g_own)).reshape(2, 2, -1, width)
    kv_up, kv_down, given_qo, g_near = lax.optimization_barrier((kv_up, kv_down, given_qo, g_near))
    kv_up, kv_down = scatter_next(kv_blocks, kv_up, kv_down, 2)
    g_far = flip(g_near, "fsdp", 1)
    qg_blocks = project_pair(
        place,
        ((x_near, x_far), in_weight, (given_qo, 0), False, 0),
        ((g_near, g_far), out_weight, (given_qo, 1), True, 0),
    )
    kv_up, kv_down = scatter_next(kv_blocks, kv_up, kv_down, 3)
    qg_up, qg_down = scatter_start(qg_blocks)
    for step in (2, 3):
        qg_up, qg_down = scatter_next(qg_blocks, qg_up, qg_down, step)
    key_values, signal, filtered = forward_filter(order, kv_blocks, [kv_up, kv_down], spread_taps)
    gated_rows, grad_filtered = gate_rows(order, qg_blocks, [qg_up, qg_down], filtered)

    gated_others = [[around(gated_rows, -k)] for k in range(1, 4)]
    kv_grads = backward_filter(order, grad_filtered, key_values, signal, spread_taps)
    kv_before = [next_block(kv_grads, 1, 1)]
    kv_behind = [next_block(kv_grads, -1, 1)]
    kv_before.append(next_block(kv_before[0], 1, 2))
    kv_behind.append(next_block(kv_behind[0], -1, 2))

    total_in = in_weight.shape[0]
    first = merge_blocks(place, gated_rows, gated_others, count)
    out_kept, out_sent = out_gradient(place, first, g_near, g_far)
    out_given = flip(out_sent, "seq", 1)
    in_kept, q_sent = in_gradient(place, x_near, x_far, first, 1, 0, total_in, None)
    q_given = flip(q_sent, "seq", 1)
    mixed_part = project_out(place, after(first, out_sent), out_weight, given_qo, 1)
    last_up, last_down, out_given = lax.optimization_barrier(
        after((kv_before[1], kv_behind[1], out_given), q_sent, mixed_part)
    )
    kv_before.append(next_block(last_up, 1, 3))
    kv_behind.append(next_block(last_down, -1, 3))

    mixed_part = mixed_part.reshape(2, 2, 2, count // 8, width)
    mixed_part = added(mixed_part[0], flip(mixed_part[1], "fsdp", 1))
    kv_behind[2], kv_before[2], mixed_part, q_given = lax.optimization_barrier(
        (kv_behind[2], kv_before[2], mixed_part, q_given)
    )
    second = merge_blocks(place, kv_grads, both_ways(kv_before, kv_behind), count)
    in_kept, k_sent = in_gradient(place, x_near, x_far, second, 0, 1, total_in, in_kept)
    k_given = flip(k_sent, "seq", 1)

    def back(part, value):
        return project_back(
            place,
            [(first, 1), (value, 0), (value, 1)],
            in_weight,
            [(given_qo, 0), (given_kv, 0), (given_kv, 1)],
            [0, 1, 2],
            part,
        )

    far_part = back(1, after(second, k_sent))
    near_part = back(0, after(second, far_part))
    parts = added(near_part, flip(far_part, "fsdp", 1)).reshape(4, count // 8, width)
    mixed_part = added(mixed_part[:, 0], flip(mixed_part[:, 1], "fsdp", 2))
    mixed_part = added(mixed_part[0], flip(mixed_part[1], "seq", 1))
    mixed_out = trade_places(mixed_part, True)
    total = parts[0].astype(f32) + flip(parts[1], "fsdp", 2).astype(f32)
    total += flip(parts[2], "seq", 1).astype(f32) + flip_both(parts[3]).astype(f32)
    in_kept, v_sent = in_gradient(place, x_near, x_far, after(second, parts), 1, 2, total_in, in_kept)
    half_taps = merge_taps(place, kv_grads, both_ways(kv_before, kv_behind), taps)
    total, k_given, mixed_out = lax.optimization_barrier((total, k_given, mixed_out))
    v_given = flip(v_sent, "seq", 1)
    given_taps = flip(after(half_taps, v_sent), "seq", 1)
    for index, given in enumerate((q_given, k_given)):
        in_kept = take_in_half(place, in_kept, given, index)
    in_kept, given_taps = lax.optimization_barrier((in_kept, given_taps))
    grad_tokens = trade_places(total.astype(bf16), True)
    grad_filters = jnp.where(
        pair == 0,
        jnp.concatenate([half_taps, given_taps], 0),
        jnp.concatenate([given_taps, half_taps], 0),
    ).astype(f32)
    grad_out_weight = take_out_half(place, out_kept, out_given)
    in_kept = take_in_half(place, in_kept, v_given, 2)
    return (mixed_out, grad_tokens, in_kept, grad_out_weight, grad_filters)


def solution(mesh):
    placed = (
        P("seq", "fsdp"),
        P(None, "seq", "fsdp"),
        P("fsdp", "seq"),
        P("fsdp", None),
        P("seq", "fsdp"),
    )
    paired = (mesh.shape["seq"], mesh.shape["fsdp"]) == (8, 4)
    return jax.shard_map(
        on_paired_mesh if paired else on_any_mesh,
        mesh=mesh,
        in_specs=placed,
        out_specs=(
            P("seq", "fsdp"),
            P("seq", "fsdp"),
            P(None, "seq", "fsdp"),
            P("fsdp", "seq"),
            P("fsdp", None),
        ),
        check_vma=False,
    )
```
